32 devices in a mesh: batch: 4 (over y, x), mp: 8 (over z, core).
Axes of the slice: x: 2, y: 2, z: 4, core: 2. Of those that a mesh axis runs over, the one named last changes fastest.
Arguments:
- input_maps: bfloat16 [2048, 2, 256, 169], P('batch', None, 'mp'), may hold values from -18 to 18
- dense_weight: bfloat16 [2, 9216, 4096], P(None, 'mp'), may hold values from -0.0625 to 0.0625
- dense_bias: float32 [2, 4096], P(None, 'mp'), may hold values from -3 to 3
- stitch_in: float32 [2, 2, 256], P(None, None, 'mp'), may hold values from 0.1 to 0.9
- stitch_out: float32 [2, 2, 4096], P(None, None, 'mp'), may hold values from 0.1 to 0.9
- weight_moment: float32 [2, 9216, 4096], P(None, 'mp'), may hold values from -6 to 6
- bias_moment: float32 [2, 4096], P(None, 'mp'), may hold values from -6 to 6
- stitch_in_moment: float32 [2, 2, 256], P(None, None, 'mp'), may hold values from -6 to 6
- stitch_out_moment: float32 [2, 2, 4096], P(None, None, 'mp'), may hold values from -6 to 6
- cotangent: bfloat16 [2048, 2, 4096], P('batch', None, 'mp'), may hold values from -6 to 6
- live_rows: int32 [4], replicated, may hold values from 1 to 512, 1536 in all
Outputs:
- activations: bfloat16 [2048, 2, 4096], P('batch', None, 'mp')
- maps_grad: bfloat16 [2048, 2, 256, 169], P('batch', None, 'mp')
- weight_grad: float32 [2, 9216, 4096], P(None, 'mp')
- bias_grad: float32 [2, 4096], P(None, 'mp')
- stitch_in_grad: float32 [2, 2, 256], P(None, None, 'mp')
- stitch_out_grad: float32 [2, 2, 4096], P(None, None, 'mp')
- weight_next: bfloat16 [2, 9216, 4096], P(None, 'mp')
- bias_next: float32 [2, 4096], P(None, 'mp')
- stitch_in_next: float32 [2, 2, 256], P(None, None, 'mp')
- stitch_out_next: float32 [2, 2, 4096], P(None, None, 'mp')
- weight_moment_next: float32 [2, 9216, 4096], P(None, 'mp')
- bias_moment_next: float32 [2, 4096], P(None, 'mp')
- stitch_in_moment_next: float32 [2, 2, 256], P(None, None, 'mp')
- stitch_out_moment_next: float32 [2, 2, 4096], P(None, None, 'mp')
The draws below stay inside these ranges and needn't reach their ends.
Inputs may be any that keep to these rules, and one draw needn't show every extreme that they name: `live_rows`: the counts sum to 1536, and at least one group uses all 512 slots.
All inputs are finite; a program needn't handle non-finite values.
Results may differ from the reference program's by a relative error of at most 0.0061.
Values may be sent and summed in bfloat16 or wider, within the bound.
A program may use at most 384 MiB of HBM per device.

```python
import math
import jax
import jax.numpy as jnp
import numpy as np
from jax import lax

C = 256
D_OUT = 4096
IMG_DEV = 512
D_IN = 9216
IMAGES = 2048
LIVE = 1536
N_BATCH = 4


def shard_levels(key, shape, shards, low, top_value):
    loudness = 1.0
    for axis_at, blocks in shards:
        draws = jax.random.uniform(jax.random.fold_in(jax.random.fold_in(key, 6), axis_at), (blocks,), jnp.float32, low / len(shards), top_value / len(shards))
        loudness = loudness * jnp.repeat(jnp.exp(draws), shape[axis_at] // blocks).reshape((-1,) + (1,) * (len(shape) - 1 - axis_at))
    return loudness


def split_up(number_of, total, most, slope):
    portions = [(1 << 20) // math.isqrt(standing ** slope) + 1 for standing in range(2, number_of + 1)]
    rest, holding = total - most - (number_of - 1), [1] * (number_of - 1)
    while rest > 0:
        candidates = [i for i in range(number_of - 1) if holding[i] < most]
        mass, remaining = sum([portions[i] for i in candidates]), rest
        for i in candidates:
            more = min(most - holding[i], max(1, remaining * portions[i] // mass), rest)
            holding[i] = holding[i] + more
            rest = rest - more
    return np.array([most] + holding)


def ragged_sizes(stream_key, amount, total, limit, slope):
    if amount == 2:
        one = jax.random.randint(stream_key, (), max(1, total - limit), min(limit, total - 1) + 1)
        return jnp.stack([one, total - one])
    tallies = jnp.asarray(split_up(amount, total, limit, slope), jnp.int32)
    twos = (amount - 1) // 2
    source_of, receiver = tallies[1:1 + 2 * twos:2], tallies[2:2 + 2 * twos:2]
    margin = jnp.minimum(source_of - 1, limit - receiver)
    moved = jax.random.randint(jax.random.fold_in(stream_key, 1), (twos,), 0, 1 << 20) % (margin + 1)
    tallies = tallies.at[1:1 + 2 * twos:2].set(source_of - moved).at[2:2 + 2 * twos:2].set(receiver + moved)
    return tallies[jax.random.permutation(jax.random.fold_in(stream_key, 2), amount)]


def bell_draw(key, shape, spread, reach, cuts=(), kind=jnp.bfloat16):
    values = jax.random.normal(key, shape, jnp.float32) * spread
    if len(cuts) > 0:
        values = shard_levels(key, shape, cuts, -0.22, 0.18) * values
    return jnp.clip(values, min=-reach, max=reach).astype(kind)


def setup_inputs(seed: int = 0) -> dict:
    seeds = jax.random.split(jax.random.key(seed), 12)
    input_maps = bell_draw(seeds[0], (IMAGES, 2, C, 169), 3.0, 18.0, ((0, 4), (2, 8)))
    dense_weight = bell_draw(seeds[1], (2, D_IN, D_OUT), D_IN ** -0.5, 0.0625, ((1, 8),))
    dense_bias = bell_draw(seeds[2], (2, D_OUT), 0.5, 3.0, ((1, 8),), jnp.float32)
    stitch_in = jnp.clip(0.1 + 0.79999997 * jax.random.uniform(seeds[3], (2, 2, C), jnp.float32) ** shard_levels(seeds[3], (2, 2, C), ((2, 8),), -0.2, 0.2), 0.1, 0.9)
    stitch_out = jnp.clip(0.1 + 0.79999997 * jax.random.uniform(seeds[4], (2, 2, D_OUT), jnp.float32) ** shard_levels(seeds[4], (2, 2, D_OUT), ((2, 8),), -0.2, 0.2), 0.1, 0.9)
    weight_moment = bell_draw(seeds[5], (2, D_IN, D_OUT), 1.0, 6.0, ((1, 8),), jnp.float32)
    bias_moment = bell_draw(seeds[6], (2, D_OUT), 1.0, 6.0, ((1, 8),), jnp.float32)
    stitch_in_moment = bell_draw(seeds[7], (2, 2, C), 1.0, 6.0, ((2, 8),), jnp.float32)
    stitch_out_moment = bell_draw(seeds[8], (2, 2, D_OUT), 1.0, 6.0, ((2, 8),), jnp.float32)
    cotangent = bell_draw(seeds[9], (IMAGES, 2, D_OUT), 1.0, 6.0, ((0, 4), (2, 8)))
    live_rows = ragged_sizes(seeds[10], N_BATCH, LIVE, IMG_DEV, 2).astype(jnp.int32)
    return {"input_maps": input_maps, "dense_weight": dense_weight, "dense_bias": dense_bias, "stitch_in": stitch_in, "stitch_out": stitch_out, "weight_moment": weight_moment, "bias_moment": bias_moment, "stitch_in_moment": stitch_in_moment, "stitch_out_moment": stitch_out_moment, "cotangent": cotangent, "live_rows": live_rows}


@jax.custom_vjp
def low(v):
    return lax.optimization_barrier(v.astype(jnp.bfloat16)).astype(jnp.float32)

@jax.custom_vjp
def low_back(v):
    return v

def low_keep(v):
    return (low(v), None)

def low_pass(kept, grad):
    return (grad,)

def back_keep(v):
    return (v, None)

def back_low(kept, grad):
    return (low(grad),)
low.defvjp(low_keep, low_pass)
low_back.defvjp(back_keep, back_low)
MOMENTUM = 0.9
DENSE_RATE = 0.01
STITCH_RATE = 0.1

def pool_table():
    pixels = jnp.arange(169, dtype=jnp.int32)
    cells = jnp.arange(36, dtype=jnp.int32)
    pixel_row = (pixels // 13)[:, None]
    pixel_col = (pixels % 13)[:, None]
    cell_row = (cells // 6)[None, :]
    cell_col = (cells % 6)[None, :]
    inside = (pixel_row >= 2 * cell_row) & (pixel_row <= 2 * cell_row + 2) & (pixel_col >= 2 * cell_col) & (pixel_col <= 2 * cell_col + 2)
    return inside.astype(jnp.float32)

def forward(input_maps, dense_weight, dense_bias, stitch_in, stitch_out, keep):
    table = pool_table()
    pooled = jnp.einsum('ntck,kq->ntcq', input_maps, table, precision=lax.Precision.HIGHEST) / 9.0
    stitched = jnp.einsum('ijc,njcq->nicq', stitch_in, pooled, precision=lax.Precision.HIGHEST)
    count = input_maps.shape[0]
    features = low_back(low(stitched.reshape(count, 2, -1)))
    summed = jnp.einsum('ntk,tko->nto', features, dense_weight, precision=lax.Precision.HIGHEST)
    hidden = low_back(summed) + dense_bias[None]
    active = jax.nn.gelu(hidden, approximate=True)
    mixed = jnp.einsum('ijo,njo->nio', stitch_out, active, precision=lax.Precision.HIGHEST)
    return mixed * keep[:, None, None]

def reference(input_maps, dense_weight, dense_bias, stitch_in, stitch_out, weight_moment, bias_moment, stitch_in_moment, stitch_out_moment, cotangent, live_rows):
    block = math.gcd(IMG_DEV, 512)
    blocks = IMAGES // block
    slots = jnp.arange(IMAGES, dtype=jnp.int32)
    owners = (slots // IMG_DEV).astype(jnp.int32)
    keep = (slots % IMG_DEV < live_rows[owners]).astype(jnp.float32)
    weight_full = dense_weight.astype(jnp.float32)
    maps_blocks = input_maps.reshape(blocks, block, 2, C, 169)
    cot_blocks = cotangent.reshape(blocks, block, 2, D_OUT)
    keep_blocks = keep.reshape(blocks, block)

    def visit(totals, pieces):
        maps_piece, cot_piece, keep_piece = pieces

        def one_block(maps_value, weight_value, bias_value, mix_first, mix_second):
            return forward(maps_value, weight_value, bias_value, mix_first, mix_second, keep_piece)
        result, pull = jax.vjp(one_block, maps_piece.astype(jnp.float32), weight_full, dense_bias, stitch_in, stitch_out)
        grads = pull(cot_piece.astype(jnp.float32))
        totals = tuple((total + grad for total, grad in zip(totals, grads[1:])))
        return (totals, (result.astype(jnp.bfloat16), grads[0].astype(jnp.bfloat16)))
    zeros = (jnp.zeros_like(weight_full), jnp.zeros_like(dense_bias), jnp.zeros_like(stitch_in), jnp.zeros_like(stitch_out))
    totals, outputs = lax.scan(visit, zeros, (maps_blocks, cot_blocks, keep_blocks))
    weight_grad, bias_grad, stitch_in_grad, stitch_out_grad = totals
    activations = outputs[0].reshape(IMAGES, 2, D_OUT)
    maps_grad = outputs[1].reshape(IMAGES, 2, C, 169)
    weight_moment_next = MOMENTUM * weight_moment + weight_grad
    weight_next = (weight_full - DENSE_RATE * weight_moment_next).astype(jnp.bfloat16)
    bias_moment_next = MOMENTUM * bias_moment + bias_grad
    bias_next = dense_bias - DENSE_RATE * bias_moment_next
    stitch_in_moment_next = MOMENTUM * stitch_in_moment + stitch_in_grad
    stitch_in_next = stitch_in - STITCH_RATE * stitch_in_moment_next
    stitch_out_moment_next = MOMENTUM * stitch_out_moment + stitch_out_grad
    stitch_out_next = stitch_out - STITCH_RATE * stitch_out_moment_next
    return (activations, maps_grad, weight_grad, bias_grad, stitch_in_grad, stitch_out_grad, weight_next, bias_next, stitch_in_next, stitch_out_next, weight_moment_next, bias_moment_next, stitch_in_moment_next, stitch_out_moment_next)
```

```python
import functools

import jax
import jax.numpy as jnp
from jax import lax
from jax.experimental import pallas as pl
from jax.experimental.pallas import tpu as pltpu
from jax.sharding import PartitionSpec as P

MESH = pl.DeviceIdType.MESH
BF16 = jnp.bfloat16
F32 = jnp.float32
VMEM_LIMIT = 60 * 1024 * 1024

MOMENTUM = 0.9
DENSE_RATE = 0.01
STITCH_RATE = 0.1


def pool_table():
    pixels = jnp.arange(169, dtype=jnp.int32)
    cells = jnp.arange(36, dtype=jnp.int32)
    pixel_row = (pixels // 13)[:, None]
    pixel_col = (pixels % 13)[:, None]
    cell_row = (cells // 6)[None, :]
    cell_col = (cells % 6)[None, :]
    inside = (
        (pixel_row >= 2 * cell_row)
        & (pixel_row <= 2 * cell_row + 2)
        & (pixel_col >= 2 * cell_col)
        & (pixel_col <= 2 * cell_col + 2)
    )
    return inside.astype(jnp.float32)


def gelu_tanh(value):
    return jax.nn.gelu(value, approximate=True)


def head(summed, cotangent, keep, dense_bias, stitch_out):
    hidden = summed + dense_bias[None]
    active, gelu_pull = jax.vjp(gelu_tanh, hidden)
    mixed = stitch_out[None, :, 0] * active[:, 0:1] + stitch_out[None, :, 1] * active[:, 1:2]
    activations = (mixed * keep[:, None, None]).astype(jnp.bfloat16)
    pulled = cotangent.astype(jnp.float32) * keep[:, None, None]
    stitch_out_grad = jnp.einsum("nio,njo->ijo", pulled, active, precision=lax.Precision.HIGHEST)
    active_grad = stitch_out[0][None] * pulled[:, 0:1] + stitch_out[1][None] * pulled[:, 1:2]
    hidden_grad = gelu_pull(active_grad)[0]
    bias_grad = jnp.sum(hidden_grad, axis=0)
    return (activations, hidden_grad.astype(jnp.bfloat16), bias_grad, stitch_out_grad)


def rows_layer(features, cotangent, keep, dense_weight, dense_bias, stitch_out):
    terms = jnp.einsum("ntk,tko->nto", features, dense_weight, preferred_element_type=jnp.float32)
    summed = lax.psum_scatter(terms, "mp", scatter_dimension=2, tiled=True)
    activations, summed_grad, bias_grad, stitch_out_grad = head(
        summed, cotangent, keep, dense_bias, stitch_out
    )
    piece = lax.all_gather(summed_grad, "mp", axis=2, tiled=True)
    inputs_grad = jnp.einsum(
        "nto,tko->ntk", piece, dense_weight, preferred_element_type=jnp.float32
    )
    update = jnp.einsum("ntk,nto->tko", features, piece, preferred_element_type=jnp.float32)
    weight_grad = update
    inputs_grad, weight_grad = (inputs_grad, weight_grad)
    return (activations, inputs_grad.astype(jnp.bfloat16), weight_grad, bias_grad, stitch_out_grad)


def dense_layer(features, cotangent, keep, dense_weight, dense_bias, stitch_out):
    return rows_layer(features, cotangent, keep, dense_weight, dense_bias, stitch_out)


def shards(
    input_maps,
    dense_weight,
    dense_bias,
    stitch_in,
    stitch_out,
    weight_moment,
    bias_moment,
    stitch_in_moment,
    stitch_out_moment,
    cotangent,
    live_rows,
):
    rows = input_maps.shape[0]
    chans = input_maps.shape[2]
    width = chans * 36
    group = lax.axis_index("batch")
    positions = jnp.arange(rows, dtype=jnp.int32)
    keep = (positions < live_rows[group]).astype(jnp.float32)
    table = pool_table()
    pooled = (
        jnp.einsum(
            "ntck,kq->ntcq",
            input_maps,
            table.astype(jnp.bfloat16),
            preferred_element_type=jnp.float32,
        )
        / 9.0
    )
    stitched = (
        stitch_in[None, :, 0, :, None] * pooled[:, 0:1]
        + stitch_in[None, :, 1, :, None] * pooled[:, 1:2]
    )
    features = stitched.reshape(rows, 2, width).astype(jnp.bfloat16)
    activations, inputs_grad, weight_grad, bias_grad, stitch_out_grad = dense_layer(
        features, cotangent, keep, dense_weight, dense_bias, stitch_out
    )
    stitched_grad = inputs_grad.astype(jnp.float32).reshape(rows, 2, chans, 36)
    stitch_in_grad = jnp.einsum(
        "nicq,njcq->ijc", stitched_grad, pooled, precision=lax.Precision.HIGHEST
    )
    pooled_grad = (
        stitch_in[0][None, :, :, None] * stitched_grad[:, 0:1]
        + stitch_in[1][None, :, :, None] * stitched_grad[:, 1:2]
    )
    maps_grad = jnp.einsum(
        "ntcq,kq->ntck", pooled_grad / 9.0, table, precision=lax.Precision.HIGHEST
    ).astype(jnp.bfloat16)
    weight_grad, bias_grad, stitch_in_grad, stitch_out_grad = lax.psum(
        (weight_grad, bias_grad, stitch_in_grad, stitch_out_grad), "batch"
    )
    weight_moment_next = MOMENTUM * weight_moment + weight_grad
    weight_next = (dense_weight.astype(jnp.float32) - DENSE_RATE * weight_moment_next).astype(
        jnp.bfloat16
    )
    bias_moment_next = MOMENTUM * bias_moment + bias_grad
    bias_next = dense_bias - DENSE_RATE * bias_moment_next
    stitch_in_moment_next = MOMENTUM * stitch_in_moment + stitch_in_grad
    stitch_in_next = stitch_in - STITCH_RATE * stitch_in_moment_next
    stitch_out_moment_next = MOMENTUM * stitch_out_moment + stitch_out_grad
    stitch_out_next = stitch_out - STITCH_RATE * stitch_out_moment_next
    return (
        activations,
        maps_grad,
        weight_grad,
        bias_grad,
        stitch_in_grad,
        stitch_out_grad,
        weight_next,
        bias_next,
        stitch_in_next,
        stitch_out_next,
        weight_moment_next,
        bias_moment_next,
        stitch_in_moment_next,
        stitch_out_moment_next,
    )


def params():
    return pltpu.CompilerParams(vmem_limit_bytes=VMEM_LIMIT)


def full(shape):
    return pl.BlockSpec(shape, lambda *_: (0,) * len(shape))


def fill_order(order, chans, inverse):
    size = order.shape[0]
    rows = lax.broadcasted_iota(jnp.int32, (size, size), 0)
    cols = lax.broadcasted_iota(jnp.int32, (size, size), 1)
    natural, cells = (cols, rows) if inverse else (rows, cols)
    shift = chans.bit_length() - 1
    hit = natural == 36 * (cells & (chans - 1)) + (cells >> shift)
    order[...] = jnp.where(hit, 1.0, 0.0).astype(BF16)


def pooled_row(maps_ref, tower, i):
    sums = None
    for dy in range(3):
        line = [maps_ref[tower, 26 * i + 13 * dy + x].astype(F32) for x in range(13)]
        cells = [line[2 * j] + line[2 * j + 1] + line[2 * j + 2] for j in range(6)]
        sums = cells if sums is None else [a + b for a, b in zip(sums, cells)]
    return [s * (1.0 / 9.0) for s in sums]


def pool_kernel(chans, maps_ref, mix_ref, ft_ref, f_ref, order, cells):
    @pl.when(pl.program_id(0) == 0)
    def _():
        fill_order(order, chans, False)

    def row(i, carry):
        first = pooled_row(maps_ref, 0, i)
        second = pooled_row(maps_ref, 1, i)
        for t in range(2):
            for j in range(6):
                value = mix_ref[t, 0] * first[j] + mix_ref[t, 1] * second[j]
                start = pl.multiple_of((6 * i + j) * chans, chans)
                cells[t, pl.ds(start, chans), :] = value.astype(BF16)
        return carry

    lax.fori_loop(0, 6, row, 0)
    for t in range(2):
        moved = jnp.dot(order[...], cells[t], preferred_element_type=F32)
        ft_ref[t] = moved.astype(BF16)
        f_ref[t] = moved.T.astype(BF16)


def pool_forward(maps, mix):
    _, cells, chans, rows = maps.shape
    width = chans * 36
    tile = 256
    return pl.pallas_call(
        functools.partial(pool_kernel, chans),
        grid=(rows // tile,),
        in_specs=[
            pl.BlockSpec((2, cells, chans, tile), lambda n: (0, 0, 0, n)),
            full((2, 2, chans, 1)),
        ],
        out_specs=[
            pl.BlockSpec((2, width, tile), lambda n: (0, 0, n)),
            pl.BlockSpec((2, tile, width), lambda n: (0, n, 0)),
        ],
        out_shape=[
            jax.ShapeDtypeStruct((2, width, rows), BF16),
            jax.ShapeDtypeStruct((2, rows, width), BF16),
        ],
        scratch_shapes=[pltpu.VMEM((width, width), BF16), pltpu.VMEM((2, width, tile), BF16)],
        compiler_params=params(),
        name="pool_forward",
    )(maps, mix)


def dense_kernel(f_ref, w_ref, o_ref):
    o_ref[0, 0] = jnp.dot(f_ref[0], w_ref[0], preferred_element_type=F32).astype(BF16)


def dense_forward(f, weight, parts):
    _, rows, width = f.shape
    outs = weight.shape[2] // parts
    return pl.pallas_call(
        dense_kernel,
        grid=(2, parts),
        in_specs=[
            pl.BlockSpec((1, rows, width), lambda t, j: (t, 0, 0)),
            pl.BlockSpec((1, width, outs), lambda t, j: (t, 0, j)),
        ],
        out_specs=pl.BlockSpec((1, 1, rows, outs), lambda t, j: (j, t, 0, 0)),
        out_shape=jax.ShapeDtypeStruct((parts, 2, rows, outs), BF16),
        compiler_params=params(),
        name="dense_forward",
    )(f, weight)


def gelu_parts(v):
    root = 0.7978845608028654
    square = v * v
    tanh = jnp.tanh(root * v * (1.0 + 0.044715 * square))
    half = 0.5 * (1.0 + tanh)
    slope = half + 0.5 * v * (1.0 - tanh * tanh) * root * (1.0 + 3.0 * 0.044715 * square)
    return v * half, slope


def head_kernel(s_ref, cot_ref, keep_ref, bias_ref, mix_ref, act_ref, grad_ref, sums_ref):
    keep = keep_ref[...]
    active, slope, pulled = [], [], []
    for t in range(2):
        value, rate = gelu_parts(s_ref[t].astype(F32) + bias_ref[t])
        active.append(value)
        slope.append(rate)
        pulled.append(cot_ref[t].astype(F32) * keep)
    for i in range(2):
        mixed = mix_ref[2 * i] * active[0] + mix_ref[2 * i + 1] * active[1]
        act_ref[i] = (mixed * keep).astype(BF16)
    for j in range(2):
        pull = mix_ref[j] * pulled[0] + mix_ref[2 + j] * pulled[1]
        grad = pull * slope[j]
        grad_ref[j] = grad.astype(BF16)
        sums_ref[4 + j] = jnp.sum(grad, axis=0, keepdims=True)
        for i in range(2):
            sums_ref[2 * i + j] = jnp.sum(pulled[i] * active[j], axis=0, keepdims=True)


def dense_head(summed, cot, keep, bias, mix):
    _, rows, outs = summed.shape
    tile = 256
    wide = pl.BlockSpec((2, rows, tile), lambda o: (0, 0, o))
    return pl.pallas_call(
        head_kernel,
        grid=(outs // tile,),
        in_specs=[
            wide,
            wide,
            full((rows, 1)),
            pl.BlockSpec((2, 1, tile), lambda o: (0, 0, o)),
            pl.BlockSpec((4, 1, tile), lambda o: (0, 0, o)),
        ],
        out_specs=[wide, wide, pl.BlockSpec((6, 1, tile), lambda o: (0, 0, o))],
        out_shape=[
            jax.ShapeDtypeStruct((2, rows, outs), BF16),
            jax.ShapeDtypeStruct((2, rows, outs), BF16),
            jax.ShapeDtypeStruct((6, 1, outs), F32),
        ],
        compiler_params=params(),
        name="dense_head",
    )(summed, cot, keep, bias, mix)


def back_kernel(parts, group_ref, w_ref, s_ref, o_ref, total):
    j = pl.program_id(1)
    part = lax.dot_general(
        w_ref[0], s_ref[0, 0, 0], (((1,), (1,)), ((), ())), preferred_element_type=F32
    )

    @pl.when(j == 0)
    def _():
        total[...] = part

    @pl.when(j > 0)
    def _():
        total[...] += part

    @pl.when(j == parts - 1)
    def _():
        o_ref[0] = total[...].astype(BF16)


def dense_backward(group, weight, gathered):
    _, parts, _, rows, outs = gathered.shape
    width = weight.shape[1]
    spec = pltpu.PrefetchScalarGridSpec(
        num_scalar_prefetch=1,
        grid=(2, parts),
        in_specs=[
            pl.BlockSpec((1, width, outs), lambda t, j, g: (t, 0, j)),
            pl.BlockSpec((1, 1, 1, rows, outs), lambda t, j, g: (g[0], j, t, 0, 0)),
        ],
        out_specs=pl.BlockSpec((1, width, rows), lambda t, j, g: (t, 0, 0)),
        scratch_shapes=[pltpu.VMEM((width, rows), F32)],
    )
    return pl.pallas_call(
        functools.partial(back_kernel, parts),
        grid_spec=spec,
        out_shape=jax.ShapeDtypeStruct((2, width, rows), BF16),
        compiler_params=params(),
        name="dense_backward",
    )(group, weight, gathered)


def unpool_kernel(chans, maps_ref, mix_ref, g_ref, out_ref, sums_ref, order, cells, above, total):
    @pl.when(pl.program_id(0) == 0)
    def _():
        fill_order(order, chans, True)
        total[...] = jnp.zeros_like(total)

    for t in range(2):
        cells[t] = jnp.dot(order[...], g_ref[t], preferred_element_type=F32)
    above[...] = jnp.zeros_like(above)

    def row(i, carry):
        pooled = [pooled_row(maps_ref, t, i) for t in range(2)]
        for j in range(6):
            start = pl.multiple_of((6 * i + j) * chans, chans)
            for t in range(2):
                grad = cells[t, pl.ds(start, chans), :]
                for s in range(2):
                    total[2 * t + s] += grad * pooled[s][j]
        for t in range(2):
            mixed = []
            for j in range(6):
                start = pl.multiple_of((6 * i + j) * chans, chans)
                value = mix_ref[0, t] * cells[0, pl.ds(start, chans), :]
                value += mix_ref[1, t] * cells[1, pl.ds(start, chans), :]
                mixed.append(value * (1.0 / 9.0))
            line = []
            for x in range(13):
                if x % 2 == 1:
                    line.append(mixed[x // 2])
                elif x == 0:
                    line.append(mixed[0])
                elif x == 12:
                    line.append(mixed[5])
                else:
                    line.append(mixed[x // 2 - 1] + mixed[x // 2])
            for x in range(13):
                out_ref[t, 26 * i + x] = (line[x] + above[t, x]).astype(BF16)
                out_ref[t, 26 * i + 13 + x] = line[x].astype(BF16)
                above[t, x] = line[x]
        return carry

    lax.fori_loop(0, 6, row, 0)
    for t in range(2):
        for x in range(13):
            out_ref[t, 156 + x] = above[t, x].astype(BF16)

    @pl.when(pl.program_id(0) == pl.num_programs(0) - 1)
    def _():
        for k in range(4):
            summed = jnp.sum(total[k], axis=1, keepdims=True)
            sums_ref[k] = jnp.broadcast_to(summed, sums_ref.shape[1:])


def pool_backward(maps, mix, grads):
    _, cells, chans, rows = maps.shape
    width = chans * 36
    tile = 256
    return pl.pallas_call(
        functools.partial(unpool_kernel, chans),
        grid=(rows // tile,),
        in_specs=[
            pl.BlockSpec((2, cells, chans, tile), lambda n: (0, 0, 0, n)),
            full((2, 2, chans, 1)),
            pl.BlockSpec((2, width, tile), lambda n: (0, 0, n)),
        ],
        out_specs=[
            pl.BlockSpec((2, cells, chans, tile), lambda n: (0, 0, 0, n)),
            full((4, chans, 128)),
        ],
        out_shape=[
            jax.ShapeDtypeStruct((2, cells, chans, rows), BF16),
            jax.ShapeDtypeStruct((4, chans, 128), F32),
        ],
        scratch_shapes=[
            pltpu.VMEM((width, width), BF16),
            pltpu.VMEM((2, width, tile), F32),
            pltpu.VMEM((2, 13, chans, tile), F32),
            pltpu.VMEM((4, chans, tile), F32),
        ],
        compiler_params=params(),
        name="pool_backward",
    )(maps, mix, grads)


def update_kernel(groups, ft_ref, s_ref, m_ref, w_ref, grad_ref, next_ref, moment_ref):
    grad = jnp.dot(ft_ref[0, 0], s_ref[0, 0, 0], preferred_element_type=F32)
    for b in range(1, groups):
        grad += jnp.dot(ft_ref[b, 0], s_ref[b, 0, 0], preferred_element_type=F32)
    grad_ref[0] = grad
    moment = MOMENTUM * m_ref[0] + grad
    moment_ref[0] = moment
    next_ref[0] = (w_ref[0].astype(F32) - DENSE_RATE * moment).astype(BF16)


def weight_update(ft_all, gathered, moment, weight):
    groups, parts, _, rows, outs = gathered.shape
    width = weight.shape[1]
    halves = 2
    tile = outs // halves
    wide = pl.BlockSpec((1, width, tile), lambda t, j: (t, 0, j))
    return pl.pallas_call(
        functools.partial(update_kernel, groups),
        grid=(2, parts * halves),
        in_specs=[
            pl.BlockSpec((groups, 1, width, rows), lambda t, j: (0, t, 0, 0)),
            pl.BlockSpec(
                (groups, 1, 1, rows, tile), lambda t, j: (0, j // halves, t, 0, j % halves)
            ),
            wide,
            wide,
        ],
        out_specs=[wide, wide, wide],
        out_shape=[
            jax.ShapeDtypeStruct(moment.shape, F32),
            jax.ShapeDtypeStruct(moment.shape, BF16),
            jax.ShapeDtypeStruct(moment.shape, F32),
        ],
        compiler_params=params(),
        name="weight_update",
    )(ft_all, gathered, moment, weight)


def fast_shards(
    mesh,
    input_maps,
    dense_weight,
    dense_bias,
    stitch_in,
    stitch_out,
    weight_moment,
    bias_moment,
    stitch_in_moment,
    stitch_out_moment,
    cotangent,
    live_rows,
):
    rows, _, chans, _ = input_maps.shape
    outs = dense_bias.shape[1]
    parts = mesh.shape["mp"]
    group = lax.axis_index("batch")
    positions = jnp.arange(rows, dtype=jnp.int32)
    keep = (positions < live_rows[group]).astype(F32)[:, None]
    maps = jnp.transpose(input_maps, (1, 3, 2, 0))
    cot = jnp.transpose(cotangent, (1, 0, 2))
    mix_in = stitch_in[..., None]
    mix_out = stitch_out.reshape(4, 1, outs)
    ft, f = pool_forward(maps, mix_in)
    ft_all = lax.all_gather(ft, "batch", axis=0, tiled=False)
    terms = dense_forward(f, dense_weight, parts)
    summed = lax.psum_scatter(terms, "mp", scatter_dimension=0, tiled=False)
    acts, grads, sums = dense_head(summed, cot, keep, dense_bias[:, None], mix_out)
    activations = jnp.transpose(acts, (1, 0, 2))
    gathered = lax.all_gather(grads, ("batch", "mp"), axis=0, tiled=False)
    gathered = gathered.reshape((mesh.shape["batch"], parts) + grads.shape)
    inputs_grad = dense_backward(group[None], dense_weight, gathered)
    maps_out, mix_sums = pool_backward(maps, mix_in, inputs_grad)
    maps_grad = jnp.transpose(maps_out, (3, 0, 2, 1))
    sums, mix_sums = lax.psum((sums, mix_sums[:, :, 0]), "batch")
    weight_grad, weight_next, weight_moment_next = weight_update(
        ft_all, gathered, weight_moment, dense_weight
    )
    stitch_out_grad = sums[:4].reshape(2, 2, outs)
    bias_grad = sums[4:].reshape(2, outs)
    stitch_in_grad = mix_sums.reshape(2, 2, chans)
    bias_moment_next = MOMENTUM * bias_moment + bias_grad
    bias_next = dense_bias - DENSE_RATE * bias_moment_next
    stitch_in_moment_next = MOMENTUM * stitch_in_moment + stitch_in_grad
    stitch_in_next = stitch_in - STITCH_RATE * stitch_in_moment_next
    stitch_out_moment_next = MOMENTUM * stitch_out_moment + stitch_out_grad
    stitch_out_next = stitch_out - STITCH_RATE * stitch_out_moment_next
    return (
        activations,
        maps_grad,
        weight_grad,
        bias_grad,
        stitch_in_grad,
        stitch_out_grad,
        weight_next,
        bias_next,
        stitch_in_next,
        stitch_out_next,
        weight_moment_next,
        bias_moment_next,
        stitch_in_moment_next,
        stitch_out_moment_next,
    )


def choose(mesh, *args):
    rows, _, chans, _ = args[0].shape
    outs = args[2].shape[1]
    if rows % 256 == 0 and outs % 256 == 0 and chans == 32:
        return fast_shards(mesh, *args)
    return shards(*args)


def solution(mesh):
    in_specs = (
        P("batch", None, "mp", None),
        P(None, "mp", None),
        P(None, "mp"),
        P(None, None, "mp"),
        P(None, None, "mp"),
        P(None, "mp", None),
        P(None, "mp"),
        P(None, None, "mp"),
        P(None, None, "mp"),
        P("batch", None, "mp"),
        P(),
    )
    out_specs = (
        P("batch", None, "mp"),
        P("batch", None, "mp", None),
        P(None, "mp", None),
        P(None, "mp"),
        P(None, None, "mp"),
        P(None, None, "mp"),
        P(None, "mp", None),
        P(None, "mp"),
        P(None, None, "mp"),
        P(None, None, "mp"),
        P(None, "mp", None),
        P(None, "mp"),
        P(None, None, "mp"),
        P(None, None, "mp"),
    )
    body = functools.partial(choose, mesh)
    return jax.shard_map(body, mesh=mesh, in_specs=in_specs, out_specs=out_specs, check_vma=False)
```

```python
import functools

import jax
import jax.numpy as jnp
from jax import lax
from jax.experimental import pallas as pl
from jax.experimental.pallas import tpu as pltpu
from jax.sharding import PartitionSpec as P

MESH = pl.DeviceIdType.MESH
BF16 = jnp.bfloat16
F32 = jnp.float32
VMEM_LIMIT = 60 * 1024 * 1024

MOMENTUM = 0.9
DENSE_RATE = 0.01
STITCH_RATE = 0.1


def pool_table():
    pixels = jnp.arange(169, dtype=jnp.int32)
    cells = jnp.arange(36, dtype=jnp.int32)
    pixel_row = (pixels // 13)[:, None]
    pixel_col = (pixels % 13)[:, None]
    cell_row = (cells // 6)[None, :]
    cell_col = (cells % 6)[None, :]
    inside = (
        (pixel_row >= 2 * cell_row)
        & (pixel_row <= 2 * cell_row + 2)
        & (pixel_col >= 2 * cell_col)
        & (pixel_col <= 2 * cell_col + 2)
    )
    return inside.astype(jnp.float32)


def gelu_tanh(value):
    return jax.nn.gelu(value, approximate=True)


def head(summed, cotangent, keep, dense_bias, stitch_out):
    hidden = summed + dense_bias[None]
    active, gelu_pull = jax.vjp(gelu_tanh, hidden)
    mixed = stitch_out[None, :, 0] * active[:, 0:1] + stitch_out[None, :, 1] * active[:, 1:2]
    activations = (mixed * keep[:, None, None]).astype(jnp.bfloat16)
    pulled = cotangent.astype(jnp.float32) * keep[:, None, None]
    stitch_out_grad = jnp.einsum("nio,njo->ijo", pulled, active, precision=lax.Precision.HIGHEST)
    active_grad = stitch_out[0][None] * pulled[:, 0:1] + stitch_out[1][None] * pulled[:, 1:2]
    hidden_grad = gelu_pull(active_grad)[0]
    bias_grad = jnp.sum(hidden_grad, axis=0)
    return (activations, hidden_grad.astype(jnp.bfloat16), bias_grad, stitch_out_grad)


def rows_layer(features, cotangent, keep, dense_weight, dense_bias, stitch_out):
    terms = jnp.einsum("ntk,tko->nto", features, dense_weight, preferred_element_type=jnp.float32)
    summed = lax.psum_scatter(terms, "mp", scatter_dimension=2, tiled=True)
    activations, summed_grad, bias_grad, stitch_out_grad = head(
        summed, cotangent, keep, dense_bias, stitch_out
    )
    piece = lax.all_gather(summed_grad, "mp", axis=2, tiled=True)
    inputs_grad = jnp.einsum(
        "nto,tko->ntk", piece, dense_weight, preferred_element_type=jnp.float32
    )
    update = jnp.einsum("ntk,nto->tko", features, piece, preferred_element_type=jnp.float32)
    weight_grad = update
    inputs_grad, weight_grad = (inputs_grad, weight_grad)
    return (activations, inputs_grad.astype(jnp.bfloat16), weight_grad, bias_grad, stitch_out_grad)


def dense_layer(features, cotangent, keep, dense_weight, dense_bias, stitch_out):
    return rows_layer(features, cotangent, keep, dense_weight, dense_bias, stitch_out)


def shards(
    input_maps,
    dense_weight,
    dense_bias,
    stitch_in,
    stitch_out,
    weight_moment,
    bias_moment,
    stitch_in_moment,
    stitch_out_moment,
    cotangent,
    live_rows,
):
    rows = input_maps.shape[0]
    chans = input_maps.shape[2]
    width = chans * 36
    group = lax.axis_index("batch")
    positions = jnp.arange(rows, dtype=jnp.int32)
    keep = (positions < live_rows[group]).astype(jnp.float32)
    table = pool_table()
    pooled = (
        jnp.einsum(
            "ntck,kq->ntcq",
            input_maps,
            table.astype(jnp.bfloat16),
            preferred_element_type=jnp.float32,
        )
        / 9.0
    )
    stitched = (
        stitch_in[None, :, 0, :, None] * pooled[:, 0:1]
        + stitch_in[None, :, 1, :, None] * pooled[:, 1:2]
    )
    features = stitched.reshape(rows, 2, width).astype(jnp.bfloat16)
    activations, inputs_grad, weight_grad, bias_grad, stitch_out_grad = dense_layer(
        features, cotangent, keep, dense_weight, dense_bias, stitch_out
    )
    stitched_grad = inputs_grad.astype(jnp.float32).reshape(rows, 2, chans, 36)
    stitch_in_grad = jnp.einsum(
        "nicq,njcq->ijc", stitched_grad, pooled, precision=lax.Precision.HIGHEST
    )
    pooled_grad = (
        stitch_in[0][None, :, :, None] * stitched_grad[:, 0:1]
        + stitch_in[1][None, :, :, None] * stitched_grad[:, 1:2]
    )
    maps_grad = jnp.einsum(
        "ntcq,kq->ntck", pooled_grad / 9.0, table, precision=lax.Precision.HIGHEST
    ).astype(jnp.bfloat16)
    weight_grad, bias_grad, stitch_in_grad, stitch_out_grad = lax.psum(
        (weight_grad, bias_grad, stitch_in_grad, stitch_out_grad), "batch"
    )
    weight_moment_next = MOMENTUM * weight_moment + weight_grad
    weight_next = (dense_weight.astype(jnp.float32) - DENSE_RATE * weight_moment_next).astype(
        jnp.bfloat16
    )
    bias_moment_next = MOMENTUM * bias_moment + bias_grad
    bias_next = dense_bias - DENSE_RATE * bias_moment_next
    stitch_in_moment_next = MOMENTUM * stitch_in_moment + stitch_in_grad
    stitch_in_next = stitch_in - STITCH_RATE * stitch_in_moment_next
    stitch_out_moment_next = MOMENTUM * stitch_out_moment + stitch_out_grad
    stitch_out_next = stitch_out - STITCH_RATE * stitch_out_moment_next
    return (
        activations,
        maps_grad,
        weight_grad,
        bias_grad,
        stitch_in_grad,
        stitch_out_grad,
        weight_next,
        bias_next,
        stitch_in_next,
        stitch_out_next,
        weight_moment_next,
        bias_moment_next,
        stitch_in_moment_next,
        stitch_out_moment_next,
    )


def params():
    return pltpu.CompilerParams(vmem_limit_bytes=VMEM_LIMIT)


def full(shape):
    return pl.BlockSpec(shape, lambda *_: (0,) * len(shape))


def fill_order(order, chans, inverse):
    size = order.shape[0]
    rows = lax.broadcasted_iota(jnp.int32, (size, size), 0)
    cols = lax.broadcasted_iota(jnp.int32, (size, size), 1)
    natural, cells = (cols, rows) if inverse else (rows, cols)
    shift = chans.bit_length() - 1
    hit = natural == 36 * (cells & (chans - 1)) + (cells >> shift)
    order[...] = jnp.where(hit, 1.0, 0.0).astype(BF16)


def spread_mix(mix_ref, wide):
    chans = wide.shape[1]
    rows = lax.broadcasted_iota(jnp.int32, (chans, chans), 0)
    cols = lax.broadcasted_iota(jnp.int32, (chans, chans), 1)
    for k in range(4):
        line = jnp.broadcast_to(mix_ref[k // 2, pl.ds(k % 2, 1), :], (chans, chans))
        column = jnp.sum(jnp.where(rows == cols, line, 0.0), axis=1, keepdims=True)
        wide[k] = jnp.broadcast_to(column, wide.shape[1:])


def pooled_row(maps_ref, tower, i, lanes):
    sums = None
    for dy in range(3):
        line = [maps_ref[tower, 26 * i + 13 * dy + x, :, lanes].astype(F32) for x in range(13)]
        cells = [line[2 * j] + line[2 * j + 1] + line[2 * j + 2] for j in range(6)]
        sums = cells if sums is None else [a + b for a, b in zip(sums, cells)]
    return [s * (1.0 / 9.0) for s in sums]


def pool_kernel(chans, maps_ref, mix_ref, ft_ref, f_ref, order, cells, wide):
    @pl.when(pl.program_id(0) == 0)
    def _():
        fill_order(order, chans, False)
        spread_mix(mix_ref, wide)

    tile = cells.shape[2]

    def row(step, carry):
        i = step // (tile // 128)
        lanes = pl.ds(pl.multiple_of(step % (tile // 128) * 128, 128), 128)
        first = pooled_row(maps_ref, 0, i, lanes)
        second = pooled_row(maps_ref, 1, i, lanes)
        for t in range(2):
            for j in range(6):
                value = wide[2 * t] * first[j] + wide[2 * t + 1] * second[j]
                start = pl.multiple_of((6 * i + j) * chans, chans)
                cells[t, pl.ds(start, chans), lanes] = value.astype(BF16)
        return carry

    lax.fori_loop(0, 6 * (tile // 128), row, 0)
    for t in range(2):
        moved = jnp.dot(order[...], cells[t], preferred_element_type=F32)
        ft_ref[t] = moved.astype(BF16)
        f_ref[t] = moved.T.astype(BF16)


def pool_forward(maps, mix):
    _, cells, chans, rows = maps.shape
    width = chans * 36
    tile = 256
    return pl.pallas_call(
        functools.partial(pool_kernel, chans),
        grid=(rows // tile,),
        in_specs=[
            pl.BlockSpec((2, cells, chans, tile), lambda n: (0, 0, 0, n)),
            full((2, 2, chans)),
        ],
        out_specs=[
            pl.BlockSpec((2, width, tile), lambda n: (0, 0, n)),
            pl.BlockSpec((2, tile, width), lambda n: (0, n, 0)),
        ],
        out_shape=[
            jax.ShapeDtypeStruct((2, width, rows), BF16),
            jax.ShapeDtypeStruct((2, rows, width), BF16),
        ],
        scratch_shapes=[
            pltpu.VMEM((width, width), BF16),
            pltpu.VMEM((2, width, tile), BF16),
            pltpu.VMEM((4, chans, 128), F32),
        ],
        compiler_params=params(),
        name="pool_forward",
    )(maps, mix)


def gelu_parts(v):
    root = 0.7978845608028654
    square = v * v
    tanh = jnp.tanh(root * v * (1.0 + 0.044715 * square))
    half = 0.5 * (1.0 + tanh)
    slope = half + 0.5 * v * (1.0 - tanh * tanh) * root * (1.0 + 3.0 * 0.044715 * square)
    return v * half, slope


def neighbours():
    b, m = lax.axis_index("batch"), lax.axis_index("mp")
    columns = (b, b + 1 - 2 * (b % 2), b + 2 - 4 * (b // 2), 3 - b)
    return b, m, m // 2, m % 2, columns


def greet(columns, m, z, c, nz):
    b, bx, by, _ = columns
    sibling = m + 1 - 2 * c
    barrier = pltpu.get_barrier_semaphore()

    def signal(bb, mm):
        pl.semaphore_signal(barrier, inc=1, device_id=(bb, mm), device_id_type=MESH)

    signal(bx, m)
    signal(by, m)
    signal(b, sibling)
    pl.when(z > 0)(lambda: signal(b, m - 2))
    pl.when(z < nz - 1)(lambda: signal(b, m + 2))
    pl.semaphore_wait(barrier, 3 + jnp.where(z > 0, 1, 0) + jnp.where(z < nz - 1, 1, 0))


def remote(src, dst, send, recv, device):
    return pltpu.make_async_remote_copy(
        src_ref=src, dst_ref=dst, send_sem=send, recv_sem=recv, device_id=device, device_id_type=MESH
    )


def unpool_row(chans, i, lanes, maps_ref, out_ref, cells, above, total, wide):
    spans = [pl.ds(pl.multiple_of((6 * i + j) * chans, chans), chans) for j in range(6)]
    pooled = [pooled_row(maps_ref, t, i, lanes) for t in range(2)]
    sums = [total[k] for k in range(4)]
    for j in range(6):
        for t in range(2):
            grad = cells[t, spans[j], lanes]
            for s in range(2):
                sums[2 * t + s] += grad * pooled[s][j]
    for k in range(4):
        total[k] = sums[k]
    for t in range(2):
        mixed = []
        for j in range(6):
            value = wide[t] * cells[0, spans[j], lanes] + wide[2 + t] * cells[1, spans[j], lanes]
            mixed.append(value * (1.0 / 9.0))
        for x in range(13):
            if x % 2 == 1 or x == 0:
                value = mixed[x // 2]
            elif x == 12:
                value = mixed[5]
            else:
                value = mixed[x // 2 - 1] + mixed[x // 2]
            out_ref[t, 26 * i + x, :, lanes] = (value + above[t, x, :, lanes]).astype(BF16)
            out_ref[t, 26 * i + 13 + x, :, lanes] = value.astype(BF16)
            above[t, x, :, lanes] = value


def gather_kernel(nz, cut, s_ref, sums_ref, w_ref, maps_ref, mix_ref,
                  g_ref, out_ref, total_ref, mixed_ref,
                  keep_sem, line_send, line_recv, cross_send, cross_recv,
                  half_send, half_recv, core_send, core_recv, small_send, small_recv,
                  maps_sem, out_sem, w_sem, col_sem,
                  maps_in, maps_out, wbuf, col, grads, cells, order, above, mix_total, wide,
                  sums_in, sums_mid, mix_in, mix_mid):
    b, m, z, c, columns = neighbours()
    rows = s_ref.shape[1]
    spans = (pl.ds(0, cut), pl.ds(cut, rows - cut))
    sibling = m + 1 - 2 * c
    load_maps = pltpu.make_async_copy(maps_ref, maps_in, maps_sem)
    load_maps.start()
    greet(columns, m, z, c, nz)

    def small(kind, axis, src, dst):
        return remote(src, dst, small_send.at[kind, axis], small_recv.at[kind, axis], (columns[1 + axis], m))

    def place(p, r, zz):
        return g_ref.at[columns[r], 2 * zz + c, :, spans[p], :]

    def half(p, r, zz, t):
        return g_ref.at[columns[r], 2 * zz + c, t, spans[p], :]

    def line(k, zz, up, own=False):
        p, r = (0, 0) if k == 0 else (1, k - 1)
        src = s_ref.at[:, spans[p], :] if own else place(p, r, zz)
        side = 1 if up else 0
        to = m + 2 if up else m - 2
        return remote(src, place(p, r, zz), line_send.at[side, k, zz], line_recv.at[k, zz], (b, to))

    def cross(p, axis, zz, own=False):
        src = s_ref.at[:, spans[p], :] if own else place(p, 0, zz)
        slot = zz if p == 0 else nz
        return remote(
            src, place(p, 0, zz), cross_send.at[axis, slot], cross_recv.at[axis, slot], (columns[1 + axis], m)
        )

    def cross_wait(p, axis, zz):
        slot = zz if p == 0 else nz
        here = place(p, 1 + axis, zz)
        remote(here, here, cross_send.at[axis, slot], cross_recv.at[axis, slot], (columns[1 + axis], m)).wait_recv()

    def diagonal(p, axis, zz):
        slot = zz if p == 0 else nz
        block = half(p, 2 - axis, zz, 1 - axis)
        return remote(block, block, half_send.at[axis, slot], half_recv.at[axis, slot], (columns[1 + axis], m))

    def diagonal_wait(p, axis, zz):
        slot = zz if p == 0 else nz
        block = half(p, 3, zz, 1 - axis)
        remote(block, block, half_send.at[axis, slot], half_recv.at[axis, slot], (columns[1 + axis], m)).wait_recv()

    def core(p, r, zz, own=False):
        src = s_ref.at[:, spans[p], :] if own else place(p, r, zz)
        return remote(src, place(p, r, zz), core_send.at[p, r, zz], core_recv.at[p, r, zz], (b, sibling))

    def core_wait(p, r, zz):
        block = g_ref.at[columns[r], 2 * zz + 1 - c, :, spans[p], :]
        remote(block, block, core_send.at[p, r, zz], core_recv.at[p, r, zz], (b, sibling)).wait_recv()

    def sides(d, body):
        if d == 0:
            body(z, None)
            return
        pl.when(z + d < nz)(lambda: body(z + d, False))
        pl.when(z - d >= 0)(lambda: body(z - d, True))

    def onward(k, zz, up):
        if up:
            pl.when(z < nz - 1)(lambda: line(k, zz, True).start())
        else:
            pl.when(z > 0)(lambda: line(k, zz, False).start())

    mine = pltpu.make_async_copy(s_ref, g_ref.at[b, m], keep_sem)
    cross(1, 0, z, True).start()
    cross(1, 1, z, True).start()
    pl.when(z < nz - 1)(lambda: line(0, z, True, True).start())
    pl.when(z > 0)(lambda: line(0, z, False, True).start())
    cross(0, 0, z, True).start()
    cross(0, 1, z, True).start()
    pl.when(z < nz - 1)(lambda: line(1, z, True, True).start())
    pl.when(z > 0)(lambda: line(1, z, False, True).start())
    first_sums = small(0, 0, sums_ref, sums_in.at[0])
    first_sums.start()
    core(0, 0, z, True).start()
    core(1, 0, z, True).start()
    mine.start()

    def pass_cross(p, zz):
        for axis in range(2):
            cross_wait(p, axis, zz)
            diagonal(p, 1 - axis, zz).start()
            core(p, 1 + axis, zz).start()

    def end_diagonal(p, zz):
        for axis in range(2):
            diagonal_wait(p, axis, zz)
        core(p, 3, zz).start()

    def arrive(zz, up):
        line(0, zz, up).wait_recv()
        onward(0, zz, up)
        cross(0, 0, zz).start()
        cross(0, 1, zz).start()
        core(0, 0, zz).start()
        line(1, zz, up).wait_recv()
        onward(1, zz, up)
        core(1, 0, zz).start()

    def late(zz, up):
        for k in range(2, 5):
            line(k, zz, up).wait_recv()
            onward(k, zz, up)
            core(1, k - 1, zz).start()

    def spread():
        for k in range(2, 5):
            pl.when(z < nz - 1)(lambda k=k: line(k, z, True).start())
            pl.when(z > 0)(lambda k=k: line(k, z, False).start())

    pass_cross(1, z)
    sides(1, arrive)
    pass_cross(0, z)
    end_diagonal(1, z)
    for d in range(2, nz):
        sides(d, arrive)
        if d == 2:
            spread()
    mine.wait()
    width, chans = w_ref.shape[1], maps_ref.shape[2]
    outs = s_ref.shape[2]
    piece = wbuf.shape[1]
    pieces = width // piece

    def weights(k):
        t, at = k // pieces, k % pieces * piece
        return pltpu.make_async_copy(w_ref.at[t, pl.ds(at, piece), :], wbuf.at[k % 2], w_sem.at[k % 2])

    def column(t, j):
        return pltpu.make_async_copy(
            g_ref.at[b, j, t], col.at[:, pl.ds(j * outs, outs)], col_sem.at[j]
        )

    def features_grad(t):
        for k in range(t * pieces, (t + 1) * pieces):
            if k + 1 < 2 * pieces:
                weights(k + 1).start()
            weights(k).wait()
            if k == t * pieces:
                for j in range(2 * nz):
                    column(t, j).wait()
            value = lax.dot_general(
                wbuf[k % 2], col[...], (((1,), (1,)), ((), ())), preferred_element_type=F32
            )
            grads[pl.ds(k % pieces * piece, piece), :] = value.astype(BF16)
        cells[t] = jnp.dot(order[...], grads[...], preferred_element_type=F32)

    blocks = rows // 128

    def maps_back(step, carry):
        i = step // blocks
        lanes = pl.ds(pl.multiple_of(step % blocks * 128, 128), 128)
        unpool_row(chans, i, lanes, maps_in, maps_out, cells, above, mix_total, wide)
        return carry

    weights(0).start()
    fill_order(order, chans, True)
    spread_mix(mix_ref, wide)
    above[...] = jnp.zeros_like(above)
    mix_total[...] = jnp.zeros_like(mix_total)
    first_sums.wait()
    sums_mid[...] = sums_ref[...] + sums_in[0]
    second_sums = small(0, 1, sums_mid, sums_in.at[1])
    second_sums.start()
    sides(1, lambda zz, up: pass_cross(0, zz))
    for zz in range(nz):
        for p in range(2):
            core_wait(p, 0, zz)
    for j in range(2 * nz):
        column(0, j).start()
    features_grad(0)
    for j in range(2 * nz):
        column(1, j).start()
    sides(1, late)
    features_grad(1)
    end_diagonal(0, z)
    load_maps.wait()
    sides(2, lambda zz, up: pass_cross(0, zz))
    lax.fori_loop(0, 3 * blocks, maps_back, 0)
    sides(2, late)
    sides(1, lambda zz, up: end_diagonal(0, zz))
    lax.fori_loop(3 * blocks, 6 * blocks, maps_back, 0)
    for t in range(2):
        for x in range(13):
            maps_out[t, 156 + x] = above[t, x].astype(BF16)
    store_maps = pltpu.make_async_copy(maps_out, out_ref, out_sem)
    store_maps.start()
    for k in range(4):
        mix_in[0, k] = jnp.broadcast_to(jnp.sum(mix_total[k], axis=1, keepdims=True), (chans, 128))
    first_mix = small(1, 0, mix_in.at[0], mix_in.at[1])
    first_mix.start()
    for d in range(3, nz):
        sides(d, lambda zz, up: pass_cross(0, zz))
        sides(d, late)
        sides(d - 1, lambda zz, up: end_diagonal(0, zz))
    first_mix.wait()
    mix_mid[...] = mix_in[0] + mix_in[1]
    second_mix = small(1, 1, mix_mid, mix_in.at[2])
    second_mix.start()
    sides(nz - 1, lambda zz, up: end_diagonal(0, zz))
    second_sums.wait()
    total_ref[...] = sums_mid[...] + sums_in[1]
    second_mix.wait()
    mixed_ref[...] = mix_mid[...] + mix_in[2]
    store_maps.wait()

    for zz in range(nz):
        for r in range(4):
            for p in range(2):
                if r > 0:
                    core_wait(p, r, zz)
                core(p, r, zz).wait_send()
        for axis in range(2):
            cross(0, axis, zz).wait_send()
            diagonal(0, axis, zz).wait_send()
        for k in range(5):
            pl.when((z < nz - 1) & (z >= zz))(lambda k=k, zz=zz: line(k, zz, True).wait_send())
            pl.when((z > 0) & (z <= zz))(lambda k=k, zz=zz: line(k, zz, False).wait_send())
    for axis in range(2):
        cross(1, axis, z).wait_send()
        diagonal(1, axis, z).wait_send()


def gather_all(mesh, grads, sums, weight, maps, mix):
    groups, parts = mesh.shape["batch"], mesh.shape["mp"]
    nz = parts // 2
    _, rows, outs = grads.shape
    _, cells, chans, _ = maps.shape
    width = weight.shape[1]
    piece = width // 3
    cut = rows * 25 // 32
    dma = pltpu.SemaphoreType.DMA
    here = pl.BlockSpec(memory_space=pltpu.VMEM)
    far = pl.BlockSpec(memory_space=pl.ANY)
    return pl.pallas_call(
        functools.partial(gather_kernel, nz, cut),
        in_specs=[far, here, far, far, here],
        out_specs=[far, far, here, here],
        out_shape=[
            jax.ShapeDtypeStruct((groups, parts) + grads.shape, BF16),
            jax.ShapeDtypeStruct(maps.shape, BF16),
            jax.ShapeDtypeStruct(sums.shape, F32),
            jax.ShapeDtypeStruct((4, chans, 128), F32),
        ],
        scratch_shapes=[
            dma,
            dma((2, 5, nz)),
            dma((5, nz)),
            dma((2, nz + 1)),
            dma((2, nz + 1)),
            dma((2, nz + 1)),
            dma((2, nz + 1)),
            dma((2, 4, nz)),
            dma((2, 4, nz)),
            dma((2, 2)),
            dma((2, 2)),
            dma,
            dma,
            dma((2,)),
            dma((parts,)),
            pltpu.VMEM(maps.shape, BF16),
            pltpu.VMEM(maps.shape, BF16),
            pltpu.VMEM((2, piece, parts * outs), BF16),
            pltpu.VMEM((rows, parts * outs), BF16),
            pltpu.VMEM((width, rows), BF16),
            pltpu.VMEM((2, width, rows), F32),
            pltpu.VMEM((width, width), BF16),
            pltpu.VMEM((2, 13, chans, rows), F32),
            pltpu.VMEM((4, chans, 128), F32),
            pltpu.VMEM((4, chans, 128), F32),
            pltpu.VMEM((2,) + sums.shape, F32),
            pltpu.VMEM(sums.shape, F32),
            pltpu.VMEM((3, 4, chans, 128), F32),
            pltpu.VMEM((4, chans, 128), F32),
        ],
        compiler_params=pltpu.CompilerParams(
            collective_id=1, has_side_effects=True, vmem_limit_bytes=VMEM_LIMIT
        ),
        name="gather_all",
    )(grads, sums, weight, maps, mix)


def head_rows(hidden, cot, keep, mix, act_ref, grad_ref, here, lanes):
    active, slope, pulled = [], [], []
    for t in range(2):
        value, rate = gelu_parts(hidden[t])
        active.append(value)
        slope.append(rate)
        pulled.append(cot[t] * keep)
    for i in range(2):
        mixed = mix[2 * i] * active[0] + mix[2 * i + 1] * active[1]
        act_ref[i, here, lanes] = (mixed * keep).astype(BF16)
    terms = [pulled[i] * active[j] for i in range(2) for j in range(2)]
    for j in range(2):
        grad = (mix[j] * pulled[0] + mix[2 + j] * pulled[1]) * slope[j]
        grad_ref[j, here, lanes] = grad.astype(BF16)
        terms.append(grad)
    return terms


def forward_kernel(nz, live_ref, f_ref, ft_ref, w_ref, cot_ref, bias_ref, mix_ref,
                   fta_ref, grad_ref, act_ref, sums_ref,
                   wbuf, pb, sb, rb, inb, w_sem, core_send, core_recv, line_send, line_recv,
                   cross_send, cross_recv, half_send, half_recv, keep_sem):
    b, m, z, c, columns = neighbours()
    sibling = m + 1 - 2 * c
    rows, outs = f_ref.shape[1], pb.shape[3]
    live = live_ref[b]

    def features(r, t):
        return fta_ref.at[t, :, pl.ds(pl.multiple_of(columns[r] * rows, rows), rows)]

    near = jnp.where(z < nz // 2, 1, 0)

    def weights(i, t, own):
        zd = near * (nz - 1 - i) + (1 - near) * i
        j = 2 * zd + (c if own else 1 - c)
        lanes = pl.ds(pl.multiple_of(j * outs, outs), outs)
        k = 2 * t + own
        return pltpu.make_async_copy(w_ref.at[t, :, lanes], wbuf.at[k], w_sem.at[k])

    for t in range(2):
        for own in range(2):
            weights(0, t, own).start()
    mine = [pltpu.make_async_copy(ft_ref.at[t], features(0, t), keep_sem.at[t]) for t in range(2)]
    greet(columns, m, z, c, nz)

    def cross(axis, t):
        return remote(ft_ref.at[t], features(0, t), cross_send.at[axis, t], cross_recv.at[axis, t],
                      (columns[1 + axis], m))

    def cross_wait(axis, t):
        here = features(1 + axis, t)
        remote(here, here, cross_send.at[axis, t], cross_recv.at[axis, t], (columns[1 + axis], m)).wait_recv()

    def diagonal(axis):
        here = features(2 - axis, 1 - axis)
        return remote(here, here, half_send.at[axis], half_recv.at[axis], (columns[1 + axis], m))

    def diagonal_wait(axis):
        here = features(3, 1 - axis)
        remote(here, here, half_send.at[axis], half_recv.at[axis], (columns[1 + axis], m)).wait_recv()

    for k in range(2):
        cross(0, k).start()
        cross(1, 1 - k).start()
    for copy in mine:
        copy.start()

    def swap(d, t):
        return remote(sb.at[d, t], rb.at[d, t], core_send.at[d, t], core_recv.at[d, t], (b, sibling))

    def hop(up, d, t):
        return remote(rb.at[d, t], inb.at[up, d, t], line_send.at[d, t], line_recv.at[up, d, t],
                      (b, m + 4 * up - 2))

    step = 64

    def relay(up, dm, t, first):
        zm = up * z + (1 - up) * (nz - 1 - z)
        d = up * dm + (1 - up) * (nz - 1 - dm)

        def go():
            swap(d, t).wait_recv()
            if not first:
                hop(up, d, t).wait_recv()

            def add(k, carry):
                here = pl.ds(pl.multiple_of(k * step, step), step)
                value = pb[d, t, here, :] + rb[d, t, here, :].astype(F32)
                if not first:
                    value += inb[up, d, t, here, :].astype(F32)
                rb[d, t, here, :] = value.astype(BF16)
                return carry

            lax.fori_loop(0, rows // step, add, 0)
            hop(up, d, t).start()

        pl.when((zm == 0 if first else zm > 0) & (zm < dm))(go)

    def produce(i, carry):
        zd = near * (nz - 1 - i) + (1 - near) * i
        for t in range(2):
            for own in range(2):
                weights(i, t, own).wait()
                part = jnp.dot(f_ref[t], wbuf[2 * t + own], preferred_element_type=F32)
                if own:
                    pb[zd, t] = part
                else:
                    sb[zd, t] = part.astype(BF16)
                    swap(zd, t).start()
                pl.when(i < nz - 1)(lambda t=t, own=own: weights(i + 1, t, own).start())
            relay(near, nz - 1 - i, t, True)
        return carry

    lax.fori_loop(0, nz, produce, 0)
    for dm in range(nz - 1, 0, -1):
        for t in range(2):
            relay(near, dm, t, False)
            relay(1 - near, dm, t, False)
        if dm == nz - 1:
            for axis in range(2):
                cross_wait(1 - axis, 1 - axis)
                diagonal(axis).start()

    for t in range(2):
        swap(z, t).wait_recv()
        pl.when(z > 0)(lambda t=t: hop(1, z, t).wait_recv())
        pl.when(z < nz - 1)(lambda t=t: hop(0, z, t).wait_recv())

        def gather(k, carry, t=t):
            here = pl.ds(pl.multiple_of(k * step, step), step)
            pb[z, t, here, :] += rb[z, t, here, :].astype(F32)
            for up in range(2):
                inside = z > 0 if up else z < nz - 1

                @pl.when(inside)
                def _(up=up):
                    pb[z, t, here, :] += inb[up, z, t, here, :].astype(F32)

            return carry

        lax.fori_loop(0, rows // step, gather, 0)
    tile, high = 256, 16
    for lane in range(outs // tile):
        lanes = pl.ds(lane * tile, tile)
        bias = [bias_ref[pl.ds(t, 1), lanes] for t in range(2)]
        mix = [mix_ref[k // 2, pl.ds(k % 2, 1), lanes] for k in range(4)]

        def block(k, totals, lanes=lanes, bias=bias, mix=mix):
            here = pl.ds(pl.multiple_of(k * high, high), high)
            hidden = [pb[z, t, here, lanes] + bias[t] for t in range(2)]
            cot = [cot_ref[t, here, lanes].astype(F32) for t in range(2)]
            place = k * high + lax.broadcasted_iota(jnp.int32, (high, tile), 0)
            keep = jnp.where(place < live, 1.0, 0.0)
            terms = head_rows(hidden, cot, keep, mix, act_ref, grad_ref, here, lanes)
            return tuple(a + v[:8] + v[8:] for a, v in zip(totals, terms))

        zero = jnp.zeros((8, tile), F32)
        totals = lax.fori_loop(0, rows // high, block, (zero,) * 6)
        for k in range(6):
            sums_ref[k, :, lanes] = jnp.sum(totals[k], axis=0, keepdims=True)

    for copy in mine:
        copy.wait()
    for axis in range(2):
        cross_wait(axis, 1 - axis)
        diagonal_wait(axis)
        diagonal(axis).wait_send()
        for t in range(2):
            cross(axis, t).wait_send()
    for d in range(nz):
        for t in range(2):
            swap(d, t).wait_send()
            pl.when(z < d)(lambda d=d, t=t: hop(1, d, t).wait_send())
            pl.when(z > d)(lambda d=d, t=t: hop(0, d, t).wait_send())


def forward_all(mesh, live, f, ft, weight, cot, bias, mix):
    groups, parts = mesh.shape["batch"], mesh.shape["mp"]
    nz = parts // 2
    _, rows, width = f.shape
    outs = weight.shape[2] // parts
    dma = pltpu.SemaphoreType.DMA
    here = pl.BlockSpec(memory_space=pltpu.VMEM)
    far = pl.BlockSpec(memory_space=pl.ANY)
    return pl.pallas_call(
        functools.partial(forward_kernel, nz),
        in_specs=[pl.BlockSpec(memory_space=pltpu.SMEM), here, far, far, here, here, here],
        out_specs=[far, here, here, here],
        out_shape=[
            jax.ShapeDtypeStruct((2, width, groups * rows), BF16),
            jax.ShapeDtypeStruct((2, rows, outs), BF16),
            jax.ShapeDtypeStruct((2, rows, outs), BF16),
            jax.ShapeDtypeStruct((6, 1, outs), F32),
        ],
        scratch_shapes=[
            pltpu.VMEM((4, width, outs), BF16),
            pltpu.VMEM((nz, 2, rows, outs), F32),
            pltpu.VMEM((nz, 2, rows, outs), BF16),
            pltpu.VMEM((nz, 2, rows, outs), BF16),
            pltpu.VMEM((2, nz, 2, rows, outs), BF16),
            dma((4,)),
            dma((nz, 2)),
            dma((nz, 2)),
            dma((nz, 2)),
            dma((2, nz, 2)),
            dma((2, 2)),
            dma((2, 2)),
            dma((2,)),
            dma((2,)),
            dma((2,)),
        ],
        compiler_params=pltpu.CompilerParams(
            collective_id=0, has_side_effects=True, vmem_limit_bytes=VMEM_LIMIT
        ),
        name="forward_all",
    )(live, f, ft, weight, cot, bias, mix)


def turn_mix(wide):
    chans = wide.shape[0]
    rows = lax.broadcasted_iota(jnp.int32, (chans, chans), 0)
    cols = lax.broadcasted_iota(jnp.int32, (chans, chans), 1)
    return jnp.sum(jnp.where(rows == cols, wide[:, :chans], 0.0), axis=0, keepdims=True)


def update_kernel(ft_ref, s_ref, m_ref, w_ref, sums_ref, mixed_ref, bias_ref, bias_m_ref, in_ref, in_m_ref,
                  out_ref, out_m_ref, grad_ref, next_ref, moment_ref, bias_g, bias_n, bias_mn,
                  in_g, in_n, in_mn, out_g, out_n, out_mn):
    @pl.when((pl.program_id(0) == 0) & (pl.program_id(1) == 0))
    def _():
        def step(grad, value, moment, rate, at, grad_to, next_to, moment_to):
            after = MOMENTUM * moment[at] + grad
            grad_to[at] = grad
            moment_to[at] = after
            next_to[at] = value[at] - rate * after

        for i in range(2):
            at = (pl.ds(i, 1), slice(None))
            step(sums_ref[4 + i], bias_ref, bias_m_ref, DENSE_RATE, at, bias_g, bias_n, bias_mn)
            for j in range(2):
                at = (i, pl.ds(j, 1), slice(None))
                step(sums_ref[2 * i + j], out_ref, out_m_ref, STITCH_RATE, at, out_g, out_n, out_mn)
                step(turn_mix(mixed_ref[2 * i + j]), in_ref, in_m_ref, STITCH_RATE, at, in_g, in_n, in_mn)

    groups, _, _, rows, tile = s_ref.shape
    grad = jnp.dot(ft_ref[0], s_ref[...].reshape(groups * rows, tile), preferred_element_type=F32)
    grad_ref[0] = grad
    moment = MOMENTUM * m_ref[0] + grad
    moment_ref[0] = moment
    next_ref[0] = (w_ref[0].astype(F32) - DENSE_RATE * moment).astype(BF16)


def weight_update(ft_all, gathered, moment, weight, sums, mixed, bias, bias_m, mix_in, mix_in_m, mix_out, mix_out_m):
    groups, parts, _, rows, outs = gathered.shape
    width = weight.shape[1]
    tile = 512 if outs % 512 == 0 else 256
    split = outs // tile
    wide = pl.BlockSpec((1, width, tile), lambda t, j: (t, 0, j))
    smalls = [bias, mix_in, mix_out]
    return pl.pallas_call(
        update_kernel,
        grid=(2, parts * split),
        in_specs=[
            pl.BlockSpec((1, width, groups * rows), lambda t, j: (t, 0, 0)),
            pl.BlockSpec((groups, 1, 1, rows, tile), lambda t, j: (0, j // split, t, 0, j % split)),
            wide,
            wide,
            full(sums.shape),
            full(mixed.shape),
        ]
        + [full(a.shape) for a in smalls for _ in range(2)],
        out_specs=[wide, wide, wide] + [full(a.shape) for a in smalls for _ in range(3)],
        out_shape=[
            jax.ShapeDtypeStruct(moment.shape, F32),
            jax.ShapeDtypeStruct(moment.shape, BF16),
            jax.ShapeDtypeStruct(moment.shape, F32),
        ]
        + [jax.ShapeDtypeStruct(a.shape, F32) for a in smalls for _ in range(3)],
        compiler_params=params(),
        name="weight_update",
    )(ft_all, gathered, moment, weight, sums, mixed, bias, bias_m, mix_in, mix_in_m, mix_out, mix_out_m)


def fast_shards(
    mesh,
    input_maps,
    dense_weight,
    dense_bias,
    stitch_in,
    stitch_out,
    weight_moment,
    bias_moment,
    stitch_in_moment,
    stitch_out_moment,
    cotangent,
    live_rows,
):
    maps = jnp.transpose(input_maps, (1, 3, 2, 0))
    cot = jnp.transpose(cotangent, (1, 0, 2))
    ft, f = pool_forward(maps, stitch_in)
    ft_all, grads, acts, sums = forward_all(
        mesh, live_rows, f, ft, dense_weight, cot, dense_bias, stitch_out
    )
    activations = jnp.transpose(acts, (1, 0, 2))
    gathered, maps_out, sums, mixed = gather_all(mesh, grads, sums, dense_weight, maps, stitch_in)
    maps_grad = jnp.transpose(maps_out, (3, 0, 2, 1))
    (
        weight_grad,
        weight_next,
        weight_moment_next,
        bias_grad,
        bias_next,
        bias_moment_next,
        stitch_in_grad,
        stitch_in_next,
        stitch_in_moment_next,
        stitch_out_grad,
        stitch_out_next,
        stitch_out_moment_next,
    ) = weight_update(
        ft_all,
        gathered,
        weight_moment,
        dense_weight,
        sums,
        mixed,
        dense_bias,
        bias_moment,
        stitch_in,
        stitch_in_moment,
        stitch_out,
        stitch_out_moment,
    )
    return (
        activations,
        maps_grad,
        weight_grad,
        bias_grad,
        stitch_in_grad,
        stitch_out_grad,
        weight_next,
        bias_next,
        stitch_in_next,
        stitch_out_next,
        weight_moment_next,
        bias_moment_next,
        stitch_in_moment_next,
        stitch_out_moment_next,
    )


def choose(mesh, *args):
    rows, _, chans, _ = args[0].shape
    outs = args[2].shape[1]
    shape = mesh.shape["batch"] == 4 and mesh.shape["mp"] == 8
    if shape and rows % 512 == 0 and outs % 256 == 0 and chans == 32:
        return fast_shards(mesh, *args)
    return shards(*args)


def solution(mesh):
    in_specs = (
        P("batch", None, "mp", None),
        P(None, "mp", None),
        P(None, "mp"),
        P(None, None, "mp"),
        P(None, None, "mp"),
        P(None, "mp", None),
        P(None, "mp"),
        P(None, None, "mp"),
        P(None, None, "mp"),
        P("batch", None, "mp"),
        P(),
    )
    out_specs = (
        P("batch", None, "mp"),
        P("batch", None, "mp", None),
        P(None, "mp", None),
        P(None, "mp"),
        P(None, None, "mp"),
        P(None, None, "mp"),
        P(None, "mp", None),
        P(None, "mp"),
        P(None, None, "mp"),
        P(None, None, "mp"),
        P(None, "mp", None),
        P(None, "mp"),
        P(None, None, "mp"),
        P(None, None, "mp"),
    )
    body = functools.partial(choose, mesh)
    return jax.shard_map(body, mesh=mesh, in_specs=in_specs, out_specs=out_specs, check_vma=False)
```

```python
import functools

import jax
import jax.numpy as jnp
from jax import lax
from jax.experimental import pallas as pl
from jax.experimental.pallas import tpu as pltpu
from jax.sharding import PartitionSpec as P

MESH = pl.DeviceIdType.MESH
BF16 = jnp.bfloat16
F32 = jnp.float32
VMEM_LIMIT = 60 * 1024 * 1024

MOMENTUM = 0.9
DENSE_RATE = 0.01
STITCH_RATE = 0.1


def pool_table():
    pixels = jnp.arange(169, dtype=jnp.int32)
    cells = jnp.arange(36, dtype=jnp.int32)
    pixel_row = (pixels // 13)[:, None]
    pixel_col = (pixels % 13)[:, None]
    cell_row = (cells // 6)[None, :]
    cell_col = (cells % 6)[None, :]
    inside = (
        (pixel_row >= 2 * cell_row)
        & (pixel_row <= 2 * cell_row + 2)
        & (pixel_col >= 2 * cell_col)
        & (pixel_col <= 2 * cell_col + 2)
    )
    return inside.astype(jnp.float32)


def gelu_tanh(value):
    return jax.nn.gelu(value, approximate=True)


def head(summed, cotangent, keep, dense_bias, stitch_out):
    hidden = summed + dense_bias[None]
    active, gelu_pull = jax.vjp(gelu_tanh, hidden)
    mixed = stitch_out[None, :, 0] * active[:, 0:1] + stitch_out[None, :, 1] * active[:, 1:2]
    activations = (mixed * keep[:, None, None]).astype(jnp.bfloat16)
    pulled = cotangent.astype(jnp.float32) * keep[:, None, None]
    stitch_out_grad = jnp.einsum("nio,njo->ijo", pulled, active, precision=lax.Precision.HIGHEST)
    active_grad = stitch_out[0][None] * pulled[:, 0:1] + stitch_out[1][None] * pulled[:, 1:2]
    hidden_grad = gelu_pull(active_grad)[0]
    bias_grad = jnp.sum(hidden_grad, axis=0)
    return (activations, hidden_grad.astype(jnp.bfloat16), bias_grad, stitch_out_grad)


def rows_layer(features, cotangent, keep, dense_weight, dense_bias, stitch_out):
    terms = jnp.einsum("ntk,tko->nto", features, dense_weight, preferred_element_type=jnp.float32)
    summed = lax.psum_scatter(terms, "mp", scatter_dimension=2, tiled=True)
    activations, summed_grad, bias_grad, stitch_out_grad = head(
        summed, cotangent, keep, dense_bias, stitch_out
    )
    piece = lax.all_gather(summed_grad, "mp", axis=2, tiled=True)
    inputs_grad = jnp.einsum(
        "nto,tko->ntk", piece, dense_weight, preferred_element_type=jnp.float32
    )
    update = jnp.einsum("ntk,nto->tko", features, piece, preferred_element_type=jnp.float32)
    weight_grad = update
    inputs_grad, weight_grad = (inputs_grad, weight_grad)
    return (activations, inputs_grad.astype(jnp.bfloat16), weight_grad, bias_grad, stitch_out_grad)


def dense_layer(features, cotangent, keep, dense_weight, dense_bias, stitch_out):
    return rows_layer(features, cotangent, keep, dense_weight, dense_bias, stitch_out)


def shards(
    input_maps,
    dense_weight,
    dense_bias,
    stitch_in,
    stitch_out,
    weight_moment,
    bias_moment,
    stitch_in_moment,
    stitch_out_moment,
    cotangent,
    live_rows,
):
    rows = input_maps.shape[0]
    chans = input_maps.shape[2]
    width = chans * 36
    group = lax.axis_index("batch")
    positions = jnp.arange(rows, dtype=jnp.int32)
    keep = (positions < live_rows[group]).astype(jnp.float32)
    table = pool_table()
    pooled = (
        jnp.einsum(
            "ntck,kq->ntcq",
            input_maps,
            table.astype(jnp.bfloat16),
            preferred_element_type=jnp.float32,
        )
        / 9.0
    )
    stitched = (
        stitch_in[None, :, 0, :, None] * pooled[:, 0:1]
        + stitch_in[None, :, 1, :, None] * pooled[:, 1:2]
    )
    features = stitched.reshape(rows, 2, width).astype(jnp.bfloat16)
    activations, inputs_grad, weight_grad, bias_grad, stitch_out_grad = dense_layer(
        features, cotangent, keep, dense_weight, dense_bias, stitch_out
    )
    stitched_grad = inputs_grad.astype(jnp.float32).reshape(rows, 2, chans, 36)
    stitch_in_grad = jnp.einsum(
        "nicq,njcq->ijc", stitched_grad, pooled, precision=lax.Precision.HIGHEST
    )
    pooled_grad = (
        stitch_in[0][None, :, :, None] * stitched_grad[:, 0:1]
        + stitch_in[1][None, :, :, None] * stitched_grad[:, 1:2]
    )
    maps_grad = jnp.einsum(
        "ntcq,kq->ntck", pooled_grad / 9.0, table, precision=lax.Precision.HIGHEST
    ).astype(jnp.bfloat16)
    weight_grad, bias_grad, stitch_in_grad, stitch_out_grad = lax.psum(
        (weight_grad, bias_grad, stitch_in_grad, stitch_out_grad), "batch"
    )
    weight_moment_next = MOMENTUM * weight_moment + weight_grad
    weight_next = (dense_weight.astype(jnp.float32) - DENSE_RATE * weight_moment_next).astype(
        jnp.bfloat16
    )
    bias_moment_next = MOMENTUM * bias_moment + bias_grad
    bias_next = dense_bias - DENSE_RATE * bias_moment_next
    stitch_in_moment_next = MOMENTUM * stitch_in_moment + stitch_in_grad
    stitch_in_next = stitch_in - STITCH_RATE * stitch_in_moment_next
    stitch_out_moment_next = MOMENTUM * stitch_out_moment + stitch_out_grad
    stitch_out_next = stitch_out - STITCH_RATE * stitch_out_moment_next
    return (
        activations,
        maps_grad,
        weight_grad,
        bias_grad,
        stitch_in_grad,
        stitch_out_grad,
        weight_next,
        bias_next,
        stitch_in_next,
        stitch_out_next,
        weight_moment_next,
        bias_moment_next,
        stitch_in_moment_next,
        stitch_out_moment_next,
    )


def params():
    return pltpu.CompilerParams(vmem_limit_bytes=VMEM_LIMIT)


def full(shape):
    return pl.BlockSpec(shape, lambda *_: (0,) * len(shape))


def fill_order(order, chans, inverse):
    size = order.shape[0]
    rows = lax.broadcasted_iota(jnp.int32, (size, size), 0)
    cols = lax.broadcasted_iota(jnp.int32, (size, size), 1)
    natural, cells = (cols, rows) if inverse else (rows, cols)
    shift = chans.bit_length() - 1
    hit = natural == 36 * (cells & (chans - 1)) + (cells >> shift)
    order[...] = jnp.where(hit, 1.0, 0.0).astype(BF16)


def spread_mix(mix_ref, wide):
    chans = wide.shape[1]
    rows = lax.broadcasted_iota(jnp.int32, (chans, chans), 0)
    cols = lax.broadcasted_iota(jnp.int32, (chans, chans), 1)
    for k in range(4):
        line = jnp.broadcast_to(mix_ref[k // 2, pl.ds(k % 2, 1), :], (chans, chans))
        column = jnp.sum(jnp.where(rows == cols, line, 0.0), axis=1, keepdims=True)
        wide[k] = jnp.broadcast_to(column, wide.shape[1:])


def pooled_row(maps_ref, tower, i, lanes):
    sums = None
    for dy in range(3):
        line = [maps_ref[tower, 26 * i + 13 * dy + x, :, lanes].astype(F32) for x in range(13)]
        cells = [line[2 * j] + line[2 * j + 1] + line[2 * j + 2] for j in range(6)]
        sums = cells if sums is None else [a + b for a, b in zip(sums, cells)]
    return [s * (1.0 / 9.0) for s in sums]


def gelu_parts(v):
    root = 0.7978845608028654
    square = v * v
    tanh = jnp.tanh(root * v * (1.0 + 0.044715 * square))
    half = 0.5 * (1.0 + tanh)
    slope = half + 0.5 * v * (1.0 - tanh * tanh) * root * (1.0 + 3.0 * 0.044715 * square)
    return v * half, slope


def neighbours():
    b, m = lax.axis_index("batch"), lax.axis_index("mp")
    columns = (b, b + 1 - 2 * (b % 2), b + 2 - 4 * (b // 2), 3 - b)
    return b, m, m // 2, m % 2, columns


def greet(columns, m, z, c, nz):
    b, bx, by, _ = columns
    sibling = m + 1 - 2 * c
    barrier = pltpu.get_barrier_semaphore()

    def signal(bb, mm):
        pl.semaphore_signal(barrier, inc=1, device_id=(bb, mm), device_id_type=MESH)

    signal(bx, m)
    signal(by, m)
    signal(b, sibling)
    pl.when(z > 0)(lambda: signal(b, m - 2))
    pl.when(z < nz - 1)(lambda: signal(b, m + 2))
    pl.semaphore_wait(barrier, 3 + jnp.where(z > 0, 1, 0) + jnp.where(z < nz - 1, 1, 0))


def remote(src, dst, send, recv, device):
    return pltpu.make_async_remote_copy(
        src_ref=src, dst_ref=dst, send_sem=send, recv_sem=recv, device_id=device, device_id_type=MESH
    )


def unpool_row(chans, i, lanes, maps_ref, out_ref, cells, above, total, wide):
    spans = [pl.ds(pl.multiple_of((6 * i + j) * chans, chans), chans) for j in range(6)]
    pooled = [pooled_row(maps_ref, t, i, lanes) for t in range(2)]
    sums = [total[k] for k in range(4)]
    for j in range(6):
        for t in range(2):
            grad = cells[t, spans[j], lanes]
            for s in range(2):
                sums[2 * t + s] += grad * pooled[s][j]
    for k in range(4):
        total[k] = sums[k]
    for t in range(2):
        mixed = []
        for j in range(6):
            value = wide[t] * cells[0, spans[j], lanes] + wide[2 + t] * cells[1, spans[j], lanes]
            mixed.append(value * (1.0 / 9.0))
        for x in range(13):
            if x % 2 == 1 or x == 0:
                value = mixed[x // 2]
            elif x == 12:
                value = mixed[5]
            else:
                value = mixed[x // 2 - 1] + mixed[x // 2]
            out_ref[t, 26 * i + x, :, lanes] = (value + above[t, x, :, lanes]).astype(BF16)
            out_ref[t, 26 * i + 13 + x, :, lanes] = value.astype(BF16)
            above[t, x, :, lanes] = value


def gather_kernel(nz, cut, s_ref, acts_ref, sums_ref, w_ref, maps_ref, mix_ref,
                  g_ref, acts_to, out_ref, total_ref, mixed_ref,
                  keep_sem, line_send, line_recv, cross_send, cross_recv,
                  half_send, half_recv, core_send, core_recv, small_send, small_recv,
                  maps_sem, out_sem, w_sem, col_sem, acts_sem, acts_in, acts_out,
                  maps_in, maps_out, wbuf, col, grads, cells, order, above, mix_total, wide,
                  sums_in, sums_mid, mix_in, mix_mid):
    b, m, z, c, columns = neighbours()
    rows = s_ref.shape[1]
    spans = (pl.ds(0, cut), pl.ds(cut, rows - cut))
    sibling = m + 1 - 2 * c
    load_maps = pltpu.make_async_copy(maps_ref, maps_in, maps_sem)
    load_acts = pltpu.make_async_copy(acts_ref, acts_in, acts_sem.at[0])
    load_acts.start()
    load_maps.start()
    greet(columns, m, z, c, nz)

    def small(kind, axis, src, dst):
        return remote(src, dst, small_send.at[kind, axis], small_recv.at[kind, axis], (columns[1 + axis], m))

    def place(p, r, zz):
        return g_ref.at[columns[r], 2 * zz + c, :, spans[p], :]

    def half(p, r, zz, t):
        return g_ref.at[columns[r], 2 * zz + c, t, spans[p], :]

    def line(k, zz, up, own=False):
        p, r = (0, 0) if k == 0 else (1, k - 1)
        src = s_ref.at[:, spans[p], :] if own else place(p, r, zz)
        side = 1 if up else 0
        to = m + 2 if up else m - 2
        return remote(src, place(p, r, zz), line_send.at[side, k, zz], line_recv.at[k, zz], (b, to))

    def cross(p, axis, zz, own=False):
        src = s_ref.at[:, spans[p], :] if own else place(p, 0, zz)
        slot = zz if p == 0 else nz
        return remote(
            src, place(p, 0, zz), cross_send.at[axis, slot], cross_recv.at[axis, slot], (columns[1 + axis], m)
        )

    def cross_wait(p, axis, zz):
        slot = zz if p == 0 else nz
        here = place(p, 1 + axis, zz)
        remote(here, here, cross_send.at[axis, slot], cross_recv.at[axis, slot], (columns[1 + axis], m)).wait_recv()

    def diagonal(p, axis, zz):
        slot = zz if p == 0 else nz
        block = half(p, 2 - axis, zz, 1 - axis)
        return remote(block, block, half_send.at[axis, slot], half_recv.at[axis, slot], (columns[1 + axis], m))

    def diagonal_wait(p, axis, zz):
        slot = zz if p == 0 else nz
        block = half(p, 3, zz, 1 - axis)
        remote(block, block, half_send.at[axis, slot], half_recv.at[axis, slot], (columns[1 + axis], m)).wait_recv()

    def core(p, r, zz, own=False):
        src = s_ref.at[:, spans[p], :] if own else place(p, r, zz)
        return remote(src, place(p, r, zz), core_send.at[p, r, zz], core_recv.at[p, r, zz], (b, sibling))

    def core_wait(p, r, zz):
        block = g_ref.at[columns[r], 2 * zz + 1 - c, :, spans[p], :]
        remote(block, block, core_send.at[p, r, zz], core_recv.at[p, r, zz], (b, sibling)).wait_recv()

    def sides(d, body):
        if d == 0:
            body(z, None)
            return
        pl.when(z + d < nz)(lambda: body(z + d, False))
        pl.when(z - d >= 0)(lambda: body(z - d, True))

    def onward(k, zz, up):
        if up:
            pl.when(z < nz - 1)(lambda: line(k, zz, True).start())
        else:
            pl.when(z > 0)(lambda: line(k, zz, False).start())

    mine = pltpu.make_async_copy(s_ref, g_ref.at[b, m], keep_sem)
    cross(1, 0, z, True).start()
    cross(1, 1, z, True).start()
    pl.when(z < nz - 1)(lambda: line(0, z, True, True).start())
    pl.when(z > 0)(lambda: line(0, z, False, True).start())
    cross(0, 0, z, True).start()
    cross(0, 1, z, True).start()
    pl.when(z < nz - 1)(lambda: line(1, z, True, True).start())
    pl.when(z > 0)(lambda: line(1, z, False, True).start())
    first_sums = small(0, 0, sums_ref, sums_in.at[0])
    first_sums.start()
    core(0, 0, z, True).start()
    core(1, 0, z, True).start()
    mine.start()

    def pass_cross(p, zz):
        for axis in range(2):
            cross_wait(p, axis, zz)
            diagonal(p, 1 - axis, zz).start()
            core(p, 1 + axis, zz).start()

    def end_diagonal(p, zz):
        for axis in range(2):
            diagonal_wait(p, axis, zz)
        core(p, 3, zz).start()

    def arrive(zz, up):
        line(0, zz, up).wait_recv()
        onward(0, zz, up)
        cross(0, 0, zz).start()
        cross(0, 1, zz).start()
        core(0, 0, zz).start()
        line(1, zz, up).wait_recv()
        onward(1, zz, up)
        core(1, 0, zz).start()

    def late(zz, up):
        for k in range(2, 5):
            line(k, zz, up).wait_recv()
            onward(k, zz, up)
            core(1, k - 1, zz).start()

    def spread():
        for k in range(2, 5):
            pl.when(z < nz - 1)(lambda k=k: line(k, z, True).start())
            pl.when(z > 0)(lambda k=k: line(k, z, False).start())

    def join_towers(k, carry):
        here = pl.ds(pl.multiple_of(k * 16, 16), 16)
        both = jnp.stack([acts_in[t, here, :].astype(F32) for t in range(2)], axis=1)
        acts_out[here, :, :] = both.astype(BF16)
        return carry

    pass_cross(1, z)
    load_acts.wait()
    lax.fori_loop(0, rows // 16, join_towers, 0)
    store_acts = pltpu.make_async_copy(acts_out, acts_to, acts_sem.at[1])
    store_acts.start()
    sides(1, arrive)
    pass_cross(0, z)
    end_diagonal(1, z)
    for d in range(2, nz):
        sides(d, arrive)
        if d == 2:
            spread()
    mine.wait()
    width, chans = w_ref.shape[1], maps_ref.shape[2]
    outs = s_ref.shape[2]
    piece = wbuf.shape[1]
    pieces = width // piece

    def weights(k):
        t, at = k // pieces, k % pieces * piece
        return pltpu.make_async_copy(w_ref.at[t, pl.ds(at, piece), :], wbuf.at[k % 2], w_sem.at[k % 2])

    def column(t, j):
        return pltpu.make_async_copy(
            g_ref.at[b, j, t], col.at[:, pl.ds(j * outs, outs)], col_sem.at[j]
        )

    def features_grad(t):
        for k in range(t * pieces, (t + 1) * pieces):
            if k + 1 < 2 * pieces:
                weights(k + 1).start()
            weights(k).wait()
            if k == t * pieces:
                for j in range(2 * nz):
                    column(t, j).wait()
            value = lax.dot_general(
                wbuf[k % 2], col[...], (((1,), (1,)), ((), ())), preferred_element_type=F32
            )
            grads[pl.ds(k % pieces * piece, piece), :] = value.astype(BF16)
        cells[t] = jnp.dot(order[...], grads[...], preferred_element_type=F32)

    blocks = rows // 128

    def maps_back(step, carry):
        i = step // blocks
        lanes = pl.ds(pl.multiple_of(step % blocks * 128, 128), 128)
        unpool_row(chans, i, lanes, maps_in, maps_out, cells, above, mix_total, wide)
        return carry

    weights(0).start()
    fill_order(order, chans, True)
    spread_mix(mix_ref, wide)
    above[...] = jnp.zeros_like(above)
    mix_total[...] = jnp.zeros_like(mix_total)
    first_sums.wait()
    sums_mid[...] = sums_ref[...] + sums_in[0]
    second_sums = small(0, 1, sums_mid, sums_in.at[1])
    second_sums.start()
    sides(1, lambda zz, up: pass_cross(0, zz))
    for zz in range(nz):
        for p in range(2):
            core_wait(p, 0, zz)
    for j in range(2 * nz):
        column(0, j).start()
    features_grad(0)
    for j in range(2 * nz):
        column(1, j).start()
    sides(1, late)
    features_grad(1)
    end_diagonal(0, z)
    load_maps.wait()
    outer = (z == 0) | (z == nz - 1)
    inner = (z > 0) & (z < nz - 1)
    pl.when(inner)(lambda: sides(2, late))
    pl.when(outer)(lambda: sides(2, lambda zz, up: pass_cross(0, zz)))
    lax.fori_loop(0, 3 * blocks, maps_back, 0)
    pl.when(outer)(lambda: sides(2, late))
    lax.fori_loop(3 * blocks, 6 * blocks, maps_back, 0)
    for t in range(2):
        for x in range(13):
            maps_out[t, 156 + x] = above[t, x].astype(BF16)
    store_maps = pltpu.make_async_copy(maps_out, out_ref, out_sem)
    store_maps.start()
    for k in range(4):
        mix_in[0, k] = jnp.broadcast_to(jnp.sum(mix_total[k], axis=1, keepdims=True), (chans, 128))
    first_mix = small(1, 0, mix_in.at[0], mix_in.at[1])
    first_mix.start()
    pl.when(inner)(lambda: sides(2, lambda zz, up: pass_cross(0, zz)))
    sides(1, lambda zz, up: end_diagonal(0, zz))
    sides(3, lambda zz, up: pass_cross(0, zz))
    first_mix.wait()
    mix_mid[...] = mix_in[0] + mix_in[1]
    second_mix = small(1, 1, mix_mid, mix_in.at[2])
    second_mix.start()
    sides(2, lambda zz, up: end_diagonal(0, zz))
    sides(3, late)
    sides(3, lambda zz, up: end_diagonal(0, zz))
    second_sums.wait()
    total_ref[...] = sums_mid[...] + sums_in[1]
    second_mix.wait()
    mixed_ref[...] = mix_mid[...] + mix_in[2]
    store_maps.wait()
    store_acts.wait()

    for zz in range(nz):
        for r in range(4):
            for p in range(2):
                if r > 0:
                    core_wait(p, r, zz)
                core(p, r, zz).wait_send()
        for axis in range(2):
            cross(0, axis, zz).wait_send()
            diagonal(0, axis, zz).wait_send()
        for k in range(5):
            pl.when((z < nz - 1) & (z >= zz))(lambda k=k, zz=zz: line(k, zz, True).wait_send())
            pl.when((z > 0) & (z <= zz))(lambda k=k, zz=zz: line(k, zz, False).wait_send())
    for axis in range(2):
        cross(1, axis, z).wait_send()
        diagonal(1, axis, z).wait_send()


def gather_all(mesh, grads, acts, sums, weight, maps, mix):
    groups, parts = mesh.shape["batch"], mesh.shape["mp"]
    nz = parts // 2
    _, rows, outs = grads.shape
    _, cells, chans, _ = maps.shape
    width = weight.shape[1]
    piece = width // 3
    cut = rows * 25 // 32
    dma = pltpu.SemaphoreType.DMA
    here = pl.BlockSpec(memory_space=pltpu.VMEM)
    far = pl.BlockSpec(memory_space=pl.ANY)
    return pl.pallas_call(
        functools.partial(gather_kernel, nz, cut),
        in_specs=[far, far, here, far, far, here],
        out_specs=[far, far, far, here, here],
        out_shape=[
            jax.ShapeDtypeStruct((groups, parts) + grads.shape, BF16),
            jax.ShapeDtypeStruct((rows, 2, outs), BF16),
            jax.ShapeDtypeStruct(maps.shape, BF16),
            jax.ShapeDtypeStruct(sums.shape, F32),
            jax.ShapeDtypeStruct((4, chans, 128), F32),
        ],
        scratch_shapes=[
            dma,
            dma((2, 5, nz)),
            dma((5, nz)),
            dma((2, nz + 1)),
            dma((2, nz + 1)),
            dma((2, nz + 1)),
            dma((2, nz + 1)),
            dma((2, 4, nz)),
            dma((2, 4, nz)),
            dma((2, 2)),
            dma((2, 2)),
            dma,
            dma,
            dma((2,)),
            dma((parts,)),
            dma((2,)),
            pltpu.VMEM((2, rows, outs), BF16),
            pltpu.VMEM((rows, 2, outs), BF16),
            pltpu.VMEM(maps.shape, BF16),
            pltpu.VMEM(maps.shape, BF16),
            pltpu.VMEM((2, piece, parts * outs), BF16),
            pltpu.VMEM((rows, parts * outs), BF16),
            pltpu.VMEM((width, rows), BF16),
            pltpu.VMEM((2, width, rows), F32),
            pltpu.VMEM((width, width), BF16),
            pltpu.VMEM((2, 13, chans, rows), F32),
            pltpu.VMEM((4, chans, 128), F32),
            pltpu.VMEM((4, chans, 128), F32),
            pltpu.VMEM((2,) + sums.shape, F32),
            pltpu.VMEM(sums.shape, F32),
            pltpu.VMEM((3, 4, chans, 128), F32),
            pltpu.VMEM((4, chans, 128), F32),
        ],
        compiler_params=pltpu.CompilerParams(
            collective_id=1, has_side_effects=True, vmem_limit_bytes=VMEM_LIMIT
        ),
        name="gather_all",
    )(grads, acts, sums, weight, maps, mix)


def head_rows(hidden, cot, keep, mix, act_ref, grad_ref, here, lanes):
    active, slope, pulled = [], [], []
    for t in range(2):
        value, rate = gelu_parts(hidden[t])
        active.append(value)
        slope.append(rate)
        pulled.append(cot[t] * keep)
    for i in range(2):
        mixed = mix[2 * i] * active[0] + mix[2 * i + 1] * active[1]
        act_ref[i, here, lanes] = (mixed * keep).astype(BF16)
    terms = [pulled[i] * active[j] for i in range(2) for j in range(2)]
    for j in range(2):
        grad = (mix[j] * pulled[0] + mix[2 + j] * pulled[1]) * slope[j]
        grad_ref[j, here, lanes] = grad.astype(BF16)
        terms.append(grad)
    return terms


def forward_kernel(nz, live_ref, maps_ref, w_ref, cot_raw, bias_ref, mix_ref, mix_in_ref,
                   fta_ref, grad_ref, act_ref, sums_ref,
                   maps_in, cells, order, wide, f_ref, ft_ref, cot_in, cot_ref, wbuf, pb, sb, rb, inb,
                   maps_sem, cot_sem, w_sem, core_send, core_recv, line_send, line_recv,
                   cross_send, cross_recv, half_send, half_recv, keep_sem):
    b, m, z, c, columns = neighbours()
    sibling = m + 1 - 2 * c
    rows, outs = f_ref.shape[1], pb.shape[3]
    live = live_ref[b]

    chans, span = maps_in.shape[2], cells.shape[2]
    halves = rows // span

    def features(r, t, h):
        start = pl.multiple_of(columns[r] * rows + h * span, span)
        return fta_ref.at[t, :, pl.ds(start, span)]

    def load_maps(h):
        lanes = pl.ds(h * span, span)
        return pltpu.make_async_copy(maps_ref.at[:, :, :, lanes], maps_in.at[:, :, :, lanes], maps_sem.at[h])

    near = jnp.where(z < nz // 2, 1, 0)

    def weights(i, t, own):
        zd = near * (nz - 1 - i) + (1 - near) * i
        j = 2 * zd + (c if own else 1 - c)
        lanes = pl.ds(pl.multiple_of(j * outs, outs), outs)
        k = 2 * t + own
        return pltpu.make_async_copy(w_ref.at[t, :, lanes], wbuf.at[k], w_sem.at[k])

    for h in range(halves):
        load_maps(h).start()
    for t in range(2):
        for own in range(2):
            weights(0, t, own).start()
    load_cot = pltpu.make_async_copy(cot_raw, cot_in, cot_sem)
    load_cot.start()
    fill_order(order, chans, False)
    spread_mix(mix_in_ref, wide)
    greet(columns, m, z, c, nz)

    def mine(t, h):
        return pltpu.make_async_copy(ft_ref.at[t, :, pl.ds(h * span, span)], features(0, t, h), keep_sem.at[t, h])

    def cross(axis, t, h):
        return remote(ft_ref.at[t, :, pl.ds(h * span, span)], features(0, t, h), cross_send.at[axis, t, h],
                      cross_recv.at[axis, t, h], (columns[1 + axis], m))

    def cross_wait(axis, t, h):
        here = features(1 + axis, t, h)
        remote(here, here, cross_send.at[axis, t, h], cross_recv.at[axis, t, h], (columns[1 + axis], m)).wait_recv()

    def diagonal(axis, h):
        here = features(2 - axis, 1 - axis, h)
        return remote(here, here, half_send.at[axis, h], half_recv.at[axis, h], (columns[1 + axis], m))

    def diagonal_wait(axis, h):
        here = features(3, 1 - axis, h)
        remote(here, here, half_send.at[axis, h], half_recv.at[axis, h], (columns[1 + axis], m)).wait_recv()

    def onward(h):
        for axis in range(2):
            cross_wait(1 - axis, 1 - axis, h)
            diagonal(axis, h).start()

    narrow = span // 128
    for h in range(halves):

        def pool_row(step, carry, h=h):
            i = step // narrow
            at = pl.multiple_of(step % narrow * 128, 128)
            lanes = pl.ds(pl.multiple_of(h * span + at, 128), 128)
            first = pooled_row(maps_in, 0, i, lanes)
            second = pooled_row(maps_in, 1, i, lanes)
            for t in range(2):
                for j in range(6):
                    value = wide[2 * t] * first[j] + wide[2 * t + 1] * second[j]
                    start = pl.multiple_of((6 * i + j) * chans, chans)
                    cells[t, pl.ds(start, chans), pl.ds(at, 128)] = value.astype(BF16)
            return carry

        load_maps(h).wait()
        lax.fori_loop(0, 6 * narrow, pool_row, 0)
        for t in range(2):
            moved = jnp.dot(order[...], cells[t], preferred_element_type=F32).astype(BF16)
            ft_ref[t, :, pl.ds(h * span, span)] = moved
            f_ref[t, pl.ds(h * span, span), :] = moved.T
        for k in range(2):
            cross(0, k, h).start()
            cross(1, 1 - k, h).start()

    def swap(d, t):
        return remote(sb.at[d, t], rb.at[d, t], core_send.at[d, t], core_recv.at[d, t], (b, sibling))

    def hop(up, d, t):
        return remote(rb.at[d, t], inb.at[up, d, t], line_send.at[d, t], line_recv.at[up, d, t],
                      (b, m + 4 * up - 2))

    step = 64

    def relay(up, dm, t, first):
        zm = up * z + (1 - up) * (nz - 1 - z)
        d = up * dm + (1 - up) * (nz - 1 - dm)

        def go():
            swap(d, t).wait_recv()
            if not first:
                hop(up, d, t).wait_recv()

            def add(k, carry):
                here = pl.ds(pl.multiple_of(k * step, step), step)
                value = pb[d, t, here, :] + rb[d, t, here, :].astype(F32)
                if not first:
                    value += inb[up, d, t, here, :].astype(F32)
                rb[d, t, here, :] = value.astype(BF16)
                return carry

            lax.fori_loop(0, rows // step, add, 0)
            hop(up, d, t).start()

        pl.when((zm == 0 if first else zm > 0) & (zm < dm))(go)

    def produce(i, carry):
        zd = near * (nz - 1 - i) + (1 - near) * i
        for t in range(2):
            for own in range(2):
                weights(i, t, own).wait()
                part = jnp.dot(f_ref[t], wbuf[2 * t + own], preferred_element_type=F32)
                if own:
                    pb[zd, t] = part
                else:
                    sb[zd, t] = part.astype(BF16)
                    swap(zd, t).start()
                pl.when(i < nz - 1)(lambda t=t, own=own: weights(i + 1, t, own).start())
            relay(near, nz - 1 - i, t, True)
        return carry

    lax.fori_loop(0, nz, produce, 0)
    onward(0)
    for t in range(2):
        for h in range(halves):
            mine(t, h).start()
    load_cot.wait()

    def part_towers(k, carry):
        here = pl.ds(pl.multiple_of(k * 16, 16), 16)
        both = cot_in[here, :, :].astype(F32)
        for t in range(2):
            cot_ref[t, here, :] = both[:, t, :].astype(BF16)
        return carry

    lax.fori_loop(0, rows // 16, part_towers, 0)
    for dm in range(nz - 1, 0, -1):
        for t in range(2):
            relay(near, dm, t, False)
            relay(1 - near, dm, t, False)
        if dm == nz - 1:
            for h in range(1, halves):
                onward(h)

    for t in range(2):
        swap(z, t).wait_recv()
        pl.when(z > 0)(lambda t=t: hop(1, z, t).wait_recv())
        pl.when(z < nz - 1)(lambda t=t: hop(0, z, t).wait_recv())

        def gather(k, carry, t=t):
            here = pl.ds(pl.multiple_of(k * step, step), step)
            pb[z, t, here, :] += rb[z, t, here, :].astype(F32)
            for up in range(2):
                inside = z > 0 if up else z < nz - 1

                @pl.when(inside)
                def _(up=up):
                    pb[z, t, here, :] += inb[up, z, t, here, :].astype(F32)

            return carry

        lax.fori_loop(0, rows // step, gather, 0)
    tile, high = 256, 16
    for lane in range(outs // tile):
        lanes = pl.ds(lane * tile, tile)
        bias = [bias_ref[pl.ds(t, 1), lanes] for t in range(2)]
        mix = [mix_ref[k // 2, pl.ds(k % 2, 1), lanes] for k in range(4)]

        def block(k, totals, lanes=lanes, bias=bias, mix=mix):
            here = pl.ds(pl.multiple_of(k * high, high), high)
            hidden = [pb[z, t, here, lanes] + bias[t] for t in range(2)]
            cot = [cot_ref[t, here, lanes].astype(F32) for t in range(2)]
            place = k * high + lax.broadcasted_iota(jnp.int32, (high, tile), 0)
            keep = jnp.where(place < live, 1.0, 0.0)
            terms = head_rows(hidden, cot, keep, mix, act_ref, grad_ref, here, lanes)
            return tuple(a + v[:8] + v[8:] for a, v in zip(totals, terms))

        zero = jnp.zeros((8, tile), F32)
        totals = lax.fori_loop(0, rows // high, block, (zero,) * 6)
        for k in range(6):
            sums_ref[k, :, lanes] = jnp.sum(totals[k], axis=0, keepdims=True)

    for h in range(halves):
        for axis in range(2):
            cross_wait(axis, 1 - axis, h)
            diagonal_wait(axis, h)
            diagonal(axis, h).wait_send()
            for t in range(2):
                cross(axis, t, h).wait_send()
        for t in range(2):
            mine(t, h).wait()
    for d in range(nz):
        for t in range(2):
            swap(d, t).wait_send()
            pl.when(z < d)(lambda d=d, t=t: hop(1, d, t).wait_send())
            pl.when(z > d)(lambda d=d, t=t: hop(0, d, t).wait_send())


def forward_all(mesh, live, maps, weight, cot, bias, mix, mix_in):
    groups, parts = mesh.shape["batch"], mesh.shape["mp"]
    nz = parts // 2
    chans, rows = maps.shape[2:]
    width = weight.shape[1]
    outs = weight.shape[2] // parts
    span = 256
    halves = rows // span
    dma = pltpu.SemaphoreType.DMA
    here = pl.BlockSpec(memory_space=pltpu.VMEM)
    far = pl.BlockSpec(memory_space=pl.ANY)
    return pl.pallas_call(
        functools.partial(forward_kernel, nz),
        in_specs=[pl.BlockSpec(memory_space=pltpu.SMEM), far, far, far, here, here, here],
        out_specs=[far, here, here, here],
        out_shape=[
            jax.ShapeDtypeStruct((2, width, groups * rows), BF16),
            jax.ShapeDtypeStruct((2, rows, outs), BF16),
            jax.ShapeDtypeStruct((2, rows, outs), BF16),
            jax.ShapeDtypeStruct((6, 1, outs), F32),
        ],
        scratch_shapes=[
            pltpu.VMEM(maps.shape, BF16),
            pltpu.VMEM((2, width, span), BF16),
            pltpu.VMEM((width, width), BF16),
            pltpu.VMEM((4, chans, 128), F32),
            pltpu.VMEM((2, rows, width), BF16),
            pltpu.VMEM((2, width, rows), BF16),
            pltpu.VMEM(cot.shape, BF16),
            pltpu.VMEM((2, rows, outs), BF16),
            pltpu.VMEM((4, width, outs), BF16),
            pltpu.VMEM((nz, 2, rows, outs), F32),
            pltpu.VMEM((nz, 2, rows, outs), BF16),
            pltpu.VMEM((nz, 2, rows, outs), BF16),
            pltpu.VMEM((2, nz, 2, rows, outs), BF16),
            dma((halves,)),
            dma,
            dma((4,)),
            dma((nz, 2)),
            dma((nz, 2)),
            dma((nz, 2)),
            dma((2, nz, 2)),
            dma((2, 2, halves)),
            dma((2, 2, halves)),
            dma((2, halves)),
            dma((2, halves)),
            dma((2, halves)),
        ],
        compiler_params=pltpu.CompilerParams(
            collective_id=0, has_side_effects=True, vmem_limit_bytes=VMEM_LIMIT
        ),
        name="forward_all",
    )(live, maps, weight, cot, bias, mix, mix_in)


def turn_mix(wide):
    chans = wide.shape[0]
    rows = lax.broadcasted_iota(jnp.int32, (chans, chans), 0)
    cols = lax.broadcasted_iota(jnp.int32, (chans, chans), 1)
    return jnp.sum(jnp.where(rows == cols, wide[:, :chans], 0.0), axis=0, keepdims=True)


def update_kernel(chunks, ft_ref, s_ref, m_ref, w_ref, maps_ref, acts_ref, sums_ref, mixed_ref,
                  bias_ref, bias_m_ref, in_ref, in_m_ref, out_ref, out_m_ref,
                  grad_to, next_to, moment_to, maps_to, acts_to, bias_g, bias_n, bias_mn,
                  in_g, in_n, in_mn, out_g, out_n, out_mn,
                  ft, s_in, m_in, w_in, g_out, n_out, m_out, maps_mid, acts_mid,
                  ft_sem, in_sem, out_sem, maps_in_sem, maps_out_sem, acts_sem):
    groups, parts, _, rows, tile = s_ref.shape
    steps, ahead, behind = 2 * parts, s_in.shape[0], g_out.shape[0]
    part = maps_mid.shape[0] // chunks

    def loads(i):
        t, j, slot = i // parts, i % parts, i % ahead
        lanes = pl.ds(pl.multiple_of(j * tile, tile), tile)
        return [
            pltpu.make_async_copy(s_ref.at[:, j, t], s_in.at[slot], in_sem.at[slot, 0]),
            pltpu.make_async_copy(m_ref.at[t, :, lanes], m_in.at[slot], in_sem.at[slot, 1]),
            pltpu.make_async_copy(w_ref.at[t, :, lanes], w_in.at[slot], in_sem.at[slot, 2]),
        ]

    def stores(i):
        t, j, slot = i // parts, i % parts, i % behind
        lanes = pl.ds(pl.multiple_of(j * tile, tile), tile)
        return [
            pltpu.make_async_copy(g_out.at[slot], grad_to.at[t, :, lanes], out_sem.at[slot, 0]),
            pltpu.make_async_copy(m_out.at[slot], moment_to.at[t, :, lanes], out_sem.at[slot, 1]),
            pltpu.make_async_copy(n_out.at[slot], next_to.at[t, :, lanes], out_sem.at[slot, 2]),
        ]

    def each(copies, act):
        for copy in copies:
            act(copy)

    start, wait = lambda copy: copy.start(), lambda copy: copy.wait()

    def maps_load(i):
        block = pl.ds(pl.multiple_of(i * part, part), part)
        return pltpu.make_async_copy(maps_ref.at[block], maps_mid.at[block], maps_in_sem.at[i])

    def maps_store(i):
        block = pl.ds(pl.multiple_of(i * part, part), part)
        return pltpu.make_async_copy(maps_mid.at[block], maps_to.at[block], maps_out_sem.at[i])

    load_acts = pltpu.make_async_copy(acts_ref, acts_mid, acts_sem.at[0])
    store_acts = pltpu.make_async_copy(acts_mid, acts_to, acts_sem.at[1])
    towers = [pltpu.make_async_copy(ft_ref.at[t], ft.at[t], ft_sem.at[t]) for t in range(2)]
    towers[0].start()
    for i in range(ahead):
        each(loads(i), start)
    towers[1].start()

    def step(grad, value, moment, rate, at, grad_ref, next_ref, moment_ref):
        after = MOMENTUM * moment[at] + grad
        grad_ref[at] = grad
        moment_ref[at] = after
        next_ref[at] = value[at] - rate * after

    for i in range(2):
        at = (pl.ds(i, 1), slice(None))
        step(sums_ref[4 + i], bias_ref, bias_m_ref, DENSE_RATE, at, bias_g, bias_n, bias_mn)
        for j in range(2):
            at = (i, pl.ds(j, 1), slice(None))
            step(sums_ref[2 * i + j], out_ref, out_m_ref, STITCH_RATE, at, out_g, out_n, out_mn)
            step(turn_mix(mixed_ref[2 * i + j]), in_ref, in_m_ref, STITCH_RATE, at, in_g, in_n, in_mn)

    towers[0].wait()

    def body(i, carry):
        slot, to = i % ahead, i % behind

        @pl.when(i >= ahead)
        def _():
            maps_load(i - ahead).wait()
            maps_store(i - ahead).start()

        pl.when(i < chunks)(lambda: maps_load(i).start())
        pl.when(i == 0)(load_acts.start)

        @pl.when(i == ahead)
        def _():
            load_acts.wait()
            store_acts.start()

        pl.when(i == parts)(towers[1].wait)
        each(loads(i), wait)
        pl.when(i >= behind)(lambda: each(stores(i - behind), wait))
        grad = jnp.dot(
            ft[i // parts], s_in[slot].reshape(groups * rows, tile), preferred_element_type=F32
        )
        g_out[to] = grad
        moment = MOMENTUM * m_in[slot] + grad
        m_out[to] = moment
        n_out[to] = (w_in[slot].astype(F32) - DENSE_RATE * moment).astype(BF16)
        each(stores(i), start)
        pl.when(i + ahead < steps)(lambda: each(loads(i + ahead), start))
        return carry

    lax.fori_loop(0, steps, body, 0)
    for k in range(behind):
        each(stores(steps - behind + k), wait)
    for i in range(chunks):
        maps_store(i).wait()
    store_acts.wait()


def weight_update(ft_all, gathered, moment, weight, maps, acts, sums, mixed, smalls):
    groups, parts, _, rows, outs = gathered.shape
    width = weight.shape[1]
    chunks = 2 * parts - 3
    here = pl.BlockSpec(memory_space=pltpu.VMEM)
    far = pl.BlockSpec(memory_space=pl.ANY)
    ahead, behind = 3, 2
    vmem, dma = pltpu.VMEM, pltpu.SemaphoreType.DMA
    return pl.pallas_call(
        functools.partial(update_kernel, chunks),
        in_specs=[far] * 6 + [here] * (2 + len(smalls)),
        out_specs=[far] * 5 + [here] * 9,
        out_shape=[
            jax.ShapeDtypeStruct(moment.shape, F32),
            jax.ShapeDtypeStruct(moment.shape, BF16),
            jax.ShapeDtypeStruct(moment.shape, F32),
            jax.ShapeDtypeStruct(maps.shape, BF16),
            jax.ShapeDtypeStruct(acts.shape, BF16),
        ]
        + [jax.ShapeDtypeStruct(a.shape, F32) for a in smalls[::2] for _ in range(3)],
        scratch_shapes=[
            vmem((2, width, groups * rows), BF16),
            vmem((ahead, groups, rows, outs), BF16),
            vmem((ahead, width, outs), F32),
            vmem((ahead, width, outs), BF16),
            vmem((behind, width, outs), F32),
            vmem((behind, width, outs), BF16),
            vmem((behind, width, outs), F32),
            vmem(maps.shape, BF16),
            vmem(acts.shape, BF16),
            dma((2,)),
            dma((ahead, 3)),
            dma((behind, 3)),
            dma((chunks,)),
            dma((chunks,)),
            dma((2,)),
        ],
        compiler_params=params(),
        name="weight_update",
    )(ft_all, gathered, moment, weight, maps, acts, sums, mixed, *smalls)


def fast_shards(
    mesh,
    input_maps,
    dense_weight,
    dense_bias,
    stitch_in,
    stitch_out,
    weight_moment,
    bias_moment,
    stitch_in_moment,
    stitch_out_moment,
    cotangent,
    live_rows,
):
    maps = jnp.transpose(input_maps, (1, 3, 2, 0))
    ft_all, grads, acts, sums = forward_all(
        mesh, live_rows, maps, dense_weight, cotangent, dense_bias, stitch_out, stitch_in
    )
    gathered, acts, maps_out, sums, mixed = gather_all(
        mesh, grads, acts, sums, dense_weight, maps, stitch_in
    )
    (
        weight_grad,
        weight_next,
        weight_moment_next,
        maps_grad,
        activations,
        bias_grad,
        bias_next,
        bias_moment_next,
        stitch_in_grad,
        stitch_in_next,
        stitch_in_moment_next,
        stitch_out_grad,
        stitch_out_next,
        stitch_out_moment_next,
    ) = weight_update(
        ft_all,
        gathered,
        weight_moment,
        dense_weight,
        maps_out.reshape((-1,) + maps_out.shape[2:]),
        acts,
        sums,
        mixed,
        [dense_bias, bias_moment, stitch_in, stitch_in_moment, stitch_out, stitch_out_moment],
    )
    maps_grad = jnp.transpose(maps_grad.reshape(maps.shape), (3, 0, 2, 1))
    return (
        activations,
        maps_grad,
        weight_grad,
        bias_grad,
        stitch_in_grad,
        stitch_out_grad,
        weight_next,
        bias_next,
        stitch_in_next,
        stitch_out_next,
        weight_moment_next,
        bias_moment_next,
        stitch_in_moment_next,
        stitch_out_moment_next,
    )


def choose(mesh, *args):
    rows, _, chans, _ = args[0].shape
    outs = args[2].shape[1]
    shape = mesh.shape["batch"] == 4 and mesh.shape["mp"] == 8
    if shape and rows % 512 == 0 and outs % 256 == 0 and chans == 32:
        return fast_shards(mesh, *args)
    return shards(*args)


def solution(mesh):
    in_specs = (
        P("batch", None, "mp", None),
        P(None, "mp", None),
        P(None, "mp"),
        P(None, None, "mp"),
        P(None, None, "mp"),
        P(None, "mp", None),
        P(None, "mp"),
        P(None, None, "mp"),
        P(None, None, "mp"),
        P("batch", None, "mp"),
        P(),
    )
    out_specs = (
        P("batch", None, "mp"),
        P("batch", None, "mp", None),
        P(None, "mp", None),
        P(None, "mp"),
        P(None, None, "mp"),
        P(None, None, "mp"),
        P(None, "mp", None),
        P(None, "mp"),
        P(None, None, "mp"),
        P(None, None, "mp"),
        P(None, "mp", None),
        P(None, "mp"),
        P(None, None, "mp"),
        P(None, None, "mp"),
    )
    body = functools.partial(choose, mesh)
    return jax.shard_map(body, mesh=mesh, in_specs=in_specs, out_specs=out_specs, check_vma=False)
```

```python
import functools

import jax
import jax.numpy as jnp
from jax import lax
from jax.experimental import pallas as pl
from jax.experimental.pallas import tpu as pltpu
from jax.sharding import PartitionSpec as P

MESH = pl.DeviceIdType.MESH
BF16 = jnp.bfloat16
F32 = jnp.float32
VMEM_LIMIT = 60 * 1024 * 1024

MOMENTUM = 0.9
DENSE_RATE = 0.01
STITCH_RATE = 0.1


def pool_table():
    pixels = jnp.arange(169, dtype=jnp.int32)
    cells = jnp.arange(36, dtype=jnp.int32)
    pixel_row = (pixels // 13)[:, None]
    pixel_col = (pixels % 13)[:, None]
    cell_row = (cells // 6)[None, :]
    cell_col = (cells % 6)[None, :]
    inside = (
        (pixel_row >= 2 * cell_row)
        & (pixel_row <= 2 * cell_row + 2)
        & (pixel_col >= 2 * cell_col)
        & (pixel_col <= 2 * cell_col + 2)
    )
    return inside.astype(jnp.float32)


def gelu_tanh(value):
    return jax.nn.gelu(value, approximate=True)


def head(summed, cotangent, keep, dense_bias, stitch_out):
    hidden = summed + dense_bias[None]
    active, gelu_pull = jax.vjp(gelu_tanh, hidden)
    mixed = stitch_out[None, :, 0] * active[:, 0:1] + stitch_out[None, :, 1] * active[:, 1:2]
    activations = (mixed * keep[:, None, None]).astype(jnp.bfloat16)
    pulled = cotangent.astype(jnp.float32) * keep[:, None, None]
    stitch_out_grad = jnp.einsum("nio,njo->ijo", pulled, active, precision=lax.Precision.HIGHEST)
    active_grad = stitch_out[0][None] * pulled[:, 0:1] + stitch_out[1][None] * pulled[:, 1:2]
    hidden_grad = gelu_pull(active_grad)[0]
    bias_grad = jnp.sum(hidden_grad, axis=0)
    return (activations, hidden_grad.astype(jnp.bfloat16), bias_grad, stitch_out_grad)


def rows_layer(features, cotangent, keep, dense_weight, dense_bias, stitch_out):
    terms = jnp.einsum("ntk,tko->nto", features, dense_weight, preferred_element_type=jnp.float32)
    summed = lax.psum_scatter(terms, "mp", scatter_dimension=2, tiled=True)
    activations, summed_grad, bias_grad, stitch_out_grad = head(
        summed, cotangent, keep, dense_bias, stitch_out
    )
    piece = lax.all_gather(summed_grad, "mp", axis=2, tiled=True)
    inputs_grad = jnp.einsum(
        "nto,tko->ntk", piece, dense_weight, preferred_element_type=jnp.float32
    )
    update = jnp.einsum("ntk,nto->tko", features, piece, preferred_element_type=jnp.float32)
    weight_grad = update
    inputs_grad, weight_grad = (inputs_grad, weight_grad)
    return (activations, inputs_grad.astype(jnp.bfloat16), weight_grad, bias_grad, stitch_out_grad)


def dense_layer(features, cotangent, keep, dense_weight, dense_bias, stitch_out):
    return rows_layer(features, cotangent, keep, dense_weight, dense_bias, stitch_out)


def shards(
    input_maps,
    dense_weight,
    dense_bias,
    stitch_in,
    stitch_out,
    weight_moment,
    bias_moment,
    stitch_in_moment,
    stitch_out_moment,
    cotangent,
    live_rows,
):
    rows = input_maps.shape[0]
    chans = input_maps.shape[2]
    width = chans * 36
    group = lax.axis_index("batch")
    positions = jnp.arange(rows, dtype=jnp.int32)
    keep = (positions < live_rows[group]).astype(jnp.float32)
    table = pool_table()
    pooled = (
        jnp.einsum(
            "ntck,kq->ntcq",
            input_maps,
            table.astype(jnp.bfloat16),
            preferred_element_type=jnp.float32,
        )
        / 9.0
    )
    stitched = (
        stitch_in[None, :, 0, :, None] * pooled[:, 0:1]
        + stitch_in[None, :, 1, :, None] * pooled[:, 1:2]
    )
    features = stitched.reshape(rows, 2, width).astype(jnp.bfloat16)
    activations, inputs_grad, weight_grad, bias_grad, stitch_out_grad = dense_layer(
        features, cotangent, keep, dense_weight, dense_bias, stitch_out
    )
    stitched_grad = inputs_grad.astype(jnp.float32).reshape(rows, 2, chans, 36)
    stitch_in_grad = jnp.einsum(
        "nicq,njcq->ijc", stitched_grad, pooled, precision=lax.Precision.HIGHEST
    )
    pooled_grad = (
        stitch_in[0][None, :, :, None] * stitched_grad[:, 0:1]
        + stitch_in[1][None, :, :, None] * stitched_grad[:, 1:2]
    )
    maps_grad = jnp.einsum(
        "ntcq,kq->ntck", pooled_grad / 9.0, table, precision=lax.Precision.HIGHEST
    ).astype(jnp.bfloat16)
    weight_grad, bias_grad, stitch_in_grad, stitch_out_grad = lax.psum(
        (weight_grad, bias_grad, stitch_in_grad, stitch_out_grad), "batch"
    )
    weight_moment_next = MOMENTUM * weight_moment + weight_grad
    weight_next = (dense_weight.astype(jnp.float32) - DENSE_RATE * weight_moment_next).astype(
        jnp.bfloat16
    )
    bias_moment_next = MOMENTUM * bias_moment + bias_grad
    bias_next = dense_bias - DENSE_RATE * bias_moment_next
    stitch_in_moment_next = MOMENTUM * stitch_in_moment + stitch_in_grad
    stitch_in_next = stitch_in - STITCH_RATE * stitch_in_moment_next
    stitch_out_moment_next = MOMENTUM * stitch_out_moment + stitch_out_grad
    stitch_out_next = stitch_out - STITCH_RATE * stitch_out_moment_next
    return (
        activations,
        maps_grad,
        weight_grad,
        bias_grad,
        stitch_in_grad,
        stitch_out_grad,
        weight_next,
        bias_next,
        stitch_in_next,
        stitch_out_next,
        weight_moment_next,
        bias_moment_next,
        stitch_in_moment_next,
        stitch_out_moment_next,
    )


def params():
    return pltpu.CompilerParams(vmem_limit_bytes=VMEM_LIMIT)


def full(shape):
    return pl.BlockSpec(shape, lambda *_: (0,) * len(shape))


def fill_order(order, chans, inverse):
    size = order.shape[0]
    rows = lax.broadcasted_iota(jnp.int32, (size, size), 0)
    cols = lax.broadcasted_iota(jnp.int32, (size, size), 1)
    natural, cells = (cols, rows) if inverse else (rows, cols)
    shift = chans.bit_length() - 1
    hit = natural == 36 * (cells & (chans - 1)) + (cells >> shift)
    order[...] = jnp.where(hit, 1.0, 0.0).astype(BF16)


def spread_mix(mix_ref, wide):
    chans = wide.shape[1]
    rows = lax.broadcasted_iota(jnp.int32, (chans, chans), 0)
    cols = lax.broadcasted_iota(jnp.int32, (chans, chans), 1)
    for k in range(4):
        line = jnp.broadcast_to(mix_ref[k // 2, pl.ds(k % 2, 1), :], (chans, chans))
        column = jnp.sum(jnp.where(rows == cols, line, 0.0), axis=1, keepdims=True)
        wide[k] = jnp.broadcast_to(column, wide.shape[1:])


def pooled_row(maps_ref, tower, i, lanes):
    sums = None
    for dy in range(3):
        line = [maps_ref[tower, 26 * i + 13 * dy + x, :, lanes].astype(F32) for x in range(13)]
        cells = [line[2 * j] + line[2 * j + 1] + line[2 * j + 2] for j in range(6)]
        sums = cells if sums is None else [a + b for a, b in zip(sums, cells)]
    return [s * (1.0 / 9.0) for s in sums]


def gelu_parts(v):
    root = 0.7978845608028654
    square = v * v
    tanh = jnp.tanh(root * v * (1.0 + 0.044715 * square))
    half = 0.5 * (1.0 + tanh)
    slope = half + 0.5 * v * (1.0 - tanh * tanh) * root * (1.0 + 3.0 * 0.044715 * square)
    return v * half, slope


def neighbours():
    b, m = lax.axis_index("batch"), lax.axis_index("mp")
    columns = (b, b + 1 - 2 * (b % 2), b + 2 - 4 * (b // 2), 3 - b)
    return b, m, m // 2, m % 2, columns


def greet(columns, m, z, c, nz):
    b, bx, by, _ = columns
    sibling = m + 1 - 2 * c
    barrier = pltpu.get_barrier_semaphore()

    def signal(bb, mm):
        pl.semaphore_signal(barrier, inc=1, device_id=(bb, mm), device_id_type=MESH)

    signal(bx, m)
    signal(by, m)
    signal(b, sibling)
    pl.when(z > 0)(lambda: signal(b, m - 2))
    pl.when(z < nz - 1)(lambda: signal(b, m + 2))
    pl.semaphore_wait(barrier, 3 + jnp.where(z > 0, 1, 0) + jnp.where(z < nz - 1, 1, 0))


def remote(src, dst, send, recv, device):
    return pltpu.make_async_remote_copy(
        src_ref=src, dst_ref=dst, send_sem=send, recv_sem=recv, device_id=device, device_id_type=MESH
    )


def unpool_row(chans, i, lanes, maps_ref, out_ref, cells, above, total, wide):
    spans = [pl.ds(pl.multiple_of((6 * i + j) * chans, chans), chans) for j in range(6)]
    pooled = [pooled_row(maps_ref, t, i, lanes) for t in range(2)]
    sums = [total[k] for k in range(4)]
    for j in range(6):
        for t in range(2):
            grad = cells[t, spans[j], lanes]
            for s in range(2):
                sums[2 * t + s] += grad * pooled[s][j]
    for k in range(4):
        total[k] = sums[k]
    for t in range(2):
        mixed = []
        for j in range(6):
            value = wide[t] * cells[0, spans[j], lanes] + wide[2 + t] * cells[1, spans[j], lanes]
            mixed.append(value * (1.0 / 9.0))
        for x in range(13):
            if x % 2 == 1 or x == 0:
                value = mixed[x // 2]
            elif x == 12:
                value = mixed[5]
            else:
                value = mixed[x // 2 - 1] + mixed[x // 2]
            out_ref[t, 26 * i + x, :, lanes] = (value + above[t, x, :, lanes]).astype(BF16)
            out_ref[t, 26 * i + 13 + x, :, lanes] = value.astype(BF16)
            above[t, x, :, lanes] = value


def gather_phase(nz, cut, s_ref, acts_in, sums_ref, w_ref, maps_in, wide,
                 g_ref, acts_to, out_ref, total_ref, mixed_ref, sums_in, mix_in, sems,
                 keep_sem, out_sem, w_sem, col_sem, acts_sem,
                 acts_out, maps_out, wbuf, col, grads, cells, order, above, mix_total):
    (line_send, line_recv, cross_send, cross_recv, half_send, half_recv, core_send, core_recv,
     small_send, small_recv, sums_mid, mix_mid) = sems
    b, m, z, c, columns = neighbours()
    rows = s_ref.shape[1]
    spans = (pl.ds(0, cut), pl.ds(cut, rows - cut))
    sibling = m + 1 - 2 * c

    def small(kind, axis, src, dst):
        return remote(src, dst, small_send.at[kind, axis], small_recv.at[kind, axis], (columns[1 + axis], m))

    def place(p, r, zz):
        return g_ref.at[columns[r], 2 * zz + c, :, spans[p], :]

    def half(p, r, zz, t):
        return g_ref.at[columns[r], 2 * zz + c, t, spans[p], :]

    def line(k, zz, up, own=False):
        p, r = (0, 0) if k == 0 else (1, k - 1)
        src = s_ref.at[:, spans[p], :] if own else place(p, r, zz)
        side = 1 if up else 0
        to = m + 2 if up else m - 2
        return remote(src, place(p, r, zz), line_send.at[side, k, zz], line_recv.at[k, zz], (b, to))

    def cross(p, axis, zz, own=False):
        src = s_ref.at[:, spans[p], :] if own else place(p, 0, zz)
        slot = zz if p == 0 else nz
        return remote(
            src, place(p, 0, zz), cross_send.at[axis, slot], cross_recv.at[axis, slot], (columns[1 + axis], m)
        )

    def cross_wait(p, axis, zz):
        slot = zz if p == 0 else nz
        here = place(p, 1 + axis, zz)
        remote(here, here, cross_send.at[axis, slot], cross_recv.at[axis, slot], (columns[1 + axis], m)).wait_recv()

    def diagonal(p, axis, zz):
        slot = zz if p == 0 else nz
        block = half(p, 2 - axis, zz, 1 - axis)
        return remote(block, block, half_send.at[axis, slot], half_recv.at[axis, slot], (columns[1 + axis], m))

    def diagonal_wait(p, axis, zz):
        slot = zz if p == 0 else nz
        block = half(p, 3, zz, 1 - axis)
        remote(block, block, half_send.at[axis, slot], half_recv.at[axis, slot], (columns[1 + axis], m)).wait_recv()

    def core(p, r, zz, own=False):
        src = s_ref.at[:, spans[p], :] if own else place(p, r, zz)
        return remote(src, place(p, r, zz), core_send.at[p, r, zz], core_recv.at[p, r, zz], (b, sibling))

    def core_wait(p, r, zz):
        block = g_ref.at[columns[r], 2 * zz + 1 - c, :, spans[p], :]
        remote(block, block, core_send.at[p, r, zz], core_recv.at[p, r, zz], (b, sibling)).wait_recv()

    def sides(d, body):
        if d == 0:
            body(z, None)
            return
        pl.when(z + d < nz)(lambda: body(z + d, False))
        pl.when(z - d >= 0)(lambda: body(z - d, True))

    def onward(k, zz, up):
        if up:
            pl.when(z < nz - 1)(lambda: line(k, zz, True).start())
        else:
            pl.when(z > 0)(lambda: line(k, zz, False).start())

    mine = pltpu.make_async_copy(s_ref, g_ref.at[b, m], keep_sem)
    cross(1, 0, z, True).start()
    cross(1, 1, z, True).start()
    pl.when(z < nz - 1)(lambda: line(0, z, True, True).start())
    pl.when(z > 0)(lambda: line(0, z, False, True).start())
    cross(0, 0, z, True).start()
    cross(0, 1, z, True).start()
    pl.when(z < nz - 1)(lambda: line(1, z, True, True).start())
    pl.when(z > 0)(lambda: line(1, z, False, True).start())
    first_sums = small(0, 0, sums_ref, sums_in.at[0])
    first_sums.start()
    core(0, 0, z, True).start()
    core(1, 0, z, True).start()
    mine.start()

    def pass_cross(p, zz):
        for axis in range(2):
            cross_wait(p, axis, zz)
            diagonal(p, 1 - axis, zz).start()
            core(p, 1 + axis, zz).start()

    def end_diagonal(p, zz):
        for axis in range(2):
            diagonal_wait(p, axis, zz)
        core(p, 3, zz).start()

    def arrive(zz, up):
        line(0, zz, up).wait_recv()
        onward(0, zz, up)
        cross(0, 0, zz).start()
        cross(0, 1, zz).start()
        core(0, 0, zz).start()
        line(1, zz, up).wait_recv()
        onward(1, zz, up)
        core(1, 0, zz).start()

    def late(zz, up):
        for k in range(2, 5):
            line(k, zz, up).wait_recv()
            onward(k, zz, up)
            core(1, k - 1, zz).start()

    def spread():
        for k in range(2, 5):
            pl.when(z < nz - 1)(lambda k=k: line(k, z, True).start())
            pl.when(z > 0)(lambda k=k: line(k, z, False).start())

    def join_towers(k, carry):
        here = pl.ds(pl.multiple_of(k * 16, 16), 16)
        both = jnp.stack([acts_in[t, here, :].astype(F32) for t in range(2)], axis=1)
        acts_out[here, :, :] = both.astype(BF16)
        return carry

    pass_cross(1, z)
    lax.fori_loop(0, rows // 16, join_towers, 0)
    store_acts = pltpu.make_async_copy(acts_out, acts_to, acts_sem)
    store_acts.start()
    sides(1, arrive)
    pass_cross(0, z)
    end_diagonal(1, z)
    for d in range(2, nz):
        sides(d, arrive)
        if d == 2:
            spread()
    mine.wait()
    width, chans = w_ref.shape[1], maps_in.shape[2]
    outs = s_ref.shape[2]
    piece = wbuf.shape[1]
    pieces = width // piece

    def weights(k):
        t, at = k // pieces, k % pieces * piece
        return pltpu.make_async_copy(w_ref.at[t, pl.ds(at, piece), :], wbuf.at[k % 2], w_sem.at[k % 2])

    def column(t, j):
        return pltpu.make_async_copy(
            g_ref.at[b, j, t], col.at[:, pl.ds(j * outs, outs)], col_sem.at[j]
        )

    def features_grad(t):
        for k in range(t * pieces, (t + 1) * pieces):
            if k + 1 < 2 * pieces:
                weights(k + 1).start()
            weights(k).wait()
            if k == t * pieces:
                for j in range(2 * nz):
                    column(t, j).wait()
            value = lax.dot_general(
                wbuf[k % 2], col[...], (((1,), (1,)), ((), ())), preferred_element_type=F32
            )
            grads[pl.ds(k % pieces * piece, piece), :] = value.astype(BF16)
        cells[t] = jnp.dot(order[...], grads[...], preferred_element_type=F32)

    blocks = rows // 128

    def maps_back(step, carry):
        i = step // blocks
        lanes = pl.ds(pl.multiple_of(step % blocks * 128, 128), 128)
        unpool_row(chans, i, lanes, maps_in, maps_out, cells, above, mix_total, wide)
        return carry

    weights(0).start()
    fill_order(order, chans, True)
    above[...] = jnp.zeros_like(above)
    mix_total[...] = jnp.zeros_like(mix_total)
    first_sums.wait()
    sums_mid[...] = sums_ref[...] + sums_in[0]
    second_sums = small(0, 1, sums_mid, sums_in.at[1])
    second_sums.start()
    sides(1, lambda zz, up: pass_cross(0, zz))
    for zz in range(nz):
        for p in range(2):
            core_wait(p, 0, zz)
    for j in range(2 * nz):
        column(0, j).start()
    features_grad(0)
    for j in range(2 * nz):
        column(1, j).start()
    sides(1, late)
    features_grad(1)
    end_diagonal(0, z)
    outer = (z == 0) | (z == nz - 1)
    inner = (z > 0) & (z < nz - 1)
    pl.when(inner)(lambda: sides(2, late))
    pl.when(outer)(lambda: sides(2, lambda zz, up: pass_cross(0, zz)))
    lax.fori_loop(0, 3 * blocks, maps_back, 0)
    pl.when(outer)(lambda: sides(2, late))
    lax.fori_loop(3 * blocks, 6 * blocks, maps_back, 0)
    for t in range(2):
        for x in range(13):
            maps_out[t, 156 + x] = above[t, x].astype(BF16)
    store_maps = pltpu.make_async_copy(maps_out, out_ref, out_sem)
    store_maps.start()
    for k in range(4):
        mix_in[0, k] = jnp.broadcast_to(jnp.sum(mix_total[k], axis=1, keepdims=True), (chans, 128))
    first_mix = small(1, 0, mix_in.at[0], mix_in.at[1])
    first_mix.start()
    pl.when(inner)(lambda: sides(2, lambda zz, up: pass_cross(0, zz)))
    sides(1, lambda zz, up: end_diagonal(0, zz))
    sides(3, lambda zz, up: pass_cross(0, zz))
    first_mix.wait()
    mix_mid[...] = mix_in[0] + mix_in[1]
    second_mix = small(1, 1, mix_mid, mix_in.at[2])
    second_mix.start()
    sides(2, lambda zz, up: end_diagonal(0, zz))
    sides(3, late)
    sides(3, lambda zz, up: end_diagonal(0, zz))
    second_sums.wait()
    total_ref[...] = sums_mid[...] + sums_in[1]
    second_mix.wait()
    mixed_ref[...] = mix_mid[...] + mix_in[2]
    store_maps.wait()
    store_acts.wait()

    for zz in range(nz):
        for r in range(4):
            for p in range(2):
                if r > 0:
                    core_wait(p, r, zz)
                core(p, r, zz).wait_send()
        for axis in range(2):
            cross(0, axis, zz).wait_send()
            diagonal(0, axis, zz).wait_send()
        for k in range(5):
            pl.when((z < nz - 1) & (z >= zz))(lambda k=k, zz=zz: line(k, zz, True).wait_send())
            pl.when((z > 0) & (z <= zz))(lambda k=k, zz=zz: line(k, zz, False).wait_send())
    for axis in range(2):
        cross(1, axis, z).wait_send()
        diagonal(1, axis, z).wait_send()


def head_rows(hidden, cot, keep, mix, act_ref, grad_ref, here, lanes):
    active, slope, pulled = [], [], []
    for t in range(2):
        value, rate = gelu_parts(hidden[t])
        active.append(value)
        slope.append(rate)
        pulled.append(cot[t] * keep)
    for i in range(2):
        mixed = mix[2 * i] * active[0] + mix[2 * i + 1] * active[1]
        act_ref[i, here, lanes] = (mixed * keep).astype(BF16)
    terms = [pulled[i] * active[j] for i in range(2) for j in range(2)]
    for j in range(2):
        grad = (mix[j] * pulled[0] + mix[2 + j] * pulled[1]) * slope[j]
        grad_ref[j, here, lanes] = grad.astype(BF16)
        terms.append(grad)
    return terms


def step_kernel(nz, cut, live_ref, maps_ref, w_ref, cot_raw, bias_ref, mix_ref, mix_in_ref,
                g_ref, fta_ref, acts_to, out_ref, total_ref, mixed_ref,
                maps_in, rb, inb, ft_ref, s_ref, acts_in, sums_ref, wide, sums_in, mix_in,
                maps_sem, swap_send, swap_recv, hop_send, hop_recv,
                feat_send, feat_recv, turn_send, turn_recv, feat_keep, *rest):
    b, m, z, c, columns = neighbours()
    sibling = m + 1 - 2 * c
    chans, rows = maps_in.shape[2:]
    width, outs = w_ref.shape[1], s_ref.shape[2]
    span = rows // 2

    def load_maps(h):
        lanes = pl.ds(h * span, span)
        return pltpu.make_async_copy(maps_ref.at[:, :, :, lanes], maps_in.at[:, :, :, lanes], maps_sem.at[h])

    for h in range(2):
        load_maps(h).start()

    def features(r, t, h):
        start = pl.multiple_of(columns[r] * rows + h * span, span)
        return fta_ref.at[t, :, pl.ds(start, span)]

    def mine(t, h):
        return pltpu.make_async_copy(ft_ref.at[t, :, pl.ds(h * span, span)], features(0, t, h), feat_keep.at[t, h])

    def feature(axis, t, h):
        return remote(ft_ref.at[t, :, pl.ds(h * span, span)], features(0, t, h), feat_send.at[axis, t, h],
                      feat_recv.at[axis, t, h], (columns[1 + axis], m))

    def feature_wait(axis, t, h):
        here = features(1 + axis, t, h)
        remote(here, here, feat_send.at[axis, t, h], feat_recv.at[axis, t, h], (columns[1 + axis], m)).wait_recv()

    def turn(axis, h):
        here = features(2 - axis, 1 - axis, h)
        return remote(here, here, turn_send.at[axis, h], turn_recv.at[axis, h], (columns[1 + axis], m))

    def turn_wait(axis, h):
        here = features(3, 1 - axis, h)
        remote(here, here, turn_send.at[axis, h], turn_recv.at[axis, h], (columns[1 + axis], m)).wait_recv()

    def forward(cells, order, f_ref, cot_in, cot_ref, wbuf, pb, sb, cot_sem, w_sem):
        live = live_ref[b]
        near = jnp.where(z < nz // 2, 1, 0)

        def weights(i, t, own):
            zd = near * (nz - 1 - i) + (1 - near) * i
            j = 2 * zd + (c if own else 1 - c)
            lanes = pl.ds(pl.multiple_of(j * outs, outs), outs)
            k = 2 * t + own
            return pltpu.make_async_copy(w_ref.at[t, :, lanes], wbuf.at[k], w_sem.at[k])

        for t in range(2):
            for own in range(2):
                weights(0, t, own).start()
        load_cot = pltpu.make_async_copy(cot_raw, cot_in, cot_sem)
        load_cot.start()
        fill_order(order, chans, False)
        spread_mix(mix_in_ref, wide)
        greet(columns, m, z, c, nz)

        def swap(d, t, h):
            here = pl.ds(h * span, span)
            return remote(sb.at[d, t, here], rb.at[d, t, here], swap_send.at[d, t, h], swap_recv.at[d, t, h], (b, sibling))

        def hop(up, d, t, h):
            here = pl.ds(h * span, span)
            return remote(rb.at[d, t, here], inb.at[d + up, t, here], hop_send.at[d, t, h], hop_recv.at[up, d, t, h],
                          (b, m + 4 * up - 2))

        step = 64

        def relay(up, dm, t, h, first):
            zm = up * z + (1 - up) * (nz - 1 - z)
            d = up * dm + (1 - up) * (nz - 1 - dm)

            def go():
                swap(d, t, h).wait_recv()
                if not first:
                    hop(up, d, t, h).wait_recv()

                def add(k, carry):
                    here = pl.ds(pl.multiple_of(h * span + k * step, step), step)
                    value = pb[d, t, here, :] + rb[d, t, here, :].astype(F32)
                    if not first:
                        value += inb[d + up, t, here, :].astype(F32)
                    rb[d, t, here, :] = value.astype(BF16)
                    return carry

                lax.fori_loop(0, span // step, add, 0)
                hop(up, d, t, h).start()

            pl.when((zm == 0 if first else zm > 0) & (zm < dm))(go)

        narrow = span // 128

        def pool(h):
            def pool_row(step, carry):
                i = step // narrow
                at = pl.multiple_of(step % narrow * 128, 128)
                lanes = pl.ds(pl.multiple_of(h * span + at, 128), 128)
                first = pooled_row(maps_in, 0, i, lanes)
                second = pooled_row(maps_in, 1, i, lanes)
                for t in range(2):
                    for j in range(6):
                        value = wide[2 * t] * first[j] + wide[2 * t + 1] * second[j]
                        start = pl.multiple_of((6 * i + j) * chans, chans)
                        cells[t, pl.ds(start, chans), pl.ds(at, 128)] = value.astype(BF16)
                return carry

            load_maps(h).wait()
            lax.fori_loop(0, 6 * narrow, pool_row, 0)
            for t in range(2):
                moved = jnp.dot(order[...], cells[t], preferred_element_type=F32).astype(BF16)
                ft_ref[t, :, pl.ds(h * span, span)] = moved
                f_ref[t, pl.ds(h * span, span), :] = moved.T
            for k in range(2):
                feature(0, k, h).start()
                feature(1, 1 - k, h).start()

        def produce(i, h):
            zd = near * (nz - 1 - i) + (1 - near) * i
            here = pl.ds(h * span, span)
            for t in range(2):
                for own in range(2):
                    if h == 0:
                        weights(i, t, own).wait()
                    part = jnp.dot(f_ref[t, here, :], wbuf[2 * t + own], preferred_element_type=F32)
                    if own:
                        pb[zd, t, here, :] = part
                    else:
                        sb[zd, t, here, :] = part.astype(BF16)
                        swap(zd, t, h).start()
                    if h == 1:
                        pl.when(i < nz - 1)(lambda t=t, own=own: weights(i + 1, t, own).start())
                relay(near, nz - 1 - i, t, h, True)

        for h in range(2):
            pool(h)
            produce(0, h)

        def both(i, carry):
            for h in range(2):
                produce(i, h)
            return carry

        lax.fori_loop(1, nz, both, 0)

        def onward(h):
            for axis in range(2):
                feature_wait(1 - axis, 1 - axis, h)
                turn(axis, h).start()

        onward(0)
        for t in range(2):
            for h in range(2):
                mine(t, h).start()
        load_cot.wait()

        def part_towers(k, carry):
            here = pl.ds(pl.multiple_of(k * 16, 16), 16)
            both = cot_in[here, :, :].astype(F32)
            for t in range(2):
                cot_ref[t, here, :] = both[:, t, :].astype(BF16)
            return carry

        lax.fori_loop(0, rows // 16, part_towers, 0)
        for dm in range(nz - 1, 0, -1):
            for h in range(2):
                for t in range(2):
                    relay(near, dm, t, h, False)
                    relay(1 - near, dm, t, h, False)
            if dm == nz - 1:
                onward(1)

        tile, high = 256, 16
        for h in range(2):
            for t in range(2):
                swap(z, t, h).wait_recv()
                pl.when(z > 0)(lambda t=t, h=h: hop(1, z, t, h).wait_recv())
                pl.when(z < nz - 1)(lambda t=t, h=h: hop(0, z, t, h).wait_recv())

                def gather(k, carry, t=t, h=h):
                    here = pl.ds(pl.multiple_of(h * span + k * step, step), step)
                    pb[z, t, here, :] += rb[z, t, here, :].astype(F32)
                    for up in range(2):
                        inside = z > 0 if up else z < nz - 1

                        @pl.when(inside)
                        def _(up=up):
                            pb[z, t, here, :] += inb[z + up, t, here, :].astype(F32)

                    return carry

                lax.fori_loop(0, span // step, gather, 0)
            for lane in range(outs // tile):
                lanes = pl.ds(lane * tile, tile)
                bias = [bias_ref[pl.ds(t, 1), lanes] for t in range(2)]
                mix = [mix_ref[k // 2, pl.ds(k % 2, 1), lanes] for k in range(4)]

                def block(k, totals, lanes=lanes, bias=bias, mix=mix):
                    here = pl.ds(pl.multiple_of(k * high, high), high)
                    hidden = [pb[z, t, here, lanes] + bias[t] for t in range(2)]
                    cot = [cot_ref[t, here, lanes].astype(F32) for t in range(2)]
                    place = k * high + lax.broadcasted_iota(jnp.int32, (high, tile), 0)
                    keep = jnp.where(place < live, 1.0, 0.0)
                    terms = head_rows(hidden, cot, keep, mix, acts_in, s_ref, here, lanes)
                    return tuple(a + v[:8] + v[8:] for a, v in zip(totals, terms))

                zero = jnp.zeros((8, tile), F32)
                count = span // high
                totals = lax.fori_loop(h * count, (h + 1) * count, block, (zero,) * 6)
                for k in range(6):
                    value = jnp.sum(totals[k], axis=0, keepdims=True)
                    sums_ref[k, :, lanes] = value if h == 0 else sums_ref[k, :, lanes] + value
        for d in range(nz):
            for t in range(2):
                for h in range(2):
                    swap(d, t, h).wait_send()
                    pl.when(z < d)(lambda d=d, t=t, h=h: hop(1, d, t, h).wait_send())
                    pl.when(z > d)(lambda d=d, t=t, h=h: hop(0, d, t, h).wait_send())

    vmem, dma = pltpu.VMEM, pltpu.SemaphoreType.DMA
    pl.run_scoped(
        forward,
        vmem((2, width, span), BF16),
        vmem((width, width), BF16),
        vmem((2, rows, width), BF16),
        vmem(cot_raw.shape, BF16),
        vmem((2, rows, outs), BF16),
        vmem((4, width, outs), BF16),
        vmem((nz, 2, rows, outs), F32),
        vmem((nz, 2, rows, outs), BF16),
        dma,
        dma((4,)),
    )
    pl.run_scoped(
        functools.partial(gather_phase, nz, cut, s_ref, acts_in, sums_ref, w_ref, maps_in, wide,
                          g_ref, acts_to, out_ref, total_ref, mixed_ref, sums_in, mix_in, rest),
        dma,
        dma,
        dma((2,)),
        dma((2 * nz,)),
        dma,
        vmem((rows, 2, outs), BF16),
        vmem(maps_in.shape, BF16),
        vmem((2, width // 3, 2 * nz * outs), BF16),
        vmem((rows, 2 * nz * outs), BF16),
        vmem((width, rows), BF16),
        vmem((2, width, rows), F32),
        vmem((width, width), BF16),
        vmem((2, 13, chans, rows), F32),
        vmem((4, chans, 128), F32),
    )
    for h in range(2):
        for axis in range(2):
            feature_wait(axis, 1 - axis, h)
            turn_wait(axis, h)
            turn(axis, h).wait_send()
            for t in range(2):
                feature(axis, t, h).wait_send()
        for t in range(2):
            mine(t, h).wait()


def step_all(mesh, live, maps, weight, cot, bias, mix, mix_in):
    groups, parts = mesh.shape["batch"], mesh.shape["mp"]
    nz = parts // 2
    chans, rows = maps.shape[2:]
    width = weight.shape[1]
    outs = weight.shape[2] // parts
    cut = rows * 25 // 32
    vmem, dma = pltpu.VMEM, pltpu.SemaphoreType.DMA
    here = pl.BlockSpec(memory_space=pltpu.VMEM)
    far = pl.BlockSpec(memory_space=pl.ANY)
    sums = (6, 1, outs)
    return pl.pallas_call(
        functools.partial(step_kernel, nz, cut),
        in_specs=[pl.BlockSpec(memory_space=pltpu.SMEM), far, far, far, here, here, here],
        out_specs=[far, far, far, far, here, here],
        out_shape=[
            jax.ShapeDtypeStruct((groups, parts, 2, rows, outs), BF16),
            jax.ShapeDtypeStruct((2, width, groups * rows), BF16),
            jax.ShapeDtypeStruct((rows, 2, outs), BF16),
            jax.ShapeDtypeStruct(maps.shape, BF16),
            jax.ShapeDtypeStruct(sums, F32),
            jax.ShapeDtypeStruct((4, chans, 128), F32),
        ],
        scratch_shapes=[
            vmem(maps.shape, BF16),
            vmem((nz, 2, rows, outs), BF16),
            vmem((nz + 1, 2, rows, outs), BF16),
            vmem((2, width, rows), BF16),
            vmem((2, rows, outs), BF16),
            vmem((2, rows, outs), BF16),
            vmem(sums, F32),
            vmem((4, chans, 128), F32),
            vmem((2,) + sums, F32),
            vmem((3, 4, chans, 128), F32),
            dma((2,)),
            dma((nz, 2, 2)),
            dma((nz, 2, 2)),
            dma((nz, 2, 2)),
            dma((2, nz, 2, 2)),
            dma((2, 2, 2)),
            dma((2, 2, 2)),
            dma((2, 2)),
            dma((2, 2)),
            dma((2, 2)),
            dma((2, 5, nz)),
            dma((5, nz)),
            dma((2, nz + 1)),
            dma((2, nz + 1)),
            dma((2, nz + 1)),
            dma((2, nz + 1)),
            dma((2, 4, nz)),
            dma((2, 4, nz)),
            dma((2, 2)),
            dma((2, 2)),
            vmem(sums, F32),
            vmem((4, chans, 128), F32),
        ],
        compiler_params=pltpu.CompilerParams(
            collective_id=0, has_side_effects=True, vmem_limit_bytes=VMEM_LIMIT
        ),
        name="step_all",
    )(live, maps, weight, cot, bias, mix, mix_in)


def turn_mix(wide):
    chans = wide.shape[0]
    rows = lax.broadcasted_iota(jnp.int32, (chans, chans), 0)
    cols = lax.broadcasted_iota(jnp.int32, (chans, chans), 1)
    return jnp.sum(jnp.where(rows == cols, wide[:, :chans], 0.0), axis=0, keepdims=True)


def update_kernel(chunks, ft_ref, s_ref, m_ref, w_ref, maps_ref, acts_ref, sums_ref, mixed_ref,
                  bias_ref, bias_m_ref, in_ref, in_m_ref, out_ref, out_m_ref,
                  grad_to, next_to, moment_to, maps_to, acts_to, bias_g, bias_n, bias_mn,
                  in_g, in_n, in_mn, out_g, out_n, out_mn,
                  ft, s_in, m_in, w_in, g_out, n_out, m_out, maps_mid, acts_mid,
                  ft_sem, in_sem, out_sem, maps_in_sem, maps_out_sem, acts_sem):
    groups, parts, _, rows, tile = s_ref.shape
    steps, ahead, behind = 2 * parts, s_in.shape[0], g_out.shape[0]
    part = maps_mid.shape[0] // chunks

    def loads(i):
        t, j, slot = i // parts, i % parts, i % ahead
        lanes = pl.ds(pl.multiple_of(j * tile, tile), tile)
        return [
            pltpu.make_async_copy(s_ref.at[:, j, t], s_in.at[slot], in_sem.at[slot, 0]),
            pltpu.make_async_copy(m_ref.at[t, :, lanes], m_in.at[slot], in_sem.at[slot, 1]),
            pltpu.make_async_copy(w_ref.at[t, :, lanes], w_in.at[slot], in_sem.at[slot, 2]),
        ]

    def stores(i):
        t, j, slot = i // parts, i % parts, i % behind
        lanes = pl.ds(pl.multiple_of(j * tile, tile), tile)
        return [
            pltpu.make_async_copy(g_out.at[slot], grad_to.at[t, :, lanes], out_sem.at[slot, 0]),
            pltpu.make_async_copy(m_out.at[slot], moment_to.at[t, :, lanes], out_sem.at[slot, 1]),
            pltpu.make_async_copy(n_out.at[slot], next_to.at[t, :, lanes], out_sem.at[slot, 2]),
        ]

    def each(copies, act):
        for copy in copies:
            act(copy)

    start, wait = lambda copy: copy.start(), lambda copy: copy.wait()

    def maps_load(i):
        block = pl.ds(pl.multiple_of(i * part, part), part)
        return pltpu.make_async_copy(maps_ref.at[block], maps_mid.at[block], maps_in_sem.at[i])

    def maps_store(i):
        block = pl.ds(pl.multiple_of(i * part, part), part)
        return pltpu.make_async_copy(maps_mid.at[block], maps_to.at[block], maps_out_sem.at[i])

    load_acts = pltpu.make_async_copy(acts_ref, acts_mid, acts_sem.at[0])
    store_acts = pltpu.make_async_copy(acts_mid, acts_to, acts_sem.at[1])
    towers = [pltpu.make_async_copy(ft_ref.at[t], ft.at[t], ft_sem.at[t]) for t in range(2)]
    towers[0].start()
    for i in range(ahead):
        each(loads(i), start)
    towers[1].start()

    def step(grad, value, moment, rate, at, grad_ref, next_ref, moment_ref):
        after = MOMENTUM * moment[at] + grad
        grad_ref[at] = grad
        moment_ref[at] = after
        next_ref[at] = value[at] - rate * after

    for i in range(2):
        at = (pl.ds(i, 1), slice(None))
        step(sums_ref[4 + i], bias_ref, bias_m_ref, DENSE_RATE, at, bias_g, bias_n, bias_mn)
        for j in range(2):
            at = (i, pl.ds(j, 1), slice(None))
            step(sums_ref[2 * i + j], out_ref, out_m_ref, STITCH_RATE, at, out_g, out_n, out_mn)
            step(turn_mix(mixed_ref[2 * i + j]), in_ref, in_m_ref, STITCH_RATE, at, in_g, in_n, in_mn)

    towers[0].wait()

    def body(i, carry):
        slot, to = i % ahead, i % behind

        @pl.when(i >= ahead)
        def _():
            maps_load(i - ahead).wait()
            maps_store(i - ahead).start()

        pl.when(i < chunks)(lambda: maps_load(i).start())
        pl.when(i == 0)(load_acts.start)

        @pl.when(i == ahead)
        def _():
            load_acts.wait()
            store_acts.start()

        pl.when(i == parts)(towers[1].wait)
        each(loads(i), wait)
        pl.when(i >= behind)(lambda: each(stores(i - behind), wait))
        grad = jnp.dot(
            ft[i // parts], s_in[slot].reshape(groups * rows, tile), preferred_element_type=F32
        )
        g_out[to] = grad
        moment = MOMENTUM * m_in[slot] + grad
        m_out[to] = moment
        n_out[to] = (w_in[slot].astype(F32) - DENSE_RATE * moment).astype(BF16)
        each(stores(i), start)
        pl.when(i + ahead < steps)(lambda: each(loads(i + ahead), start))
        return carry

    lax.fori_loop(0, steps, body, 0)
    for k in range(behind):
        each(stores(steps - behind + k), wait)
    for i in range(chunks):
        maps_store(i).wait()
    store_acts.wait()


def weight_update(ft_all, gathered, moment, weight, maps, acts, sums, mixed, smalls):
    groups, parts, _, rows, outs = gathered.shape
    width = weight.shape[1]
    chunks = 2 * parts - 3
    here = pl.BlockSpec(memory_space=pltpu.VMEM)
    far = pl.BlockSpec(memory_space=pl.ANY)
    ahead, behind = 3, 2
    vmem, dma = pltpu.VMEM, pltpu.SemaphoreType.DMA
    return pl.pallas_call(
        functools.partial(update_kernel, chunks),
        in_specs=[far] * 6 + [here] * (2 + len(smalls)),
        out_specs=[far] * 5 + [here] * 9,
        out_shape=[
            jax.ShapeDtypeStruct(moment.shape, F32),
            jax.ShapeDtypeStruct(moment.shape, BF16),
            jax.ShapeDtypeStruct(moment.shape, F32),
            jax.ShapeDtypeStruct(maps.shape, BF16),
            jax.ShapeDtypeStruct(acts.shape, BF16),
        ]
        + [jax.ShapeDtypeStruct(a.shape, F32) for a in smalls[::2] for _ in range(3)],
        scratch_shapes=[
            vmem((2, width, groups * rows), BF16),
            vmem((ahead, groups, rows, outs), BF16),
            vmem((ahead, width, outs), F32),
            vmem((ahead, width, outs), BF16),
            vmem((behind, width, outs), F32),
            vmem((behind, width, outs), BF16),
            vmem((behind, width, outs), F32),
            vmem(maps.shape, BF16),
            vmem(acts.shape, BF16),
            dma((2,)),
            dma((ahead, 3)),
            dma((behind, 3)),
            dma((chunks,)),
            dma((chunks,)),
            dma((2,)),
        ],
        compiler_params=params(),
        name="weight_update",
    )(ft_all, gathered, moment, weight, maps, acts, sums, mixed, *smalls)


def fast_shards(
    mesh,
    input_maps,
    dense_weight,
    dense_bias,
    stitch_in,
    stitch_out,
    weight_moment,
    bias_moment,
    stitch_in_moment,
    stitch_out_moment,
    cotangent,
    live_rows,
):
    maps = jnp.transpose(input_maps, (1, 3, 2, 0))
    gathered, ft_all, acts, maps_out, sums, mixed = step_all(
        mesh, live_rows, maps, dense_weight, cotangent, dense_bias, stitch_out, stitch_in
    )
    (
        weight_grad,
        weight_next,
        weight_moment_next,
        maps_grad,
        activations,
        bias_grad,
        bias_next,
        bias_moment_next,
        stitch_in_grad,
        stitch_in_next,
        stitch_in_moment_next,
        stitch_out_grad,
        stitch_out_next,
        stitch_out_moment_next,
    ) = weight_update(
        ft_all,
        gathered,
        weight_moment,
        dense_weight,
        maps_out.reshape((-1,) + maps_out.shape[2:]),
        acts,
        sums,
        mixed,
        [dense_bias, bias_moment, stitch_in, stitch_in_moment, stitch_out, stitch_out_moment],
    )
    maps_grad = jnp.transpose(maps_grad.reshape(maps.shape), (3, 0, 2, 1))
    return (
        activations,
        maps_grad,
        weight_grad,
        bias_grad,
        stitch_in_grad,
        stitch_out_grad,
        weight_next,
        bias_next,
        stitch_in_next,
        stitch_out_next,
        weight_moment_next,
        bias_moment_next,
        stitch_in_moment_next,
        stitch_out_moment_next,
    )


def choose(mesh, *args):
    rows, _, chans, _ = args[0].shape
    outs = args[2].shape[1]
    shape = mesh.shape["batch"] == 4 and mesh.shape["mp"] == 8
    if shape and rows % 512 == 0 and outs % 256 == 0 and chans == 32:
        return fast_shards(mesh, *args)
    return shards(*args)


def solution(mesh):
    in_specs = (
        P("batch", None, "mp", None),
        P(None, "mp", None),
        P(None, "mp"),
        P(None, None, "mp"),
        P(None, None, "mp"),
        P(None, "mp", None),
        P(None, "mp"),
        P(None, None, "mp"),
        P(None, None, "mp"),
        P("batch", None, "mp"),
        P(),
    )
    out_specs = (
        P("batch", None, "mp"),
        P("batch", None, "mp", None),
        P(None, "mp", None),
        P(None, "mp"),
        P(None, None, "mp"),
        P(None, None, "mp"),
        P(None, "mp", None),
        P(None, "mp"),
        P(None, None, "mp"),
        P(None, None, "mp"),
        P(None, "mp", None),
        P(None, "mp"),
        P(None, None, "mp"),
        P(None, None, "mp"),
    )
    body = functools.partial(choose, mesh)
    return jax.shard_map(body, mesh=mesh, in_specs=in_specs, out_specs=out_specs, check_vma=False)
```

```python
import functools

import jax
import jax.numpy as jnp
from jax import lax
from jax.experimental import pallas as pl
from jax.experimental.pallas import tpu as pltpu
from jax.sharding import PartitionSpec as P

MESH = pl.DeviceIdType.MESH
BF16 = jnp.bfloat16
F32 = jnp.float32
VMEM_LIMIT = 60 * 1024 * 1024

MOMENTUM = 0.9
DENSE_RATE = 0.01
STITCH_RATE = 0.1


def pool_table():
    pixels = jnp.arange(169, dtype=jnp.int32)
    cells = jnp.arange(36, dtype=jnp.int32)
    pixel_row = (pixels // 13)[:, None]
    pixel_col = (pixels % 13)[:, None]
    cell_row = (cells // 6)[None, :]
    cell_col = (cells % 6)[None, :]
    inside = (
        (pixel_row >= 2 * cell_row)
        & (pixel_row <= 2 * cell_row + 2)
        & (pixel_col >= 2 * cell_col)
        & (pixel_col <= 2 * cell_col + 2)
    )
    return inside.astype(jnp.float32)


def gelu_tanh(value):
    return jax.nn.gelu(value, approximate=True)


def head(summed, cotangent, keep, dense_bias, stitch_out):
    hidden = summed + dense_bias[None]
    active, gelu_pull = jax.vjp(gelu_tanh, hidden)
    mixed = stitch_out[None, :, 0] * active[:, 0:1] + stitch_out[None, :, 1] * active[:, 1:2]
    activations = (mixed * keep[:, None, None]).astype(jnp.bfloat16)
    pulled = cotangent.astype(jnp.float32) * keep[:, None, None]
    stitch_out_grad = jnp.einsum("nio,njo->ijo", pulled, active, precision=lax.Precision.HIGHEST)
    active_grad = stitch_out[0][None] * pulled[:, 0:1] + stitch_out[1][None] * pulled[:, 1:2]
    hidden_grad = gelu_pull(active_grad)[0]
    bias_grad = jnp.sum(hidden_grad, axis=0)
    return (activations, hidden_grad.astype(jnp.bfloat16), bias_grad, stitch_out_grad)


def rows_layer(features, cotangent, keep, dense_weight, dense_bias, stitch_out):
    terms = jnp.einsum("ntk,tko->nto", features, dense_weight, preferred_element_type=jnp.float32)
    summed = lax.psum_scatter(terms, "mp", scatter_dimension=2, tiled=True)
    activations, summed_grad, bias_grad, stitch_out_grad = head(
        summed, cotangent, keep, dense_bias, stitch_out
    )
    piece = lax.all_gather(summed_grad, "mp", axis=2, tiled=True)
    inputs_grad = jnp.einsum(
        "nto,tko->ntk", piece, dense_weight, preferred_element_type=jnp.float32
    )
    update = jnp.einsum("ntk,nto->tko", features, piece, preferred_element_type=jnp.float32)
    weight_grad = update
    inputs_grad, weight_grad = (inputs_grad, weight_grad)
    return (activations, inputs_grad.astype(jnp.bfloat16), weight_grad, bias_grad, stitch_out_grad)


def dense_layer(features, cotangent, keep, dense_weight, dense_bias, stitch_out):
    return rows_layer(features, cotangent, keep, dense_weight, dense_bias, stitch_out)


def shards(
    input_maps,
    dense_weight,
    dense_bias,
    stitch_in,
    stitch_out,
    weight_moment,
    bias_moment,
    stitch_in_moment,
    stitch_out_moment,
    cotangent,
    live_rows,
):
    rows = input_maps.shape[0]
    chans = input_maps.shape[2]
    width = chans * 36
    group = lax.axis_index("batch")
    positions = jnp.arange(rows, dtype=jnp.int32)
    keep = (positions < live_rows[group]).astype(jnp.float32)
    table = pool_table()
    pooled = (
        jnp.einsum(
            "ntck,kq->ntcq",
            input_maps,
            table.astype(jnp.bfloat16),
            preferred_element_type=jnp.float32,
        )
        / 9.0
    )
    stitched = (
        stitch_in[None, :, 0, :, None] * pooled[:, 0:1]
        + stitch_in[None, :, 1, :, None] * pooled[:, 1:2]
    )
    features = stitched.reshape(rows, 2, width).astype(jnp.bfloat16)
    activations, inputs_grad, weight_grad, bias_grad, stitch_out_grad = dense_layer(
        features, cotangent, keep, dense_weight, dense_bias, stitch_out
    )
    stitched_grad = inputs_grad.astype(jnp.float32).reshape(rows, 2, chans, 36)
    stitch_in_grad = jnp.einsum(
        "nicq,njcq->ijc", stitched_grad, pooled, precision=lax.Precision.HIGHEST
    )
    pooled_grad = (
        stitch_in[0][None, :, :, None] * stitched_grad[:, 0:1]
        + stitch_in[1][None, :, :, None] * stitched_grad[:, 1:2]
    )
    maps_grad = jnp.einsum(
        "ntcq,kq->ntck", pooled_grad / 9.0, table, precision=lax.Precision.HIGHEST
    ).astype(jnp.bfloat16)
    weight_grad, bias_grad, stitch_in_grad, stitch_out_grad = lax.psum(
        (weight_grad, bias_grad, stitch_in_grad, stitch_out_grad), "batch"
    )
    weight_moment_next = MOMENTUM * weight_moment + weight_grad
    weight_next = (dense_weight.astype(jnp.float32) - DENSE_RATE * weight_moment_next).astype(
        jnp.bfloat16
    )
    bias_moment_next = MOMENTUM * bias_moment + bias_grad
    bias_next = dense_bias - DENSE_RATE * bias_moment_next
    stitch_in_moment_next = MOMENTUM * stitch_in_moment + stitch_in_grad
    stitch_in_next = stitch_in - STITCH_RATE * stitch_in_moment_next
    stitch_out_moment_next = MOMENTUM * stitch_out_moment + stitch_out_grad
    stitch_out_next = stitch_out - STITCH_RATE * stitch_out_moment_next
    return (
        activations,
        maps_grad,
        weight_grad,
        bias_grad,
        stitch_in_grad,
        stitch_out_grad,
        weight_next,
        bias_next,
        stitch_in_next,
        stitch_out_next,
        weight_moment_next,
        bias_moment_next,
        stitch_in_moment_next,
        stitch_out_moment_next,
    )


def params():
    return pltpu.CompilerParams(vmem_limit_bytes=VMEM_LIMIT)


def full(shape):
    return pl.BlockSpec(shape, lambda *_: (0,) * len(shape))


def fill_order(order, chans, inverse):
    size = order.shape[0]
    rows = lax.broadcasted_iota(jnp.int32, (size, size), 0)
    cols = lax.broadcasted_iota(jnp.int32, (size, size), 1)
    natural, cells = (cols, rows) if inverse else (rows, cols)
    shift = chans.bit_length() - 1
    hit = natural == 36 * (cells & (chans - 1)) + (cells >> shift)
    order[...] = jnp.where(hit, 1.0, 0.0).astype(BF16)


def spread_mix(mix_ref, wide):
    chans = wide.shape[1]
    rows = lax.broadcasted_iota(jnp.int32, (chans, chans), 0)
    cols = lax.broadcasted_iota(jnp.int32, (chans, chans), 1)
    for k in range(4):
        line = jnp.broadcast_to(mix_ref[k // 2, pl.ds(k % 2, 1), :], (chans, chans))
        column = jnp.sum(jnp.where(rows == cols, line, 0.0), axis=1, keepdims=True)
        wide[k] = jnp.broadcast_to(column, wide.shape[1:])


def pooled_row(maps_ref, tower, i, lanes):
    sums = None
    for dy in range(3):
        line = [maps_ref[tower, 26 * i + 13 * dy + x, :, lanes].astype(F32) for x in range(13)]
        cells = [line[2 * j] + line[2 * j + 1] + line[2 * j + 2] for j in range(6)]
        sums = cells if sums is None else [a + b for a, b in zip(sums, cells)]
    return [s * (1.0 / 9.0) for s in sums]


def gelu_parts(v):
    root = 0.7978845608028654
    square = v * v
    tanh = jnp.tanh(root * v * (1.0 + 0.044715 * square))
    half = 0.5 * (1.0 + tanh)
    slope = half + 0.5 * v * (1.0 - tanh * tanh) * root * (1.0 + 3.0 * 0.044715 * square)
    return v * half, slope


def neighbours():
    b, m = lax.axis_index("batch"), lax.axis_index("mp")
    columns = (b, b + 1 - 2 * (b % 2), b + 2 - 4 * (b // 2), 3 - b)
    return b, m, m // 2, m % 2, columns


def greet(columns, m, z, c, nz):
    b, bx, by, _ = columns
    sibling = m + 1 - 2 * c
    barrier = pltpu.get_barrier_semaphore()

    def signal(bb, mm):
        pl.semaphore_signal(barrier, inc=1, device_id=(bb, mm), device_id_type=MESH)

    signal(bx, m)
    signal(by, m)
    signal(b, sibling)
    pl.when(z > 0)(lambda: signal(b, m - 2))
    pl.when(z < nz - 1)(lambda: signal(b, m + 2))
    pl.semaphore_wait(barrier, 3 + jnp.where(z > 0, 1, 0) + jnp.where(z < nz - 1, 1, 0))


def remote(src, dst, send, recv, device):
    return pltpu.make_async_remote_copy(
        src_ref=src, dst_ref=dst, send_sem=send, recv_sem=recv, device_id=device, device_id_type=MESH
    )


def unpool_row(chans, i, lanes, maps_ref, out_ref, cells, above, total, wide):
    spans = [pl.ds(pl.multiple_of((6 * i + j) * chans, chans), chans) for j in range(6)]
    pooled = [pooled_row(maps_ref, t, i, lanes) for t in range(2)]
    sums = [total[k] for k in range(4)]
    for j in range(6):
        for t in range(2):
            grad = cells[t, spans[j], lanes]
            for s in range(2):
                sums[2 * t + s] += grad * pooled[s][j]
    for k in range(4):
        total[k] = sums[k]
    for t in range(2):
        mixed = []
        for j in range(6):
            value = wide[t] * cells[0, spans[j], lanes] + wide[2 + t] * cells[1, spans[j], lanes]
            mixed.append(value * (1.0 / 9.0))
        for x in range(13):
            if x % 2 == 1 or x == 0:
                value = mixed[x // 2]
            elif x == 12:
                value = mixed[5]
            else:
                value = mixed[x // 2 - 1] + mixed[x // 2]
            out_ref[t, 26 * i + x, :, lanes] = (value + above[t, x, :, lanes]).astype(BF16)
            out_ref[t, 26 * i + 13 + x, :, lanes] = value.astype(BF16)
            above[t, x, :, lanes] = value


def shares(live_ref, groups, base):
    counts = [live_ref[k] for k in range(groups)]
    excess, free = [], []
    taken = given = 0
    for count in counts:
        excess.append(taken)
        free.append(given)
        taken = taken + jnp.maximum(count - base, 0)
        given = given + jnp.maximum(base - count, 0)
    return counts, excess, free


def picks(count, free, other, excess, base, spare, slots_in_lanes):
    shape = (spare, base) if slots_in_lanes else (base, spare)
    slot = lax.broadcasted_iota(jnp.int32, shape, 1 if slots_in_lanes else 0)
    row = lax.broadcasted_iota(jnp.int32, shape, 0 if slots_in_lanes else 1)
    hit = (slot - count + free == row + excess) & (slot >= count) & (row < other - base)
    return jnp.where(hit, 1.0, 0.0).astype(BF16)


def gather_phase(nz, cut, base, features_on, live_ref, pool_ref, pool, s_ref, acts_in, sums_ref, w_ref, maps_in, wide,
                 g_ref, acts_to, out_ref, total_ref, mixed_ref, sums_in, mix_in, sems,
                 keep_sem, out_sem, w_sem, col_sem, acts_sem,
                 acts_out, maps_out, wbuf, col, grads, cells, order, above, mix_total):
    (line_send, line_recv, cross_send, cross_recv, half_send, half_recv, core_send, core_recv,
     small_send, small_recv, sums_mid, mix_mid) = sems
    b, m, z, c, columns = neighbours()
    rows = s_ref.shape[1]
    spans = (pl.ds(0, cut), pl.ds(cut, base - cut), pl.ds(base, rows - base))
    spare = rows - base
    sibling = m + 1 - 2 * c

    def small(kind, axis, src, dst):
        return remote(src, dst, small_send.at[kind, axis], small_recv.at[kind, axis], (columns[1 + axis], m))

    def place(p, r, zz):
        return g_ref.at[columns[r], 2 * zz + c, :, spans[p], :]

    def half(p, r, zz, t):
        return g_ref.at[columns[r], 2 * zz + c, t, spans[p], :]

    def line(k, zz, up, own=False):
        p, r = {0: (0, 0), 5: (2, 0)}.get(k, (1, k - 1))
        src = s_ref.at[:, spans[p], :] if own else place(p, r, zz)
        side = 1 if up else 0
        to = m + 2 if up else m - 2
        return remote(src, place(p, r, zz), line_send.at[side, k, zz], line_recv.at[k, zz], (b, to))

    def cross(p, axis, zz, own=False):
        src = s_ref.at[:, spans[p], :] if own else place(p, 0, zz)
        slot = zz if p == 0 else nz
        return remote(
            src, place(p, 0, zz), cross_send.at[axis, slot], cross_recv.at[axis, slot], (columns[1 + axis], m)
        )

    def cross_wait(p, axis, zz):
        slot = zz if p == 0 else nz
        here = place(p, 1 + axis, zz)
        remote(here, here, cross_send.at[axis, slot], cross_recv.at[axis, slot], (columns[1 + axis], m)).wait_recv()

    def diagonal(p, axis, zz):
        slot = zz if p == 0 else nz
        block = half(p, 2 - axis, zz, 1 - axis)
        return remote(block, block, half_send.at[axis, slot], half_recv.at[axis, slot], (columns[1 + axis], m))

    def diagonal_wait(p, axis, zz):
        slot = zz if p == 0 else nz
        block = half(p, 3, zz, 1 - axis)
        remote(block, block, half_send.at[axis, slot], half_recv.at[axis, slot], (columns[1 + axis], m)).wait_recv()

    def core(p, r, zz, own=False):
        src = s_ref.at[:, spans[p], :] if own else place(p, r, zz)
        return remote(src, place(p, r, zz), core_send.at[p, r, zz], core_recv.at[p, r, zz], (b, sibling))

    def core_wait(p, r, zz):
        block = g_ref.at[columns[r], 2 * zz + 1 - c, :, spans[p], :]
        remote(block, block, core_send.at[p, r, zz], core_recv.at[p, r, zz], (b, sibling)).wait_recv()

    def sides(d, body):
        if d == 0:
            body(z, None)
            return
        pl.when(z + d < nz)(lambda: body(z + d, False))
        pl.when(z - d >= 0)(lambda: body(z - d, True))

    def onward(k, zz, up):
        if up:
            pl.when(z < nz - 1)(lambda: line(k, zz, True).start())
        else:
            pl.when(z > 0)(lambda: line(k, zz, False).start())

    mine = pltpu.make_async_copy(s_ref, g_ref.at[b, m], keep_sem)

    def launch(k):
        pl.when(z < nz - 1)(lambda: line(k, z, True, True).start())
        pl.when(z > 0)(lambda: line(k, z, False, True).start())

    first_sums = small(0, 0, sums_ref, sums_in.at[0])
    first_sums.start()
    for axis in range(2):
        pool.come(axis)
        pool.turn(1 - axis).start()
    launch(5)
    core(2, 0, z, True).start()
    counts, excess, free = shares(live_ref, 4, base)
    live = live_ref[b]
    offset = 0
    for k in range(1, 4):
        offset = offset + jnp.where(b >= k, jnp.maximum(base - counts[k - 1], 0), 0)
    chosen = jnp.concatenate(
        [picks(live, offset, counts[k], excess[k], base, spare, False) for k in range(4)], axis=1
    )
    for axis in range(2):
        pool.end(axis)
    for t in range(2):
        moved = jnp.dot(chosen, pool_ref[t], preferred_element_type=F32)
        s_ref[t, :base, :] = (s_ref[t, :base, :].astype(F32) + moved).astype(BF16)
    cross(1, 0, z, True).start()
    cross(1, 1, z, True).start()
    launch(0)
    cross(0, 0, z, True).start()
    cross(0, 1, z, True).start()
    launch(1)
    core(0, 0, z, True).start()
    core(1, 0, z, True).start()
    features_on(0)
    mine.start()

    def pass_cross(p, zz):
        for axis in range(2):
            cross_wait(p, axis, zz)
            diagonal(p, 1 - axis, zz).start()
            core(p, 1 + axis, zz).start()

    def end_diagonal(p, zz):
        for axis in range(2):
            diagonal_wait(p, axis, zz)
        core(p, 3, zz).start()

    def arrive(zz, up):
        line(0, zz, up).wait_recv()
        onward(0, zz, up)
        cross(0, 0, zz).start()
        cross(0, 1, zz).start()
        core(0, 0, zz).start()
        for k, p in ((1, 1), (5, 2)):
            line(k, zz, up).wait_recv()
            onward(k, zz, up)
            core(p, 0, zz).start()

    def late(zz, up):
        for k in range(2, 5):
            line(k, zz, up).wait_recv()
            onward(k, zz, up)
            core(1, k - 1, zz).start()

    def spread():
        for k in range(2, 5):
            pl.when(z < nz - 1)(lambda k=k: line(k, z, True).start())
            pl.when(z > 0)(lambda k=k: line(k, z, False).start())

    def join_towers(k, carry):
        here = pl.ds(pl.multiple_of(k * 16, 16), 16)
        both = jnp.stack([acts_in[t, here, :].astype(F32) for t in range(2)], axis=1)
        acts_out[here, :, :] = both.astype(BF16)
        return carry

    pass_cross(1, z)
    lax.fori_loop(0, rows // 16, join_towers, 0)
    store_acts = pltpu.make_async_copy(acts_out, acts_to, acts_sem)
    store_acts.start()
    sides(1, arrive)
    pass_cross(0, z)
    end_diagonal(1, z)
    sides(2, arrive)
    width, chans = w_ref.shape[1], maps_in.shape[2]
    outs = s_ref.shape[2]
    piece = wbuf.shape[1]
    pieces = width // piece

    def weights(k):
        t, at = k // pieces, k % pieces * piece
        return pltpu.make_async_copy(w_ref.at[t, pl.ds(at, piece), :], wbuf.at[k % 2], w_sem.at[k % 2])

    def column(t, j):
        return pltpu.make_async_copy(
            g_ref.at[b, j, t], col.at[:, pl.ds(j * outs, outs)], col_sem.at[j]
        )

    def features_grad(t):
        for k in range(t * pieces, (t + 1) * pieces):
            if k + 1 < 2 * pieces:
                weights(k + 1).start()
            weights(k).wait()
            if k == t * pieces:
                for j in range(2 * nz):
                    column(t, j).wait()
            value = lax.dot_general(
                wbuf[k % 2], col[...], (((1,), (1,)), ((), ())), preferred_element_type=F32
            )
            lane = lax.broadcasted_iota(jnp.int32, value.shape, 1)
            grads[pl.ds(k % pieces * piece, piece), :] = jnp.where(lane < live, value, 0.0).astype(BF16)
        cells[t] = jnp.dot(order[...], grads[...], preferred_element_type=F32)

    blocks = rows // 128

    def maps_back(step, carry):
        i = step // blocks
        lanes = pl.ds(pl.multiple_of(step % blocks * 128, 128), 128)
        unpool_row(chans, i, lanes, maps_in, maps_out, cells, above, mix_total, wide)
        return carry

    weights(0).start()
    fill_order(order, chans, True)
    above[...] = jnp.zeros_like(above)
    mix_total[...] = jnp.zeros_like(mix_total)
    first_sums.wait()
    sums_mid[...] = sums_ref[...] + sums_in[0]
    second_sums = small(0, 1, sums_mid, sums_in.at[1])
    second_sums.start()
    outer = (z == 0) | (z == nz - 1)
    inner = (z > 0) & (z < nz - 1)

    @pl.when(outer)
    def _():
        sides(1, lambda zz, up: pass_cross(0, zz))
        sides(3, arrive)
        spread()

    mine.wait()
    for zz in range(nz):
        for p in range(3):
            core_wait(p, 0, zz)
    for j in range(2 * nz):
        column(0, j).start()
    features_grad(0)
    for j in range(2 * nz):
        column(1, j).start()
    pl.when(inner)(spread)
    pl.when(outer)(lambda: sides(1, late))
    features_grad(1)

    @pl.when(inner)
    def _():
        sides(1, lambda zz, up: pass_cross(0, zz))
        sides(1, late)

    end_diagonal(0, z)
    pl.when(inner)(lambda: sides(2, late))
    pl.when(outer)(lambda: sides(2, lambda zz, up: pass_cross(0, zz)))
    lax.fori_loop(0, 3 * blocks, maps_back, 0)
    pl.when(outer)(lambda: sides(2, late))
    lax.fori_loop(3 * blocks, 6 * blocks, maps_back, 0)
    for t in range(2):
        for x in range(13):
            maps_out[t, 156 + x] = above[t, x].astype(BF16)
    store_maps = pltpu.make_async_copy(maps_out, out_ref, out_sem)
    store_maps.start()
    for k in range(4):
        mix_in[0, k] = jnp.broadcast_to(jnp.sum(mix_total[k], axis=1, keepdims=True), (chans, 128))
    first_mix = small(1, 0, mix_in.at[0], mix_in.at[1])
    first_mix.start()
    pl.when(inner)(lambda: sides(2, lambda zz, up: pass_cross(0, zz)))
    sides(1, lambda zz, up: end_diagonal(0, zz))
    sides(3, lambda zz, up: pass_cross(0, zz))
    first_mix.wait()
    mix_mid[...] = mix_in[0] + mix_in[1]
    second_mix = small(1, 1, mix_mid, mix_in.at[2])
    second_mix.start()
    sides(2, lambda zz, up: end_diagonal(0, zz))
    sides(3, late)
    sides(3, lambda zz, up: end_diagonal(0, zz))
    second_sums.wait()
    total_ref[...] = sums_mid[...] + sums_in[1]
    second_mix.wait()
    mixed_ref[...] = mix_mid[...] + mix_in[2]
    store_maps.wait()
    store_acts.wait()

    for zz in range(nz):
        for r in range(4):
            for p in range(2):
                if r > 0:
                    core_wait(p, r, zz)
                core(p, r, zz).wait_send()
        core(2, 0, zz).wait_send()
        for axis in range(2):
            cross(0, axis, zz).wait_send()
            diagonal(0, axis, zz).wait_send()
        for k in range(6):
            pl.when((z < nz - 1) & (z >= zz))(lambda k=k, zz=zz: line(k, zz, True).wait_send())
            pl.when((z > 0) & (z <= zz))(lambda k=k, zz=zz: line(k, zz, False).wait_send())
    for axis in range(2):
        cross(1, axis, z).wait_send()
        diagonal(1, axis, z).wait_send()


def head_rows(hidden, cot, keep, mix, act_ref, grad_ref, here, lanes):
    active, slope, pulled = [], [], []
    for t in range(2):
        value, rate = gelu_parts(hidden[t])
        active.append(value)
        slope.append(rate)
        pulled.append(cot[t] * keep)
    for i in range(2):
        mixed = mix[2 * i] * active[0] + mix[2 * i + 1] * active[1]
        act_ref[i, here, lanes] = (mixed * keep).astype(BF16)
    terms = [pulled[i] * active[j] for i in range(2) for j in range(2)]
    for j in range(2):
        grad = (mix[j] * pulled[0] + mix[2 + j] * pulled[1]) * slope[j]
        grad_ref[j, here, lanes] = grad.astype(BF16)
        terms.append(grad)
    return terms


def step_kernel(nz, cut, base, live_ref, maps_ref, w_ref, cot_raw, bias_ref, mix_ref, mix_in_ref,
                g_ref, fta_ref, acts_to, out_ref, total_ref, mixed_ref,
                maps_in, rb, inb, ft_ref, s_ref, acts_in, sums_ref, wide, sums_in, mix_in,
                maps_sem, swap_send, swap_recv, hop_send, hop_recv,
                feat_send, feat_recv, turn_send, turn_recv, feat_keep,
                pool_ref, pool_send, pool_recv, pool_turn_send, pool_turn_recv, *rest):
    b, m, z, c, columns = neighbours()
    sibling = m + 1 - 2 * c
    chans, rows = maps_in.shape[2:]
    width, outs = w_ref.shape[1], s_ref.shape[2]
    span = rows // 2

    def load_maps(h):
        lanes = pl.ds(h * span, span)
        return pltpu.make_async_copy(maps_ref.at[:, :, :, lanes], maps_in.at[:, :, :, lanes], maps_sem.at[h])

    for h in (1, 0):
        load_maps(h).start()

    def features(r, t, h):
        start = pl.multiple_of(columns[r] * rows + h * span, span)
        return fta_ref.at[t, :, pl.ds(start, span)]

    def mine(t, h):
        return pltpu.make_async_copy(ft_ref.at[t, :, pl.ds(h * span, span)], features(0, t, h), feat_keep.at[t, h])

    def feature(axis, t, h):
        return remote(ft_ref.at[t, :, pl.ds(h * span, span)], features(0, t, h), feat_send.at[axis, t, h],
                      feat_recv.at[axis, t, h], (columns[1 + axis], m))

    def feature_wait(axis, t, h):
        here = features(1 + axis, t, h)
        remote(here, here, feat_send.at[axis, t, h], feat_recv.at[axis, t, h], (columns[1 + axis], m)).wait_recv()

    def turn(axis, h):
        here = features(2 - axis, 1 - axis, h)
        return remote(here, here, turn_send.at[axis, h], turn_recv.at[axis, h], (columns[1 + axis], m))

    def turn_wait(axis, h):
        here = features(3, 1 - axis, h)
        remote(here, here, turn_send.at[axis, h], turn_recv.at[axis, h], (columns[1 + axis], m)).wait_recv()

    def features_on(h):
        for axis in range(2):
            feature_wait(1 - axis, 1 - axis, h)
            turn(axis, h).start()

    spare = rows - base

    class pool:
        def slot(r, t=None):
            start = pl.ds(pl.multiple_of(columns[r] * spare, spare), spare)
            return pool_ref.at[:, start, :] if t is None else pool_ref.at[t, start, :]

        def go(axis):
            return remote(s_ref.at[:, pl.ds(base, spare), :], pool.slot(0), pool_send.at[axis], pool_recv.at[axis],
                          (columns[1 + axis], m))

        def come(axis):
            here = pool.slot(1 + axis)
            remote(here, here, pool_send.at[axis], pool_recv.at[axis], (columns[1 + axis], m)).wait_recv()

        def turn(axis):
            here = pool.slot(2 - axis, 1 - axis)
            return remote(here, here, pool_turn_send.at[axis], pool_turn_recv.at[axis], (columns[1 + axis], m))

        def end(axis):
            here = pool.slot(3, 1 - axis)
            remote(here, here, pool_turn_send.at[axis], pool_turn_recv.at[axis], (columns[1 + axis], m)).wait_recv()

    def forward(cells, order, f_ref, cot_in, cot_ref, wbuf, pb, sb, cot_sem, w_sem):
        live = live_ref[b]
        near = jnp.where(z < nz // 2, 1, 0)

        def weights(i, t, own):
            zd = near * (nz - 1 - i) + (1 - near) * i
            j = 2 * zd + (c if own else 1 - c)
            lanes = pl.ds(pl.multiple_of(j * outs, outs), outs)
            k = 2 * t + own
            return pltpu.make_async_copy(w_ref.at[t, :, lanes], wbuf.at[k], w_sem.at[k])

        for t in range(2):
            for own in range(2):
                weights(0, t, own).start()
        load_cot = pltpu.make_async_copy(cot_raw, cot_in, cot_sem)
        load_cot.start()
        fill_order(order, chans, False)
        spread_mix(mix_in_ref, wide)
        greet(columns, m, z, c, nz)

        def swap(d, t, h):
            here = pl.ds(h * span, span)
            return remote(sb.at[d, t, here], rb.at[d, t, here], swap_send.at[d, t, h], swap_recv.at[d, t, h], (b, sibling))

        def hop(up, d, t, h):
            here = pl.ds(h * span, span)
            return remote(rb.at[d, t, here], inb.at[d + up, t, here], hop_send.at[d, t, h], hop_recv.at[up, d, t, h],
                          (b, m + 4 * up - 2))

        step = 64

        def relay(up, dm, t, h, first):
            zm = up * z + (1 - up) * (nz - 1 - z)
            d = up * dm + (1 - up) * (nz - 1 - dm)

            def go():
                swap(d, t, h).wait_recv()
                if not first:
                    hop(up, d, t, h).wait_recv()

                def add(k, carry):
                    here = pl.ds(pl.multiple_of(h * span + k * step, step), step)
                    value = pb[d, t, here, :] + rb[d, t, here, :].astype(F32)
                    if not first:
                        value += inb[d + up, t, here, :].astype(F32)
                    rb[d, t, here, :] = value.astype(BF16)
                    return carry

                lax.fori_loop(0, span // step, add, 0)
                hop(up, d, t, h).start()

            pl.when((zm == 0 if first else zm > 0) & (zm < dm))(go)

        narrow = span // 128

        def pool_maps(h):
            def pool_row(step, carry):
                i = step // narrow
                at = pl.multiple_of(step % narrow * 128, 128)
                lanes = pl.ds(pl.multiple_of(h * span + at, 128), 128)
                first = pooled_row(maps_in, 0, i, lanes)
                second = pooled_row(maps_in, 1, i, lanes)
                for t in range(2):
                    for j in range(6):
                        value = wide[2 * t] * first[j] + wide[2 * t + 1] * second[j]
                        start = pl.multiple_of((6 * i + j) * chans, chans)
                        cells[t, pl.ds(start, chans), pl.ds(at, 128)] = value.astype(BF16)
                return carry

            load_maps(h).wait()
            lax.fori_loop(0, 6 * narrow, pool_row, 0)
            for t in range(2):
                moved = jnp.dot(order[...], cells[t], preferred_element_type=F32).astype(BF16)
                ft_ref[t, :, pl.ds(h * span, span)] = moved
                f_ref[t, pl.ds(h * span, span), :] = moved.T
            for k in range(2):
                feature(0, k, h).start()
                feature(1, 1 - k, h).start()

        def produce(i, h):
            zd = near * (nz - 1 - i) + (1 - near) * i
            here = pl.ds(h * span, span)
            for t in range(2):
                for own in range(2):
                    if h == 1:
                        weights(i, t, own).wait()
                    part = jnp.dot(f_ref[t, here, :], wbuf[2 * t + own], preferred_element_type=F32)
                    if own:
                        pb[zd, t, here, :] = part
                    else:
                        sb[zd, t, here, :] = part.astype(BF16)
                        swap(zd, t, h).start()
                    if h == 0:
                        pl.when(i < nz - 1)(lambda t=t, own=own: weights(i + 1, t, own).start())
                relay(near, nz - 1 - i, t, h, True)

        for h in (1, 0):
            pool_maps(h)
            produce(0, h)

        def both(i, carry):
            for h in (1, 0):
                produce(i, h)
            return carry

        lax.fori_loop(1, nz, both, 0)

        features_on(1)
        for t in range(2):
            for h in range(2):
                mine(t, h).start()
        load_cot.wait()

        def part_towers(k, carry):
            here = pl.ds(pl.multiple_of(k * 16, 16), 16)
            both = cot_in[here, :, :].astype(F32)
            for t in range(2):
                cot_ref[t, here, :] = both[:, t, :].astype(BF16)
            return carry

        lax.fori_loop(0, rows // 16, part_towers, 0)
        for dm in range(nz - 1, 0, -1):
            for h in (1, 0):
                for t in range(2):
                    relay(near, dm, t, h, False)
                    relay(1 - near, dm, t, h, False)

        tile, high = 256, 16
        for h in (1, 0):
            for t in range(2):
                swap(z, t, h).wait_recv()
                pl.when(z > 0)(lambda t=t, h=h: hop(1, z, t, h).wait_recv())
                pl.when(z < nz - 1)(lambda t=t, h=h: hop(0, z, t, h).wait_recv())

                def gather(k, carry, t=t, h=h):
                    here = pl.ds(pl.multiple_of(h * span + k * step, step), step)
                    pb[z, t, here, :] += rb[z, t, here, :].astype(F32)
                    for up in range(2):
                        inside = z > 0 if up else z < nz - 1

                        @pl.when(inside)
                        def _(up=up):
                            pb[z, t, here, :] += inb[z + up, t, here, :].astype(F32)

                    return carry

                lax.fori_loop(0, span // step, gather, 0)
            for lane in range(outs // tile):
                lanes = pl.ds(lane * tile, tile)
                bias = [bias_ref[pl.ds(t, 1), lanes] for t in range(2)]
                mix = [mix_ref[k // 2, pl.ds(k % 2, 1), lanes] for k in range(4)]

                def block(k, totals, lanes=lanes, bias=bias, mix=mix):
                    here = pl.ds(pl.multiple_of(k * high, high), high)
                    hidden = [pb[z, t, here, lanes] + bias[t] for t in range(2)]
                    cot = [cot_ref[t, here, lanes].astype(F32) for t in range(2)]
                    place = k * high + lax.broadcasted_iota(jnp.int32, (high, tile), 0)
                    keep = jnp.where(place < live, 1.0, 0.0)
                    terms = head_rows(hidden, cot, keep, mix, acts_in, s_ref, here, lanes)
                    return tuple(a + v[:8] + v[8:] for a, v in zip(totals, terms))

                zero = jnp.zeros((8, tile), F32)
                count = span // high
                totals = lax.fori_loop(h * count, (h + 1) * count, block, (zero,) * 6)
                for k in range(6):
                    value = jnp.sum(totals[k], axis=0, keepdims=True)
                    sums_ref[k, :, lanes] = value if h == 1 else sums_ref[k, :, lanes] + value
            if h == 1:
                here = pl.ds(pl.multiple_of(b * spare, spare), spare)
                pool_ref[:, here, :] = s_ref[:, base:, :]
                for axis in range(2):
                    pool.go(axis).start()
        for d in range(nz):
            for t in range(2):
                for h in range(2):
                    swap(d, t, h).wait_send()
                    pl.when(z < d)(lambda d=d, t=t, h=h: hop(1, d, t, h).wait_send())
                    pl.when(z > d)(lambda d=d, t=t, h=h: hop(0, d, t, h).wait_send())

    vmem, dma = pltpu.VMEM, pltpu.SemaphoreType.DMA
    pl.run_scoped(
        forward,
        vmem((2, width, span), BF16),
        vmem((width, width), BF16),
        vmem((2, rows, width), BF16),
        vmem(cot_raw.shape, BF16),
        vmem((2, rows, outs), BF16),
        vmem((4, width, outs), BF16),
        vmem((nz, 2, rows, outs), F32),
        vmem((nz, 2, rows, outs), BF16),
        dma,
        dma((4,)),
    )
    pl.run_scoped(
        functools.partial(gather_phase, nz, cut, base, features_on, live_ref, pool_ref, pool, s_ref, acts_in, sums_ref, w_ref, maps_in, wide,
                          g_ref, acts_to, out_ref, total_ref, mixed_ref, sums_in, mix_in, rest),
        dma,
        dma,
        dma((2,)),
        dma((2 * nz,)),
        dma,
        vmem((rows, 2, outs), BF16),
        vmem(maps_in.shape, BF16),
        vmem((2, width // 3, 2 * nz * outs), BF16),
        vmem((rows, 2 * nz * outs), BF16),
        vmem((width, rows), BF16),
        vmem((2, width, rows), F32),
        vmem((width, width), BF16),
        vmem((2, 13, chans, rows), F32),
        vmem((4, chans, 128), F32),
    )
    for h in range(2):
        for axis in range(2):
            feature_wait(axis, 1 - axis, h)
            turn_wait(axis, h)
            turn(axis, h).wait_send()
            for t in range(2):
                feature(axis, t, h).wait_send()
        for t in range(2):
            mine(t, h).wait()
    for axis in range(2):
        pool.go(axis).wait_send()
        pool.turn(axis).wait_send()


def step_all(mesh, live, maps, weight, cot, bias, mix, mix_in):
    groups, parts = mesh.shape["batch"], mesh.shape["mp"]
    nz = parts // 2
    chans, rows = maps.shape[2:]
    width = weight.shape[1]
    outs = weight.shape[2] // parts
    base = rows * 3 // 4
    cut = rows * 19 // 32
    vmem, dma = pltpu.VMEM, pltpu.SemaphoreType.DMA
    here = pl.BlockSpec(memory_space=pltpu.VMEM)
    far = pl.BlockSpec(memory_space=pl.ANY)
    sums = (6, 1, outs)
    return pl.pallas_call(
        functools.partial(step_kernel, nz, cut, base),
        in_specs=[pl.BlockSpec(memory_space=pltpu.SMEM), far, far, far, here, here, here],
        out_specs=[far, far, far, far, here, here],
        out_shape=[
            jax.ShapeDtypeStruct((groups, parts, 2, rows, outs), BF16),
            jax.ShapeDtypeStruct((2, width, groups * rows), BF16),
            jax.ShapeDtypeStruct((rows, 2, outs), BF16),
            jax.ShapeDtypeStruct(maps.shape, BF16),
            jax.ShapeDtypeStruct(sums, F32),
            jax.ShapeDtypeStruct((4, chans, 128), F32),
        ],
        scratch_shapes=[
            vmem(maps.shape, BF16),
            vmem((nz, 2, rows, outs), BF16),
            vmem((nz + 1, 2, rows, outs), BF16),
            vmem((2, width, rows), BF16),
            vmem((2, rows, outs), BF16),
            vmem((2, rows, outs), BF16),
            vmem(sums, F32),
            vmem((4, chans, 128), F32),
            vmem((2,) + sums, F32),
            vmem((3, 4, chans, 128), F32),
            dma((2,)),
            dma((nz, 2, 2)),
            dma((nz, 2, 2)),
            dma((nz, 2, 2)),
            dma((2, nz, 2, 2)),
            dma((2, 2, 2)),
            dma((2, 2, 2)),
            dma((2, 2)),
            dma((2, 2)),
            dma((2, 2)),
            vmem((2, groups * (rows - base), outs), BF16),
            dma((2,)),
            dma((2,)),
            dma((2,)),
            dma((2,)),
            dma((2, 6, nz)),
            dma((6, nz)),
            dma((2, nz + 1)),
            dma((2, nz + 1)),
            dma((2, nz + 1)),
            dma((2, nz + 1)),
            dma((3, 4, nz)),
            dma((3, 4, nz)),
            dma((2, 2)),
            dma((2, 2)),
            vmem(sums, F32),
            vmem((4, chans, 128), F32),
        ],
        compiler_params=pltpu.CompilerParams(
            collective_id=0, has_side_effects=True, vmem_limit_bytes=VMEM_LIMIT
        ),
        name="step_all",
    )(live, maps, weight, cot, bias, mix, mix_in)


def turn_mix(wide):
    chans = wide.shape[0]
    rows = lax.broadcasted_iota(jnp.int32, (chans, chans), 0)
    cols = lax.broadcasted_iota(jnp.int32, (chans, chans), 1)
    return jnp.sum(jnp.where(rows == cols, wide[:, :chans], 0.0), axis=0, keepdims=True)


def update_kernel(chunks, base, live_ref, ft_ref, s_ref, m_ref, w_ref, maps_ref, acts_ref, sums_ref, mixed_ref,
                  bias_ref, bias_m_ref, in_ref, in_m_ref, out_ref, out_m_ref,
                  grad_to, next_to, moment_to, maps_to, acts_to, bias_g, bias_n, bias_mn,
                  in_g, in_n, in_mn, out_g, out_n, out_mn,
                  raw, chosen, ft, s_in, m_in, w_in, g_out, n_out, m_out, maps_mid, acts_mid,
                  ft_sem, in_sem, out_sem, maps_in_sem, maps_out_sem, acts_sem):
    groups, parts, _, rows, tile = s_ref.shape
    spare = rows - base
    steps, ahead, behind = 2 * parts, s_in.shape[0], g_out.shape[0]
    part = maps_mid.shape[0] // chunks

    def loads(i):
        t, j, slot = i // parts, i % parts, i % ahead
        lanes = pl.ds(pl.multiple_of(j * tile, tile), tile)
        return [
            pltpu.make_async_copy(s_ref.at[:, j, t, pl.ds(0, base), :], s_in.at[slot], in_sem.at[slot, 0]),
            pltpu.make_async_copy(m_ref.at[t, :, lanes], m_in.at[slot], in_sem.at[slot, 1]),
            pltpu.make_async_copy(w_ref.at[t, :, lanes], w_in.at[slot], in_sem.at[slot, 2]),
        ]

    def stores(i):
        t, j, slot = i // parts, i % parts, i % behind
        lanes = pl.ds(pl.multiple_of(j * tile, tile), tile)
        return [
            pltpu.make_async_copy(g_out.at[slot], grad_to.at[t, :, lanes], out_sem.at[slot, 0]),
            pltpu.make_async_copy(m_out.at[slot], moment_to.at[t, :, lanes], out_sem.at[slot, 1]),
            pltpu.make_async_copy(n_out.at[slot], next_to.at[t, :, lanes], out_sem.at[slot, 2]),
        ]

    def each(copies, act):
        for copy in copies:
            act(copy)

    start, wait = lambda copy: copy.start(), lambda copy: copy.wait()

    def maps_load(i):
        block = pl.ds(pl.multiple_of(i * part, part), part)
        return pltpu.make_async_copy(maps_ref.at[block], maps_mid.at[block], maps_in_sem.at[i])

    def maps_store(i):
        block = pl.ds(pl.multiple_of(i * part, part), part)
        return pltpu.make_async_copy(maps_mid.at[block], maps_to.at[block], maps_out_sem.at[i])

    load_acts = pltpu.make_async_copy(acts_ref, acts_mid, acts_sem.at[0])
    store_acts = pltpu.make_async_copy(acts_mid, acts_to, acts_sem.at[1])
    towers = [pltpu.make_async_copy(ft_ref.at[t], raw, ft_sem.at[t]) for t in range(2)]
    towers[0].start()
    each(loads(0), start)
    counts, excess, free = shares(live_ref, groups, base)
    for k in range(groups):
        for n in range(groups):
            chosen[pl.ds(n * spare, spare), pl.ds(k * base, base)] = picks(
                counts[k], free[k], counts[n], excess[n], base, spare, True
            )

    def pack(t):
        towers[t].wait()
        last = jnp.concatenate([raw[:, k * rows + base : (k + 1) * rows] for k in range(groups)], axis=1)
        for k in range(groups):
            lanes = pl.ds(k * base, base)
            moved = jnp.dot(last, chosen[:, lanes], preferred_element_type=F32)
            lane = lax.broadcasted_iota(jnp.int32, moved.shape, 1)
            kept = raw[:, k * rows : k * rows + base].astype(F32)
            ft[:, lanes] = jnp.where(lane < counts[k], kept, moved).astype(BF16)

    def step(grad, value, moment, rate, at, grad_ref, next_ref, moment_ref):
        after = MOMENTUM * moment[at] + grad
        grad_ref[at] = grad
        moment_ref[at] = after
        next_ref[at] = value[at] - rate * after

    for i in range(2):
        at = (pl.ds(i, 1), slice(None))
        step(sums_ref[4 + i], bias_ref, bias_m_ref, DENSE_RATE, at, bias_g, bias_n, bias_mn)
        for j in range(2):
            at = (i, pl.ds(j, 1), slice(None))
            step(sums_ref[2 * i + j], out_ref, out_m_ref, STITCH_RATE, at, out_g, out_n, out_mn)
            step(turn_mix(mixed_ref[2 * i + j]), in_ref, in_m_ref, STITCH_RATE, at, in_g, in_n, in_mn)

    pack(0)
    towers[1].start()
    for i in range(1, ahead):
        each(loads(i), start)

    def body(i, carry):
        slot, to = i % ahead, i % behind

        @pl.when(i >= ahead)
        def _():
            maps_load(i - ahead).wait()
            maps_store(i - ahead).start()

        pl.when(i < chunks)(lambda: maps_load(i).start())
        pl.when(i == 0)(load_acts.start)

        @pl.when(i == ahead)
        def _():
            load_acts.wait()
            store_acts.start()

        pl.when(i == parts)(lambda: pack(1))
        each(loads(i), wait)
        pl.when(i >= behind)(lambda: each(stores(i - behind), wait))
        grad = jnp.dot(
            ft[...], s_in[slot].reshape(groups * base, tile), preferred_element_type=F32
        )
        g_out[to] = grad
        moment = MOMENTUM * m_in[slot] + grad
        m_out[to] = moment
        n_out[to] = (w_in[slot].astype(F32) - DENSE_RATE * moment).astype(BF16)
        each(stores(i), start)
        pl.when(i + ahead < steps)(lambda: each(loads(i + ahead), start))
        return carry

    lax.fori_loop(0, steps, body, 0)
    for k in range(behind):
        each(stores(steps - behind + k), wait)
    for i in range(chunks):
        maps_store(i).wait()
    store_acts.wait()


def weight_update(live, ft_all, gathered, moment, weight, maps, acts, sums, mixed, smalls):
    groups, parts, _, rows, outs = gathered.shape
    width = weight.shape[1]
    chunks = 2 * parts - 3
    base = rows * 3 // 4
    here = pl.BlockSpec(memory_space=pltpu.VMEM)
    far = pl.BlockSpec(memory_space=pl.ANY)
    ahead, behind = 3, 2
    vmem, dma = pltpu.VMEM, pltpu.SemaphoreType.DMA
    return pl.pallas_call(
        functools.partial(update_kernel, chunks, base),
        in_specs=[pl.BlockSpec(memory_space=pltpu.SMEM)] + [far] * 6 + [here] * (2 + len(smalls)),
        out_specs=[far] * 5 + [here] * 9,
        out_shape=[
            jax.ShapeDtypeStruct(moment.shape, F32),
            jax.ShapeDtypeStruct(moment.shape, BF16),
            jax.ShapeDtypeStruct(moment.shape, F32),
            jax.ShapeDtypeStruct(maps.shape, BF16),
            jax.ShapeDtypeStruct(acts.shape, BF16),
        ]
        + [jax.ShapeDtypeStruct(a.shape, F32) for a in smalls[::2] for _ in range(3)],
        scratch_shapes=[
            vmem((width, groups * rows), BF16),
            vmem((groups * (rows - base), groups * base), BF16),
            vmem((width, groups * base), BF16),
            vmem((ahead, groups, base, outs), BF16),
            vmem((ahead, width, outs), F32),
            vmem((ahead, width, outs), BF16),
            vmem((behind, width, outs), F32),
            vmem((behind, width, outs), BF16),
            vmem((behind, width, outs), F32),
            vmem(maps.shape, BF16),
            vmem(acts.shape, BF16),
            dma((2,)),
            dma((ahead, 3)),
            dma((behind, 3)),
            dma((chunks,)),
            dma((chunks,)),
            dma((2,)),
        ],
        compiler_params=params(),
        name="weight_update",
    )(live, ft_all, gathered, moment, weight, maps, acts, sums, mixed, *smalls)


def fast_shards(
    mesh,
    input_maps,
    dense_weight,
    dense_bias,
    stitch_in,
    stitch_out,
    weight_moment,
    bias_moment,
    stitch_in_moment,
    stitch_out_moment,
    cotangent,
    live_rows,
):
    maps = jnp.transpose(input_maps, (1, 3, 2, 0))
    gathered, ft_all, acts, maps_out, sums, mixed = step_all(
        mesh, live_rows, maps, dense_weight, cotangent, dense_bias, stitch_out, stitch_in
    )
    (
        weight_grad,
        weight_next,
        weight_moment_next,
        maps_grad,
        activations,
        bias_grad,
        bias_next,
        bias_moment_next,
        stitch_in_grad,
        stitch_in_next,
        stitch_in_moment_next,
        stitch_out_grad,
        stitch_out_next,
        stitch_out_moment_next,
    ) = weight_update(
        live_rows,
        ft_all,
        gathered,
        weight_moment,
        dense_weight,
        maps_out.reshape((-1,) + maps_out.shape[2:]),
        acts,
        sums,
        mixed,
        [dense_bias, bias_moment, stitch_in, stitch_in_moment, stitch_out, stitch_out_moment],
    )
    maps_grad = jnp.transpose(maps_grad.reshape(maps.shape), (3, 0, 2, 1))
    return (
        activations,
        maps_grad,
        weight_grad,
        bias_grad,
        stitch_in_grad,
        stitch_out_grad,
        weight_next,
        bias_next,
        stitch_in_next,
        stitch_out_next,
        weight_moment_next,
        bias_moment_next,
        stitch_in_moment_next,
        stitch_out_moment_next,
    )


def choose(mesh, *args):
    rows, _, chans, _ = args[0].shape
    outs = args[2].shape[1]
    shape = mesh.shape["batch"] == 4 and mesh.shape["mp"] == 8
    if shape and rows == 512 and outs == 512 and chans == 32:
        return fast_shards(mesh, *args)
    return shards(*args)


def solution(mesh):
    in_specs = (
        P("batch", None, "mp", None),
        P(None, "mp", None),
        P(None, "mp"),
        P(None, None, "mp"),
        P(None, None, "mp"),
        P(None, "mp", None),
        P(None, "mp"),
        P(None, None, "mp"),
        P(None, None, "mp"),
        P("batch", None, "mp"),
        P(),
    )
    out_specs = (
        P("batch", None, "mp"),
        P("batch", None, "mp", None),
        P(None, "mp", None),
        P(None, "mp"),
        P(None, None, "mp"),
        P(None, None, "mp"),
        P(None, "mp", None),
        P(None, "mp"),
        P(None, None, "mp"),
        P(None, None, "mp"),
        P(None, "mp", None),
        P(None, "mp"),
        P(None, None, "mp"),
        P(None, None, "mp"),
    )
    body = functools.partial(choose, mesh)
    return jax.shard_map(body, mesh=mesh, in_specs=in_specs, out_specs=out_specs, check_vma=False)
```

```python
import functools

import jax
import jax.numpy as jnp
from jax import lax
from jax.experimental import pallas as pl
from jax.experimental.pallas import tpu as pltpu
from jax.sharding import PartitionSpec as P

MESH = pl.DeviceIdType.MESH
BF16 = jnp.bfloat16
F32 = jnp.float32
VMEM_LIMIT = 60 * 1024 * 1024

MOMENTUM = 0.9
DENSE_RATE = 0.01
STITCH_RATE = 0.1


def pool_table():
    pixels = jnp.arange(169, dtype=jnp.int32)
    cells = jnp.arange(36, dtype=jnp.int32)
    pixel_row = (pixels // 13)[:, None]
    pixel_col = (pixels % 13)[:, None]
    cell_row = (cells // 6)[None, :]
    cell_col = (cells % 6)[None, :]
    inside = (
        (pixel_row >= 2 * cell_row)
        & (pixel_row <= 2 * cell_row + 2)
        & (pixel_col >= 2 * cell_col)
        & (pixel_col <= 2 * cell_col + 2)
    )
    return inside.astype(jnp.float32)


def gelu_tanh(value):
    return jax.nn.gelu(value, approximate=True)


def head(summed, cotangent, keep, dense_bias, stitch_out):
    hidden = summed + dense_bias[None]
    active, gelu_pull = jax.vjp(gelu_tanh, hidden)
    mixed = stitch_out[None, :, 0] * active[:, 0:1] + stitch_out[None, :, 1] * active[:, 1:2]
    activations = (mixed * keep[:, None, None]).astype(jnp.bfloat16)
    pulled = cotangent.astype(jnp.float32) * keep[:, None, None]
    stitch_out_grad = jnp.einsum("nio,njo->ijo", pulled, active, precision=lax.Precision.HIGHEST)
    active_grad = stitch_out[0][None] * pulled[:, 0:1] + stitch_out[1][None] * pulled[:, 1:2]
    hidden_grad = gelu_pull(active_grad)[0]
    bias_grad = jnp.sum(hidden_grad, axis=0)
    return (activations, hidden_grad.astype(jnp.bfloat16), bias_grad, stitch_out_grad)


def rows_layer(features, cotangent, keep, dense_weight, dense_bias, stitch_out):
    terms = jnp.einsum("ntk,tko->nto", features, dense_weight, preferred_element_type=jnp.float32)
    summed = lax.psum_scatter(terms, "mp", scatter_dimension=2, tiled=True)
    activations, summed_grad, bias_grad, stitch_out_grad = head(
        summed, cotangent, keep, dense_bias, stitch_out
    )
    piece = lax.all_gather(summed_grad, "mp", axis=2, tiled=True)
    inputs_grad = jnp.einsum(
        "nto,tko->ntk", piece, dense_weight, preferred_element_type=jnp.float32
    )
    update = jnp.einsum("ntk,nto->tko", features, piece, preferred_element_type=jnp.float32)
    weight_grad = update
    inputs_grad, weight_grad = (inputs_grad, weight_grad)
    return (activations, inputs_grad.astype(jnp.bfloat16), weight_grad, bias_grad, stitch_out_grad)


def dense_layer(features, cotangent, keep, dense_weight, dense_bias, stitch_out):
    return rows_layer(features, cotangent, keep, dense_weight, dense_bias, stitch_out)


def shards(
    input_maps,
    dense_weight,
    dense_bias,
    stitch_in,
    stitch_out,
    weight_moment,
    bias_moment,
    stitch_in_moment,
    stitch_out_moment,
    cotangent,
    live_rows,
):
    rows = input_maps.shape[0]
    chans = input_maps.shape[2]
    width = chans * 36
    group = lax.axis_index("batch")
    positions = jnp.arange(rows, dtype=jnp.int32)
    keep = (positions < live_rows[group]).astype(jnp.float32)
    table = pool_table()
    pooled = (
        jnp.einsum(
            "ntck,kq->ntcq",
            input_maps,
            table.astype(jnp.bfloat16),
            preferred_element_type=jnp.float32,
        )
        / 9.0
    )
    stitched = (
        stitch_in[None, :, 0, :, None] * pooled[:, 0:1]
        + stitch_in[None, :, 1, :, None] * pooled[:, 1:2]
    )
    features = stitched.reshape(rows, 2, width).astype(jnp.bfloat16)
    activations, inputs_grad, weight_grad, bias_grad, stitch_out_grad = dense_layer(
        features, cotangent, keep, dense_weight, dense_bias, stitch_out
    )
    stitched_grad = inputs_grad.astype(jnp.float32).reshape(rows, 2, chans, 36)
    stitch_in_grad = jnp.einsum(
        "nicq,njcq->ijc", stitched_grad, pooled, precision=lax.Precision.HIGHEST
    )
    pooled_grad = (
        stitch_in[0][None, :, :, None] * stitched_grad[:, 0:1]
        + stitch_in[1][None, :, :, None] * stitched_grad[:, 1:2]
    )
    maps_grad = jnp.einsum(
        "ntcq,kq->ntck", pooled_grad / 9.0, table, precision=lax.Precision.HIGHEST
    ).astype(jnp.bfloat16)
    weight_grad, bias_grad, stitch_in_grad, stitch_out_grad = lax.psum(
        (weight_grad, bias_grad, stitch_in_grad, stitch_out_grad), "batch"
    )
    weight_moment_next = MOMENTUM * weight_moment + weight_grad
    weight_next = (dense_weight.astype(jnp.float32) - DENSE_RATE * weight_moment_next).astype(
        jnp.bfloat16
    )
    bias_moment_next = MOMENTUM * bias_moment + bias_grad
    bias_next = dense_bias - DENSE_RATE * bias_moment_next
    stitch_in_moment_next = MOMENTUM * stitch_in_moment + stitch_in_grad
    stitch_in_next = stitch_in - STITCH_RATE * stitch_in_moment_next
    stitch_out_moment_next = MOMENTUM * stitch_out_moment + stitch_out_grad
    stitch_out_next = stitch_out - STITCH_RATE * stitch_out_moment_next
    return (
        activations,
        maps_grad,
        weight_grad,
        bias_grad,
        stitch_in_grad,
        stitch_out_grad,
        weight_next,
        bias_next,
        stitch_in_next,
        stitch_out_next,
        weight_moment_next,
        bias_moment_next,
        stitch_in_moment_next,
        stitch_out_moment_next,
    )


def params():
    return pltpu.CompilerParams(vmem_limit_bytes=VMEM_LIMIT)


def full(shape):
    return pl.BlockSpec(shape, lambda *_: (0,) * len(shape))


def fill_order(order, chans, inverse):
    size = order.shape[0]
    rows = lax.broadcasted_iota(jnp.int32, (size, size), 0)
    cols = lax.broadcasted_iota(jnp.int32, (size, size), 1)
    natural, cells = (cols, rows) if inverse else (rows, cols)
    shift = chans.bit_length() - 1
    hit = natural == 36 * (cells & (chans - 1)) + (cells >> shift)
    order[...] = jnp.where(hit, 1.0, 0.0).astype(BF16)


def spread_mix(mix_ref, wide):
    chans = wide.shape[1]
    rows = lax.broadcasted_iota(jnp.int32, (chans, chans), 0)
    cols = lax.broadcasted_iota(jnp.int32, (chans, chans), 1)
    for k in range(4):
        line = jnp.broadcast_to(mix_ref[k // 2, pl.ds(k % 2, 1), :], (chans, chans))
        column = jnp.sum(jnp.where(rows == cols, line, 0.0), axis=1, keepdims=True)
        wide[k] = jnp.broadcast_to(column, wide.shape[1:])


def pooled_row(maps_ref, tower, i, lanes):
    sums = None
    for dy in range(3):
        line = [maps_ref[tower, 26 * i + 13 * dy + x, :, lanes].astype(F32) for x in range(13)]
        cells = [line[2 * j] + line[2 * j + 1] + line[2 * j + 2] for j in range(6)]
        sums = cells if sums is None else [a + b for a, b in zip(sums, cells)]
    return [s * (1.0 / 9.0) for s in sums]


def gelu_parts(v):
    root = 0.7978845608028654
    square = v * v
    tanh = jnp.tanh(root * v * (1.0 + 0.044715 * square))
    half = 0.5 * (1.0 + tanh)
    slope = half + 0.5 * v * (1.0 - tanh * tanh) * root * (1.0 + 3.0 * 0.044715 * square)
    return v * half, slope


def neighbours():
    b, m = lax.axis_index("batch"), lax.axis_index("mp")
    columns = (b, b + 1 - 2 * (b % 2), b + 2 - 4 * (b // 2), 3 - b)
    return b, m, m // 2, m % 2, columns


def greet(columns, m, z, c, nz):
    b, bx, by, _ = columns
    sibling = m + 1 - 2 * c
    barrier = pltpu.get_barrier_semaphore()

    def signal(bb, mm):
        pl.semaphore_signal(barrier, inc=1, device_id=(bb, mm), device_id_type=MESH)

    signal(bx, m)
    signal(by, m)
    signal(b, sibling)
    pl.when(z > 0)(lambda: signal(b, m - 2))
    pl.when(z < nz - 1)(lambda: signal(b, m + 2))
    pl.semaphore_wait(barrier, 3 + jnp.where(z > 0, 1, 0) + jnp.where(z < nz - 1, 1, 0))


def remote(src, dst, send, recv, device):
    return pltpu.make_async_remote_copy(
        src_ref=src, dst_ref=dst, send_sem=send, recv_sem=recv, device_id=device, device_id_type=MESH
    )


def mix_row(chans, i, lanes, maps_ref, cells, total):
    pooled = [pooled_row(maps_ref, t, i, lanes) for t in range(2)]
    sums = [total[k] for k in range(4)]
    for j in range(6):
        span = pl.ds(pl.multiple_of((6 * i + j) * chans, chans), chans)
        for t in range(2):
            grad = cells[t, span, lanes].astype(F32)
            for s in range(2):
                sums[2 * t + s] += grad * pooled[s][j]
    for k in range(4):
        total[k] = sums[k]


def unpool_row(chans, i, channels, lanes, cells, above, wide, out_ref):
    start, count = channels
    rows = pl.ds(start, count)
    for t in range(2):
        mixed = []
        for j in range(6):
            span = pl.ds(pl.multiple_of((6 * i + j) * chans + start, count), count)
            first, second = (cells[k, span, lanes].astype(F32) for k in range(2))
            mixed.append((wide[t, rows] * first + wide[2 + t, rows] * second) * (1.0 / 9.0))
        for x in range(13):
            if x % 2 == 1 or x == 0:
                value = mixed[x // 2]
            elif x == 12:
                value = mixed[5]
            else:
                value = mixed[x // 2 - 1] + mixed[x // 2]
            out_ref[t, 26 * i + x, rows, lanes] = (value + above[t, x, :, lanes]).astype(BF16)
            out_ref[t, 26 * i + 13 + x, rows, lanes] = value.astype(BF16)
            above[t, x, :, lanes] = value


def shares(live_ref, groups, base):
    counts = [live_ref[k] for k in range(groups)]
    excess, free = [], []
    taken = given = 0
    for count in counts:
        excess.append(taken)
        free.append(given)
        taken = taken + jnp.maximum(count - base, 0)
        given = given + jnp.maximum(base - count, 0)
    return counts, excess, free


def picks(count, free, other, excess, base, spare, slots_in_lanes):
    shape = (spare, base) if slots_in_lanes else (base, spare)
    slot = lax.broadcasted_iota(jnp.int32, shape, 1 if slots_in_lanes else 0)
    row = lax.broadcasted_iota(jnp.int32, shape, 0 if slots_in_lanes else 1)
    hit = (slot - count + free == row + excess) & (slot >= count) & (row < other - base)
    return jnp.where(hit, 1.0, 0.0).astype(BF16)


def gather_phase(nz, cut, base, features_on, live_ref, pool_ref, pool, s_ref, acts_in, sums_ref, w_ref, maps_in, wide,
                 g_ref, acts_to, out_ref, total_ref, mixed_ref, sums_in, mix_in, sems,
                 keep_sem, out_sem, w_sem, col_sem, acts_sem,
                 acts_out, wbuf, col, grads, cells, order, mix_total):
    (line_send, line_recv, cross_send, cross_recv, half_send, half_recv, core_send, core_recv,
     small_send, small_recv, sums_mid, mix_mid) = sems
    b, m, z, c, columns = neighbours()
    rows = s_ref.shape[1]
    spans = (pl.ds(0, cut), pl.ds(cut, base - cut), pl.ds(base, rows - base))
    spare = rows - base
    sibling = m + 1 - 2 * c

    def small(kind, axis, src, dst):
        return remote(src, dst, small_send.at[kind, axis], small_recv.at[kind, axis], (columns[1 + axis], m))

    def place(p, r, zz):
        return g_ref.at[columns[r], 2 * zz + c, :, spans[p], :]

    def half(p, r, zz, t):
        return g_ref.at[columns[r], 2 * zz + c, t, spans[p], :]

    def line(k, zz, up, own=False):
        p, r = {0: (0, 0), 5: (2, 0)}.get(k, (1, k - 1))
        src = s_ref.at[:, spans[p], :] if own else place(p, r, zz)
        side = 1 if up else 0
        to = m + 2 if up else m - 2
        return remote(src, place(p, r, zz), line_send.at[side, k, zz], line_recv.at[k, zz], (b, to))

    def cross(p, axis, zz, own=False):
        src = s_ref.at[:, spans[p], :] if own else place(p, 0, zz)
        slot = zz if p == 0 else nz
        return remote(
            src, place(p, 0, zz), cross_send.at[axis, slot], cross_recv.at[axis, slot], (columns[1 + axis], m)
        )

    def cross_wait(p, axis, zz):
        slot = zz if p == 0 else nz
        here = place(p, 1 + axis, zz)
        remote(here, here, cross_send.at[axis, slot], cross_recv.at[axis, slot], (columns[1 + axis], m)).wait_recv()

    def diagonal(p, axis, zz):
        slot = zz if p == 0 else nz
        block = half(p, 2 - axis, zz, 1 - axis)
        return remote(block, block, half_send.at[axis, slot], half_recv.at[axis, slot], (columns[1 + axis], m))

    def diagonal_wait(p, axis, zz):
        slot = zz if p == 0 else nz
        block = half(p, 3, zz, 1 - axis)
        remote(block, block, half_send.at[axis, slot], half_recv.at[axis, slot], (columns[1 + axis], m)).wait_recv()

    def core(p, r, zz, own=False):
        src = s_ref.at[:, spans[p], :] if own else place(p, r, zz)
        return remote(src, place(p, r, zz), core_send.at[p, r, zz], core_recv.at[p, r, zz], (b, sibling))

    def core_wait(p, r, zz):
        block = g_ref.at[columns[r], 2 * zz + 1 - c, :, spans[p], :]
        remote(block, block, core_send.at[p, r, zz], core_recv.at[p, r, zz], (b, sibling)).wait_recv()

    def sides(d, body):
        if d == 0:
            body(z, None)
            return
        pl.when(z + d < nz)(lambda: body(z + d, False))
        pl.when(z - d >= 0)(lambda: body(z - d, True))

    def onward(k, zz, up):
        if up:
            pl.when(z < nz - 1)(lambda: line(k, zz, True).start())
        else:
            pl.when(z > 0)(lambda: line(k, zz, False).start())

    mine = pltpu.make_async_copy(s_ref, g_ref.at[b, m], keep_sem)

    def launch(k):
        pl.when(z < nz - 1)(lambda: line(k, z, True, True).start())
        pl.when(z > 0)(lambda: line(k, z, False, True).start())

    first_sums = small(0, 0, sums_ref, sums_in.at[0])
    first_sums.start()
    launch(5)
    core(2, 0, z, True).start()
    counts, excess, free = shares(live_ref, 4, base)
    live = live_ref[b]
    offset = 0
    for k in range(1, 4):
        offset = offset + jnp.where(b >= k, jnp.maximum(base - counts[k - 1], 0), 0)
    chosen = jnp.concatenate(
        [picks(live, offset, counts[k], excess[k], base, spare, False) for k in range(4)], axis=1
    )
    for axis in range(2):
        pool.end(axis)
    for t in range(2):
        moved = jnp.dot(chosen, pool_ref[t], preferred_element_type=F32)
        s_ref[t, :base, :] = (s_ref[t, :base, :].astype(F32) + moved).astype(BF16)
    cross(1, 0, z, True).start()
    cross(1, 1, z, True).start()
    launch(0)
    cross(0, 0, z, True).start()
    cross(0, 1, z, True).start()
    launch(1)
    core(0, 0, z, True).start()
    core(1, 0, z, True).start()
    mine.start()

    def pass_cross(p, zz):
        for axis in range(2):
            cross_wait(p, axis, zz)
            diagonal(p, 1 - axis, zz).start()
            core(p, 1 + axis, zz).start()

    def end_diagonal(p, zz):
        for axis in range(2):
            diagonal_wait(p, axis, zz)
        core(p, 3, zz).start()

    def arrive(zz, up):
        line(0, zz, up).wait_recv()
        onward(0, zz, up)
        cross(0, 0, zz).start()
        cross(0, 1, zz).start()
        core(0, 0, zz).start()
        for k, p in ((1, 1), (5, 2)):
            line(k, zz, up).wait_recv()
            onward(k, zz, up)
            core(p, 0, zz).start()

    def late(zz, up):
        for k in range(2, 5):
            line(k, zz, up).wait_recv()
            onward(k, zz, up)
            core(1, k - 1, zz).start()

    def spread():
        for k in range(2, 5):
            pl.when(z < nz - 1)(lambda k=k: line(k, z, True).start())
            pl.when(z > 0)(lambda k=k: line(k, z, False).start())

    def join_towers(k, carry):
        here = pl.ds(pl.multiple_of(k * 16, 16), 16)
        both = jnp.stack([acts_in[t, here, :].astype(F32) for t in range(2)], axis=1)
        acts_out[here, :, :] = both.astype(BF16)
        return carry

    pass_cross(1, z)
    lax.fori_loop(0, rows // 16, join_towers, 0)
    store_acts = pltpu.make_async_copy(acts_out, acts_to, acts_sem)
    store_acts.start()
    sides(1, arrive)
    pass_cross(0, z)
    end_diagonal(1, z)
    sides(2, arrive)
    width, chans = w_ref.shape[1], maps_in.shape[2]
    outs = s_ref.shape[2]
    piece = wbuf.shape[1]
    pieces = width // piece

    def weights(k):
        t, at = k // pieces, k % pieces * piece
        return pltpu.make_async_copy(w_ref.at[t, pl.ds(at, piece), :], wbuf.at[k % 2], w_sem.at[k % 2])

    def column(t, j):
        return pltpu.make_async_copy(
            g_ref.at[b, j, t], col.at[:, pl.ds(j * outs, outs)], col_sem.at[j]
        )

    def features_grad(t):
        for k in range(t * pieces, (t + 1) * pieces):
            if k + 1 < 2 * pieces:
                weights(k + 1).start()
            weights(k).wait()
            if k == t * pieces:
                for j in range(2 * nz):
                    column(t, j).wait()
            value = lax.dot_general(
                wbuf[k % 2], col[...], (((1,), (1,)), ((), ())), preferred_element_type=F32
            )
            lane = lax.broadcasted_iota(jnp.int32, value.shape, 1)
            grads[pl.ds(k % pieces * piece, piece), :] = jnp.where(lane < live, value, 0.0).astype(BF16)
        cells[t] = jnp.dot(order[...], grads[...], preferred_element_type=F32).astype(BF16)

    blocks = rows // 128

    def maps_back(step, carry):
        i = step // blocks
        lanes = pl.ds(pl.multiple_of(step % blocks * 128, 128), 128)
        mix_row(chans, i, lanes, maps_in, cells, mix_total)
        return carry

    weights(0).start()
    fill_order(order, chans, True)
    mix_total[...] = jnp.zeros_like(mix_total)
    first_sums.wait()
    sums_mid[...] = sums_ref[...] + sums_in[0]
    second_sums = small(0, 1, sums_mid, sums_in.at[1])
    second_sums.start()
    outer = (z == 0) | (z == nz - 1)
    inner = (z > 0) & (z < nz - 1)

    @pl.when(outer)
    def _():
        sides(1, lambda zz, up: pass_cross(0, zz))
        sides(3, arrive)
        spread()

    features_on(0)
    mine.wait()
    for zz in range(nz):
        for p in range(3):
            core_wait(p, 0, zz)
    for j in range(2 * nz):
        column(0, j).start()
    features_grad(0)
    for j in range(2 * nz):
        column(1, j).start()
    pl.when(inner)(spread)
    pl.when(outer)(lambda: sides(1, late))
    features_grad(1)

    @pl.when(inner)
    def _():
        sides(1, lambda zz, up: pass_cross(0, zz))
        sides(1, late)

    end_diagonal(0, z)
    pl.when(inner)(lambda: sides(2, late))
    pl.when(outer)(lambda: sides(2, lambda zz, up: pass_cross(0, zz)))
    lax.fori_loop(0, 3 * blocks, maps_back, 0)
    pl.when(outer)(lambda: sides(2, late))
    lax.fori_loop(3 * blocks, 6 * blocks, maps_back, 0)
    store_cells = pltpu.make_async_copy(cells, out_ref, out_sem)
    store_cells.start()
    for k in range(4):
        mix_in[0, k] = jnp.broadcast_to(jnp.sum(mix_total[k], axis=1, keepdims=True), (chans, 128))
    first_mix = small(1, 0, mix_in.at[0], mix_in.at[1])
    first_mix.start()
    pl.when(inner)(lambda: sides(2, lambda zz, up: pass_cross(0, zz)))
    sides(1, lambda zz, up: end_diagonal(0, zz))
    sides(3, lambda zz, up: pass_cross(0, zz))
    first_mix.wait()
    mix_mid[...] = mix_in[0] + mix_in[1]
    second_mix = small(1, 1, mix_mid, mix_in.at[2])
    second_mix.start()
    sides(2, lambda zz, up: end_diagonal(0, zz))
    sides(3, late)
    sides(3, lambda zz, up: end_diagonal(0, zz))
    second_sums.wait()
    total_ref[...] = sums_mid[...] + sums_in[1]
    second_mix.wait()
    mixed_ref[...] = mix_mid[...] + mix_in[2]
    store_cells.wait()
    store_acts.wait()

    for zz in range(nz):
        for r in range(4):
            for p in range(2):
                if r > 0:
                    core_wait(p, r, zz)
                core(p, r, zz).wait_send()
        core(2, 0, zz).wait_send()
        for axis in range(2):
            cross(0, axis, zz).wait_send()
            diagonal(0, axis, zz).wait_send()
        for k in range(6):
            pl.when((z < nz - 1) & (z >= zz))(lambda k=k, zz=zz: line(k, zz, True).wait_send())
            pl.when((z > 0) & (z <= zz))(lambda k=k, zz=zz: line(k, zz, False).wait_send())
    for axis in range(2):
        cross(1, axis, z).wait_send()
        diagonal(1, axis, z).wait_send()


def head_rows(hidden, cot, keep, mix, act_ref, grad_ref, here, lanes):
    active, slope, pulled = [], [], []
    for t in range(2):
        value, rate = gelu_parts(hidden[t])
        active.append(value)
        slope.append(rate)
        pulled.append(cot[t] * keep)
    for i in range(2):
        mixed = mix[2 * i] * active[0] + mix[2 * i + 1] * active[1]
        act_ref[i, here, lanes] = (mixed * keep).astype(BF16)
    terms = [pulled[i] * active[j] for i in range(2) for j in range(2)]
    for j in range(2):
        grad = (mix[j] * pulled[0] + mix[2 + j] * pulled[1]) * slope[j]
        grad_ref[j, here, lanes] = grad.astype(BF16)
        terms.append(grad)
    return terms


def step_kernel(nz, cut, base, live_ref, maps_ref, w_ref, cot_raw, bias_ref, mix_ref, mix_in_ref,
                g_ref, fta_ref, acts_to, out_ref, total_ref, mixed_ref,
                maps_in, rb, inb, ft_ref, s_ref, acts_in, sums_ref, wide, sums_in, mix_in,
                maps_sem, swap_send, swap_recv, hop_send, hop_recv,
                feat_send, feat_recv, turn_send, turn_recv, feat_keep,
                pool_ref, pool_send, pool_recv, pool_turn_send, pool_turn_recv, *rest):
    b, m, z, c, columns = neighbours()
    sibling = m + 1 - 2 * c
    chans, rows = maps_in.shape[2:]
    width, outs = w_ref.shape[1], s_ref.shape[2]
    span = rows // 2

    def load_maps(h):
        lanes = pl.ds(h * span, span)
        return pltpu.make_async_copy(maps_ref.at[:, :, :, lanes], maps_in.at[:, :, :, lanes], maps_sem.at[h])

    for h in (1, 0):
        load_maps(h).start()

    def features(r, t, h):
        start = pl.multiple_of(columns[r] * rows + h * span, span)
        return fta_ref.at[t, :, pl.ds(start, span)]

    def mine(t, h):
        return pltpu.make_async_copy(ft_ref.at[t, :, pl.ds(h * span, span)], features(0, t, h), feat_keep.at[t, h])

    def feature(axis, t, h):
        return remote(ft_ref.at[t, :, pl.ds(h * span, span)], features(0, t, h), feat_send.at[axis, t, h],
                      feat_recv.at[axis, t, h], (columns[1 + axis], m))

    def feature_wait(axis, t, h):
        here = features(1 + axis, t, h)
        remote(here, here, feat_send.at[axis, t, h], feat_recv.at[axis, t, h], (columns[1 + axis], m)).wait_recv()

    def turn(axis, h):
        here = features(2 - axis, 1 - axis, h)
        return remote(here, here, turn_send.at[axis, h], turn_recv.at[axis, h], (columns[1 + axis], m))

    def turn_wait(axis, h):
        here = features(3, 1 - axis, h)
        remote(here, here, turn_send.at[axis, h], turn_recv.at[axis, h], (columns[1 + axis], m)).wait_recv()

    def features_on(h):
        for axis in range(2):
            feature_wait(1 - axis, 1 - axis, h)
            turn(axis, h).start()

    spare = rows - base

    class pool:
        def slot(r, t=None):
            start = pl.ds(pl.multiple_of(columns[r] * spare, spare), spare)
            return pool_ref.at[:, start, :] if t is None else pool_ref.at[t, start, :]

        def go(axis):
            return remote(s_ref.at[:, pl.ds(base, spare), :], pool.slot(0), pool_send.at[axis], pool_recv.at[axis],
                          (columns[1 + axis], m))

        def come(axis):
            here = pool.slot(1 + axis)
            remote(here, here, pool_send.at[axis], pool_recv.at[axis], (columns[1 + axis], m)).wait_recv()

        def turn(axis):
            here = pool.slot(2 - axis, 1 - axis)
            return remote(here, here, pool_turn_send.at[axis], pool_turn_recv.at[axis], (columns[1 + axis], m))

        def end(axis):
            here = pool.slot(3, 1 - axis)
            remote(here, here, pool_turn_send.at[axis], pool_turn_recv.at[axis], (columns[1 + axis], m)).wait_recv()

    def forward(cells, order, f_ref, cot_in, cot_ref, wbuf, pb, sb, cot_sem, w_sem):
        live = live_ref[b]
        near = jnp.where(z < nz // 2, 1, 0)

        def weights(i, t, own):
            zd = near * (nz - 1 - i) + (1 - near) * i
            j = 2 * zd + (c if own else 1 - c)
            lanes = pl.ds(pl.multiple_of(j * outs, outs), outs)
            k = 2 * t + own
            return pltpu.make_async_copy(w_ref.at[t, :, lanes], wbuf.at[k], w_sem.at[k])

        for t in range(2):
            for own in range(2):
                weights(0, t, own).start()
        load_cot = pltpu.make_async_copy(cot_raw, cot_in, cot_sem)
        load_cot.start()
        fill_order(order, chans, False)
        spread_mix(mix_in_ref, wide)
        greet(columns, m, z, c, nz)

        def swap(d, t, h):
            here = pl.ds(h * span, span)
            return remote(sb.at[d, t, here], rb.at[d, t, here], swap_send.at[d, t, h], swap_recv.at[d, t, h], (b, sibling))

        def hop(up, d, t, h):
            here = pl.ds(h * span, span)
            return remote(rb.at[d, t, here], inb.at[d + up, t, here], hop_send.at[d, t, h], hop_recv.at[up, d, t, h],
                          (b, m + 4 * up - 2))

        step = 64

        def relay(up, dm, t, h, first):
            zm = up * z + (1 - up) * (nz - 1 - z)
            d = up * dm + (1 - up) * (nz - 1 - dm)

            def go():
                swap(d, t, h).wait_recv()
                if not first:
                    hop(up, d, t, h).wait_recv()

                def add(k, carry):
                    here = pl.ds(pl.multiple_of(h * span + k * step, step), step)
                    value = pb[d, t, here, :] + rb[d, t, here, :].astype(F32)
                    if not first:
                        value += inb[d + up, t, here, :].astype(F32)
                    rb[d, t, here, :] = value.astype(BF16)
                    return carry

                lax.fori_loop(0, span // step, add, 0)
                hop(up, d, t, h).start()

            pl.when((zm == 0 if first else zm > 0) & (zm < dm))(go)

        narrow = span // 128

        def pool_maps(h):
            def pool_row(step, carry):
                i = step // narrow
                at = pl.multiple_of(step % narrow * 128, 128)
                lanes = pl.ds(pl.multiple_of(h * span + at, 128), 128)
                first = pooled_row(maps_in, 0, i, lanes)
                second = pooled_row(maps_in, 1, i, lanes)
                for t in range(2):
                    for j in range(6):
                        value = wide[2 * t] * first[j] + wide[2 * t + 1] * second[j]
                        start = pl.multiple_of((6 * i + j) * chans, chans)
                        cells[t, pl.ds(start, chans), pl.ds(at, 128)] = value.astype(BF16)
                return carry

            load_maps(h).wait()
            lax.fori_loop(0, 6 * narrow, pool_row, 0)
            for t in range(2):
                moved = jnp.dot(order[...], cells[t], preferred_element_type=F32).astype(BF16)
                ft_ref[t, :, pl.ds(h * span, span)] = moved
                f_ref[t, pl.ds(h * span, span), :] = moved.T
            for k in range(2):
                feature(0, k, h).start()
                feature(1, 1 - k, h).start()

        def produce(i, h):
            zd = near * (nz - 1 - i) + (1 - near) * i
            here = pl.ds(h * span, span)
            for t in range(2):
                for own in range(2):
                    if h == 1:
                        weights(i, t, own).wait()
                    part = jnp.dot(f_ref[t, here, :], wbuf[2 * t + own], preferred_element_type=F32)
                    if own:
                        pb[zd, t, here, :] = part
                    else:
                        sb[zd, t, here, :] = part.astype(BF16)
                        swap(zd, t, h).start()
                    if h == 0:
                        pl.when(i < nz - 1)(lambda t=t, own=own: weights(i + 1, t, own).start())
                relay(near, nz - 1 - i, t, h, True)

        for h in (1, 0):
            pool_maps(h)
            produce(0, h)

        def both(i, carry):
            for h in (1, 0):
                produce(i, h)
            return carry

        lax.fori_loop(1, nz, both, 0)

        features_on(1)
        for t in range(2):
            for h in range(2):
                mine(t, h).start()
        load_cot.wait()

        def part_towers(k, carry):
            here = pl.ds(pl.multiple_of(k * 16, 16), 16)
            both = cot_in[here, :, :].astype(F32)
            for t in range(2):
                cot_ref[t, here, :] = both[:, t, :].astype(BF16)
            return carry

        lax.fori_loop(0, rows // 16, part_towers, 0)
        for dm in range(nz - 1, 0, -1):
            for h in (1, 0):
                for t in range(2):
                    relay(near, dm, t, h, False)
                    relay(1 - near, dm, t, h, False)

        tile, high = 256, 16
        for h in (1, 0):
            for t in range(2):
                swap(z, t, h).wait_recv()
                pl.when(z > 0)(lambda t=t, h=h: hop(1, z, t, h).wait_recv())
                pl.when(z < nz - 1)(lambda t=t, h=h: hop(0, z, t, h).wait_recv())

                def gather(k, carry, t=t, h=h):
                    here = pl.ds(pl.multiple_of(h * span + k * step, step), step)
                    pb[z, t, here, :] += rb[z, t, here, :].astype(F32)
                    for up in range(2):
                        inside = z > 0 if up else z < nz - 1

                        @pl.when(inside)
                        def _(up=up):
                            pb[z, t, here, :] += inb[z + up, t, here, :].astype(F32)

                    return carry

                lax.fori_loop(0, span // step, gather, 0)
            if h == 0:
                for axis in range(2):
                    pool.come(axis)
                    pool.turn(1 - axis).start()
            for lane in range(outs // tile):
                lanes = pl.ds(lane * tile, tile)
                bias = [bias_ref[pl.ds(t, 1), lanes] for t in range(2)]
                mix = [mix_ref[k // 2, pl.ds(k % 2, 1), lanes] for k in range(4)]

                def block(k, totals, lanes=lanes, bias=bias, mix=mix):
                    here = pl.ds(pl.multiple_of(k * high, high), high)
                    hidden = [pb[z, t, here, lanes] + bias[t] for t in range(2)]
                    cot = [cot_ref[t, here, lanes].astype(F32) for t in range(2)]
                    place = k * high + lax.broadcasted_iota(jnp.int32, (high, tile), 0)
                    keep = jnp.where(place < live, 1.0, 0.0)
                    terms = head_rows(hidden, cot, keep, mix, acts_in, s_ref, here, lanes)
                    return tuple(a + v[:8] + v[8:] for a, v in zip(totals, terms))

                zero = jnp.zeros((8, tile), F32)
                count = span // high
                totals = lax.fori_loop(h * count, (h + 1) * count, block, (zero,) * 6)
                for k in range(6):
                    value = jnp.sum(totals[k], axis=0, keepdims=True)
                    sums_ref[k, :, lanes] = value if h == 1 else sums_ref[k, :, lanes] + value
            if h == 1:
                here = pl.ds(pl.multiple_of(b * spare, spare), spare)
                pool_ref[:, here, :] = s_ref[:, base:, :]
                for axis in range(2):
                    pool.go(axis).start()
        for d in range(nz):
            for t in range(2):
                for h in range(2):
                    swap(d, t, h).wait_send()
                    pl.when(z < d)(lambda d=d, t=t, h=h: hop(1, d, t, h).wait_send())
                    pl.when(z > d)(lambda d=d, t=t, h=h: hop(0, d, t, h).wait_send())

    vmem, dma = pltpu.VMEM, pltpu.SemaphoreType.DMA
    pl.run_scoped(
        forward,
        vmem((2, width, span), BF16),
        vmem((width, width), BF16),
        vmem((2, rows, width), BF16),
        vmem(cot_raw.shape, BF16),
        vmem((2, rows, outs), BF16),
        vmem((4, width, outs), BF16),
        vmem((nz, 2, rows, outs), F32),
        vmem((nz, 2, rows, outs), BF16),
        dma,
        dma((4,)),
    )
    pl.run_scoped(
        functools.partial(gather_phase, nz, cut, base, features_on, live_ref, pool_ref, pool, s_ref, acts_in, sums_ref, w_ref, maps_in, wide,
                          g_ref, acts_to, out_ref, total_ref, mixed_ref, sums_in, mix_in, rest),
        dma,
        dma,
        dma((2,)),
        dma((2 * nz,)),
        dma,
        vmem((rows, 2, outs), BF16),
        vmem((2, width // 3, 2 * nz * outs), BF16),
        vmem((rows, 2 * nz * outs), BF16),
        vmem((width, rows), BF16),
        vmem((2, width, rows), BF16),
        vmem((width, width), BF16),
        vmem((4, chans, 128), F32),
    )
    for h in range(2):
        for axis in range(2):
            feature_wait(axis, 1 - axis, h)
            turn_wait(axis, h)
            turn(axis, h).wait_send()
            for t in range(2):
                feature(axis, t, h).wait_send()
        for t in range(2):
            mine(t, h).wait()
    for axis in range(2):
        pool.go(axis).wait_send()
        pool.turn(axis).wait_send()


def step_all(mesh, live, maps, weight, cot, bias, mix, mix_in):
    groups, parts = mesh.shape["batch"], mesh.shape["mp"]
    nz = parts // 2
    chans, rows = maps.shape[2:]
    width = weight.shape[1]
    outs = weight.shape[2] // parts
    base = rows * 3 // 4
    cut = rows * 19 // 32
    vmem, dma = pltpu.VMEM, pltpu.SemaphoreType.DMA
    here = pl.BlockSpec(memory_space=pltpu.VMEM)
    far = pl.BlockSpec(memory_space=pl.ANY)
    sums = (6, 1, outs)
    return pl.pallas_call(
        functools.partial(step_kernel, nz, cut, base),
        in_specs=[pl.BlockSpec(memory_space=pltpu.SMEM), far, far, far, here, here, here],
        out_specs=[far, far, far, far, here, here],
        out_shape=[
            jax.ShapeDtypeStruct((groups, parts, 2, rows, outs), BF16),
            jax.ShapeDtypeStruct((2, width, groups * rows), BF16),
            jax.ShapeDtypeStruct((rows, 2, outs), BF16),
            jax.ShapeDtypeStruct((2, width, rows), BF16),
            jax.ShapeDtypeStruct(sums, F32),
            jax.ShapeDtypeStruct((4, chans, 128), F32),
        ],
        scratch_shapes=[
            vmem(maps.shape, BF16),
            vmem((nz, 2, rows, outs), BF16),
            vmem((nz + 1, 2, rows, outs), BF16),
            vmem((2, width, rows), BF16),
            vmem((2, rows, outs), BF16),
            vmem((2, rows, outs), BF16),
            vmem(sums, F32),
            vmem((4, chans, 128), F32),
            vmem((2,) + sums, F32),
            vmem((3, 4, chans, 128), F32),
            dma((2,)),
            dma((nz, 2, 2)),
            dma((nz, 2, 2)),
            dma((nz, 2, 2)),
            dma((2, nz, 2, 2)),
            dma((2, 2, 2)),
            dma((2, 2, 2)),
            dma((2, 2)),
            dma((2, 2)),
            dma((2, 2)),
            vmem((2, groups * (rows - base), outs), BF16),
            dma((2,)),
            dma((2,)),
            dma((2,)),
            dma((2,)),
            dma((2, 6, nz)),
            dma((6, nz)),
            dma((2, nz + 1)),
            dma((2, nz + 1)),
            dma((2, nz + 1)),
            dma((2, nz + 1)),
            dma((3, 4, nz)),
            dma((3, 4, nz)),
            dma((2, 2)),
            dma((2, 2)),
            vmem(sums, F32),
            vmem((4, chans, 128), F32),
        ],
        compiler_params=pltpu.CompilerParams(
            collective_id=0, has_side_effects=True, vmem_limit_bytes=VMEM_LIMIT
        ),
        name="step_all",
    )(live, maps, weight, cot, bias, mix, mix_in)


def turn_mix(wide):
    chans = wide.shape[0]
    rows = lax.broadcasted_iota(jnp.int32, (chans, chans), 0)
    cols = lax.broadcasted_iota(jnp.int32, (chans, chans), 1)
    return jnp.sum(jnp.where(rows == cols, wide[:, :chans], 0.0), axis=0, keepdims=True)


def update_kernel(base, live_ref, ft_ref, s_ref, m_ref, w_ref, cells_ref, acts_ref, sums_ref, mixed_ref,
                  bias_ref, bias_m_ref, in_ref, in_m_ref, out_ref, out_m_ref,
                  grad_to, next_to, moment_to, maps_to, acts_to, bias_g, bias_n, bias_mn,
                  in_g, in_n, in_mn, out_g, out_n, out_mn,
                  raw, chosen, ft, s_in, m_in, w_in, g_out, n_out, m_out, maps_out, cells, above, wide, acts_mid,
                  ft_sem, in_sem, out_sem, cells_sem, maps_sem, acts_sem):
    groups, parts, _, rows, tile = s_ref.shape
    spare = rows - base
    steps, ahead, behind = 2 * parts, s_in.shape[0], g_out.shape[0]
    chans, lanes_all = maps_out.shape[2:]
    share = chans // 2

    def loads(i):
        t, j, slot = i // parts, i % parts, i % ahead
        lanes = pl.ds(pl.multiple_of(j * tile, tile), tile)
        return [
            pltpu.make_async_copy(s_ref.at[:, j, t, pl.ds(0, base), :], s_in.at[slot], in_sem.at[slot, 0]),
            pltpu.make_async_copy(m_ref.at[t, :, lanes], m_in.at[slot], in_sem.at[slot, 1]),
            pltpu.make_async_copy(w_ref.at[t, :, lanes], w_in.at[slot], in_sem.at[slot, 2]),
        ]

    def stores(i):
        t, j, slot = i // parts, i % parts, i % behind
        lanes = pl.ds(pl.multiple_of(j * tile, tile), tile)
        return [
            pltpu.make_async_copy(g_out.at[slot], grad_to.at[t, :, lanes], out_sem.at[slot, 0]),
            pltpu.make_async_copy(m_out.at[slot], moment_to.at[t, :, lanes], out_sem.at[slot, 1]),
            pltpu.make_async_copy(n_out.at[slot], next_to.at[t, :, lanes], out_sem.at[slot, 2]),
        ]

    def each(copies, act):
        for copy in copies:
            act(copy)

    start, wait = lambda copy: copy.start(), lambda copy: copy.wait()

    load_cells = pltpu.make_async_copy(cells_ref, cells, cells_sem)

    def maps_store(unit, t):
        rows_two = pl.ds(pl.multiple_of(unit % 6 * 26, 26), 26)
        block = (t, rows_two, pl.ds(pl.multiple_of(unit // 6 * share, share), share))
        return pltpu.make_async_copy(maps_out.at[block], maps_to.at[block], maps_sem.at[unit, t])

    def last_store(half, t):
        block = (t, pl.ds(156, 13), pl.ds(half * share, share))
        return pltpu.make_async_copy(maps_out.at[block], maps_to.at[block], maps_sem.at[12 + half, t])

    def unpool(unit):
        i = unit % 6
        start = pl.multiple_of(unit // 6 * share, share)

        @pl.when(i == 0)
        def _():
            above[...] = jnp.zeros_like(above)

        def lane_block(k, carry):
            lanes = pl.ds(pl.multiple_of(k * 128, 128), 128)
            unpool_row(chans, i, (start, share), lanes, cells, above, wide, maps_out)
            return carry

        lax.fori_loop(0, lanes_all // 128, lane_block, 0)
        for t in range(2):
            maps_store(unit, t).start()
        for half in range(2):

            @pl.when(unit == 6 * half + 5)
            def _(half=half):
                for t in range(2):
                    for x in range(13):
                        maps_out[t, 156 + x, pl.ds(half * share, share)] = above[t, x].astype(BF16)
                    last_store(half, t).start()

    load_acts = pltpu.make_async_copy(acts_ref, acts_mid, acts_sem.at[0])
    store_acts = pltpu.make_async_copy(acts_mid, acts_to, acts_sem.at[1])
    towers = [pltpu.make_async_copy(ft_ref.at[t], raw, ft_sem.at[t]) for t in range(2)]
    towers[0].start()
    each(loads(0), start)
    counts, excess, free = shares(live_ref, groups, base)
    for k in range(groups):
        for n in range(groups):
            chosen[pl.ds(n * spare, spare), pl.ds(k * base, base)] = picks(
                counts[k], free[k], counts[n], excess[n], base, spare, True
            )

    def pack(t):
        towers[t].wait()
        last = jnp.concatenate([raw[:, k * rows + base : (k + 1) * rows] for k in range(groups)], axis=1)
        for k in range(groups):
            lanes = pl.ds(k * base, base)
            moved = jnp.dot(last, chosen[:, lanes], preferred_element_type=F32)
            lane = lax.broadcasted_iota(jnp.int32, moved.shape, 1)
            kept = raw[:, k * rows : k * rows + base].astype(F32)
            ft[:, lanes] = jnp.where(lane < counts[k], kept, moved).astype(BF16)

    def step(grad, value, moment, rate, at, grad_ref, next_ref, moment_ref):
        after = MOMENTUM * moment[at] + grad
        grad_ref[at] = grad
        moment_ref[at] = after
        next_ref[at] = value[at] - rate * after

    for i in range(2):
        at = (pl.ds(i, 1), slice(None))
        step(sums_ref[4 + i], bias_ref, bias_m_ref, DENSE_RATE, at, bias_g, bias_n, bias_mn)
        for j in range(2):
            at = (i, pl.ds(j, 1), slice(None))
            step(sums_ref[2 * i + j], out_ref, out_m_ref, STITCH_RATE, at, out_g, out_n, out_mn)
            step(turn_mix(mixed_ref[2 * i + j]), in_ref, in_m_ref, STITCH_RATE, at, in_g, in_n, in_mn)

    spread_mix(in_ref, wide)
    pack(0)
    towers[1].start()
    for i in range(1, ahead):
        each(loads(i), start)

    def body(i, carry):
        slot, to = i % ahead, i % behind

        pl.when(i == 0)(load_acts.start)
        pl.when(i == 0)(load_cells.start)
        pl.when(i == 2)(load_cells.wait)
        pl.when((i >= 2) & (i < 14))(lambda: unpool(i - 2))

        @pl.when(i == ahead)
        def _():
            load_acts.wait()
            store_acts.start()

        pl.when(i == parts)(lambda: pack(1))
        each(loads(i), wait)
        pl.when(i >= behind)(lambda: each(stores(i - behind), wait))
        grad = jnp.dot(
            ft[...], s_in[slot].reshape(groups * base, tile), preferred_element_type=F32
        )
        g_out[to] = grad
        moment = MOMENTUM * m_in[slot] + grad
        m_out[to] = moment
        n_out[to] = (w_in[slot].astype(F32) - DENSE_RATE * moment).astype(BF16)
        each(stores(i), start)
        pl.when(i + ahead < steps)(lambda: each(loads(i + ahead), start))
        return carry

    lax.fori_loop(0, steps, body, 0)
    for k in range(behind):
        each(stores(steps - behind + k), wait)
    for t in range(2):
        for unit in range(12):
            maps_store(unit, t).wait()
        for half in range(2):
            last_store(half, t).wait()
    store_acts.wait()


def weight_update(live, ft_all, gathered, moment, weight, maps_shape, cells, acts, sums, mixed, smalls):
    groups, parts, _, rows, outs = gathered.shape
    width = weight.shape[1]
    chans = maps_shape[2]
    base = rows * 3 // 4
    here = pl.BlockSpec(memory_space=pltpu.VMEM)
    far = pl.BlockSpec(memory_space=pl.ANY)
    ahead, behind = 3, 2
    vmem, dma = pltpu.VMEM, pltpu.SemaphoreType.DMA
    return pl.pallas_call(
        functools.partial(update_kernel, base),
        in_specs=[pl.BlockSpec(memory_space=pltpu.SMEM)] + [far] * 6 + [here] * (2 + len(smalls)),
        out_specs=[far] * 5 + [here] * 9,
        out_shape=[
            jax.ShapeDtypeStruct(moment.shape, F32),
            jax.ShapeDtypeStruct(moment.shape, BF16),
            jax.ShapeDtypeStruct(moment.shape, F32),
            jax.ShapeDtypeStruct(maps_shape, BF16),
            jax.ShapeDtypeStruct(acts.shape, BF16),
        ]
        + [jax.ShapeDtypeStruct(a.shape, F32) for a in smalls[::2] for _ in range(3)],
        scratch_shapes=[
            vmem((width, groups * rows), BF16),
            vmem((groups * (rows - base), groups * base), BF16),
            vmem((width, groups * base), BF16),
            vmem((ahead, groups, base, outs), BF16),
            vmem((ahead, width, outs), F32),
            vmem((ahead, width, outs), BF16),
            vmem((behind, width, outs), F32),
            vmem((behind, width, outs), BF16),
            vmem((behind, width, outs), F32),
            vmem(maps_shape, BF16),
            vmem(cells.shape, BF16),
            vmem((2, 13, chans // 2, rows), F32),
            vmem((4, chans, 128), F32),
            vmem(acts.shape, BF16),
            dma((2,)),
            dma((ahead, 3)),
            dma((behind, 3)),
            dma,
            dma((14, 2)),
            dma((2,)),
        ],
        compiler_params=params(),
        name="weight_update",
    )(live, ft_all, gathered, moment, weight, cells, acts, sums, mixed, *smalls)


def fast_shards(
    mesh,
    input_maps,
    dense_weight,
    dense_bias,
    stitch_in,
    stitch_out,
    weight_moment,
    bias_moment,
    stitch_in_moment,
    stitch_out_moment,
    cotangent,
    live_rows,
):
    maps = jnp.transpose(input_maps, (1, 3, 2, 0))
    gathered, ft_all, acts, cells, sums, mixed = step_all(
        mesh, live_rows, maps, dense_weight, cotangent, dense_bias, stitch_out, stitch_in
    )
    (
        weight_grad,
        weight_next,
        weight_moment_next,
        maps_grad,
        activations,
        bias_grad,
        bias_next,
        bias_moment_next,
        stitch_in_grad,
        stitch_in_next,
        stitch_in_moment_next,
        stitch_out_grad,
        stitch_out_next,
        stitch_out_moment_next,
    ) = weight_update(
        live_rows,
        ft_all,
        gathered,
        weight_moment,
        dense_weight,
        maps.shape,
        cells,
        acts,
        sums,
        mixed,
        [dense_bias, bias_moment, stitch_in, stitch_in_moment, stitch_out, stitch_out_moment],
    )
    maps_grad = jnp.transpose(maps_grad, (3, 0, 2, 1))
    return (
        activations,
        maps_grad,
        weight_grad,
        bias_grad,
        stitch_in_grad,
        stitch_out_grad,
        weight_next,
        bias_next,
        stitch_in_next,
        stitch_out_next,
        weight_moment_next,
        bias_moment_next,
        stitch_in_moment_next,
        stitch_out_moment_next,
    )


def choose(mesh, *args):
    rows, _, chans, _ = args[0].shape
    outs = args[2].shape[1]
    shape = mesh.shape["batch"] == 4 and mesh.shape["mp"] == 8
    if shape and rows == 512 and outs == 512 and chans == 32:
        return fast_shards(mesh, *args)
    return shards(*args)


def solution(mesh):
    in_specs = (
        P("batch", None, "mp", None),
        P(None, "mp", None),
        P(None, "mp"),
        P(None, None, "mp"),
        P(None, None, "mp"),
        P(None, "mp", None),
        P(None, "mp"),
        P(None, None, "mp"),
        P(None, None, "mp"),
        P("batch", None, "mp"),
        P(),
    )
    out_specs = (
        P("batch", None, "mp"),
        P("batch", None, "mp", None),
        P(None, "mp", None),
        P(None, "mp"),
        P(None, None, "mp"),
        P(None, None, "mp"),
        P(None, "mp", None),
        P(None, "mp"),
        P(None, None, "mp"),
        P(None, None, "mp"),
        P(None, "mp", None),
        P(None, "mp"),
        P(None, None, "mp"),
        P(None, None, "mp"),
    )
    body = functools.partial(choose, mesh)
    return jax.shard_map(body, mesh=mesh, in_specs=in_specs, out_specs=out_specs, check_vma=False)
```

```python
import functools

import jax
import jax.numpy as jnp
from jax import lax
from jax.experimental import pallas as pl
from jax.experimental.pallas import tpu as pltpu
from jax.sharding import PartitionSpec as P

MESH = pl.DeviceIdType.MESH
BF16 = jnp.bfloat16
F32 = jnp.float32
VMEM_LIMIT = 60 * 1024 * 1024

MOMENTUM = 0.9
DENSE_RATE = 0.01
STITCH_RATE = 0.1


def pool_table():
    pixels = jnp.arange(169, dtype=jnp.int32)
    cells = jnp.arange(36, dtype=jnp.int32)
    pixel_row = (pixels // 13)[:, None]
    pixel_col = (pixels % 13)[:, None]
    cell_row = (cells // 6)[None, :]
    cell_col = (cells % 6)[None, :]
    inside = (
        (pixel_row >= 2 * cell_row)
        & (pixel_row <= 2 * cell_row + 2)
        & (pixel_col >= 2 * cell_col)
        & (pixel_col <= 2 * cell_col + 2)
    )
    return inside.astype(jnp.float32)


def gelu_tanh(value):
    return jax.nn.gelu(value, approximate=True)


def head(summed, cotangent, keep, dense_bias, stitch_out):
    hidden = summed + dense_bias[None]
    active, gelu_pull = jax.vjp(gelu_tanh, hidden)
    mixed = stitch_out[None, :, 0] * active[:, 0:1] + stitch_out[None, :, 1] * active[:, 1:2]
    activations = (mixed * keep[:, None, None]).astype(jnp.bfloat16)
    pulled = cotangent.astype(jnp.float32) * keep[:, None, None]
    stitch_out_grad = jnp.einsum("nio,njo->ijo", pulled, active, precision=lax.Precision.HIGHEST)
    active_grad = stitch_out[0][None] * pulled[:, 0:1] + stitch_out[1][None] * pulled[:, 1:2]
    hidden_grad = gelu_pull(active_grad)[0]
    bias_grad = jnp.sum(hidden_grad, axis=0)
    return (activations, hidden_grad.astype(jnp.bfloat16), bias_grad, stitch_out_grad)


def rows_layer(features, cotangent, keep, dense_weight, dense_bias, stitch_out):
    terms = jnp.einsum("ntk,tko->nto", features, dense_weight, preferred_element_type=jnp.float32)
    summed = lax.psum_scatter(terms, "mp", scatter_dimension=2, tiled=True)
    activations, summed_grad, bias_grad, stitch_out_grad = head(
        summed, cotangent, keep, dense_bias, stitch_out
    )
    piece = lax.all_gather(summed_grad, "mp", axis=2, tiled=True)
    inputs_grad = jnp.einsum(
        "nto,tko->ntk", piece, dense_weight, preferred_element_type=jnp.float32
    )
    update = jnp.einsum("ntk,nto->tko", features, piece, preferred_element_type=jnp.float32)
    weight_grad = update
    inputs_grad, weight_grad = (inputs_grad, weight_grad)
    return (activations, inputs_grad.astype(jnp.bfloat16), weight_grad, bias_grad, stitch_out_grad)


def dense_layer(features, cotangent, keep, dense_weight, dense_bias, stitch_out):
    return rows_layer(features, cotangent, keep, dense_weight, dense_bias, stitch_out)


def shards(
    input_maps,
    dense_weight,
    dense_bias,
    stitch_in,
    stitch_out,
    weight_moment,
    bias_moment,
    stitch_in_moment,
    stitch_out_moment,
    cotangent,
    live_rows,
):
    rows = input_maps.shape[0]
    chans = input_maps.shape[2]
    width = chans * 36
    group = lax.axis_index("batch")
    positions = jnp.arange(rows, dtype=jnp.int32)
    keep = (positions < live_rows[group]).astype(jnp.float32)
    table = pool_table()
    pooled = (
        jnp.einsum(
            "ntck,kq->ntcq",
            input_maps,
            table.astype(jnp.bfloat16),
            preferred_element_type=jnp.float32,
        )
        / 9.0
    )
    stitched = (
        stitch_in[None, :, 0, :, None] * pooled[:, 0:1]
        + stitch_in[None, :, 1, :, None] * pooled[:, 1:2]
    )
    features = stitched.reshape(rows, 2, width).astype(jnp.bfloat16)
    activations, inputs_grad, weight_grad, bias_grad, stitch_out_grad = dense_layer(
        features, cotangent, keep, dense_weight, dense_bias, stitch_out
    )
    stitched_grad = inputs_grad.astype(jnp.float32).reshape(rows, 2, chans, 36)
    stitch_in_grad = jnp.einsum(
        "nicq,njcq->ijc", stitched_grad, pooled, precision=lax.Precision.HIGHEST
    )
    pooled_grad = (
        stitch_in[0][None, :, :, None] * stitched_grad[:, 0:1]
        + stitch_in[1][None, :, :, None] * stitched_grad[:, 1:2]
    )
    maps_grad = jnp.einsum(
        "ntcq,kq->ntck", pooled_grad / 9.0, table, precision=lax.Precision.HIGHEST
    ).astype(jnp.bfloat16)
    weight_grad, bias_grad, stitch_in_grad, stitch_out_grad = lax.psum(
        (weight_grad, bias_grad, stitch_in_grad, stitch_out_grad), "batch"
    )
    weight_moment_next = MOMENTUM * weight_moment + weight_grad
    weight_next = (dense_weight.astype(jnp.float32) - DENSE_RATE * weight_moment_next).astype(
        jnp.bfloat16
    )
    bias_moment_next = MOMENTUM * bias_moment + bias_grad
    bias_next = dense_bias - DENSE_RATE * bias_moment_next
    stitch_in_moment_next = MOMENTUM * stitch_in_moment + stitch_in_grad
    stitch_in_next = stitch_in - STITCH_RATE * stitch_in_moment_next
    stitch_out_moment_next = MOMENTUM * stitch_out_moment + stitch_out_grad
    stitch_out_next = stitch_out - STITCH_RATE * stitch_out_moment_next
    return (
        activations,
        maps_grad,
        weight_grad,
        bias_grad,
        stitch_in_grad,
        stitch_out_grad,
        weight_next,
        bias_next,
        stitch_in_next,
        stitch_out_next,
        weight_moment_next,
        bias_moment_next,
        stitch_in_moment_next,
        stitch_out_moment_next,
    )


def params():
    return pltpu.CompilerParams(vmem_limit_bytes=VMEM_LIMIT)


def full(shape):
    return pl.BlockSpec(shape, lambda *_: (0,) * len(shape))


def fill_order(order, chans, inverse):
    size = order.shape[0]
    rows = lax.broadcasted_iota(jnp.int32, (size, size), 0)
    cols = lax.broadcasted_iota(jnp.int32, (size, size), 1)
    natural, cells = (cols, rows) if inverse else (rows, cols)
    shift = chans.bit_length() - 1
    hit = natural == 36 * (cells & (chans - 1)) + (cells >> shift)
    order[...] = jnp.where(hit, 1.0, 0.0).astype(BF16)


def spread_mix(mix_ref, wide):
    chans = wide.shape[1]
    rows = lax.broadcasted_iota(jnp.int32, (chans, chans), 0)
    cols = lax.broadcasted_iota(jnp.int32, (chans, chans), 1)
    for k in range(4):
        line = jnp.broadcast_to(mix_ref[k // 2, pl.ds(k % 2, 1), :], (chans, chans))
        column = jnp.sum(jnp.where(rows == cols, line, 0.0), axis=1, keepdims=True)
        wide[k] = jnp.broadcast_to(column, wide.shape[1:])


def pooled_row(maps_ref, tower, i, lanes):
    sums = None
    for dy in range(3):
        line = [maps_ref[tower, 26 * i + 13 * dy + x, :, lanes].astype(F32) for x in range(13)]
        cells = [line[2 * j] + line[2 * j + 1] + line[2 * j + 2] for j in range(6)]
        sums = cells if sums is None else [a + b for a, b in zip(sums, cells)]
    return [s * (1.0 / 9.0) for s in sums]


def gelu_parts(v):
    root = 0.7978845608028654
    square = v * v
    tanh = jnp.tanh(root * v * (1.0 + 0.044715 * square))
    half = 0.5 * (1.0 + tanh)
    slope = half + 0.5 * v * (1.0 - tanh * tanh) * root * (1.0 + 3.0 * 0.044715 * square)
    return v * half, slope


def neighbours():
    b, m = lax.axis_index("batch"), lax.axis_index("mp")
    columns = (b, b + 1 - 2 * (b % 2), b + 2 - 4 * (b // 2), 3 - b)
    return b, m, m // 2, m % 2, columns


def greet(columns, m, z, c, nz):
    b, bx, by, _ = columns
    sibling = m + 1 - 2 * c
    barrier = pltpu.get_barrier_semaphore()

    def signal(bb, mm):
        pl.semaphore_signal(barrier, inc=1, device_id=(bb, mm), device_id_type=MESH)

    signal(bx, m)
    signal(by, m)
    signal(b, sibling)
    pl.when(z > 0)(lambda: signal(b, m - 2))
    pl.when(z < nz - 1)(lambda: signal(b, m + 2))
    pl.semaphore_wait(barrier, 3 + jnp.where(z > 0, 1, 0) + jnp.where(z < nz - 1, 1, 0))


def remote(src, dst, send, recv, device):
    return pltpu.make_async_remote_copy(
        src_ref=src, dst_ref=dst, send_sem=send, recv_sem=recv, device_id=device, device_id_type=MESH
    )


def mix_row(chans, i, lanes, maps_ref, cells, total):
    pooled = [pooled_row(maps_ref, t, i, lanes) for t in range(2)]
    sums = [total[k] for k in range(4)]
    for j in range(6):
        span = pl.ds(pl.multiple_of((6 * i + j) * chans, chans), chans)
        for t in range(2):
            grad = cells[t, span, lanes].astype(F32)
            for s in range(2):
                sums[2 * t + s] += grad * pooled[s][j]
    for k in range(4):
        total[k] = sums[k]


def unpool_row(chans, i, channels, lanes, cells, above, wide, out_ref):
    start, count = channels
    rows = pl.ds(start, count)
    for t in range(2):
        mixed = []
        for j in range(6):
            span = pl.ds(pl.multiple_of((6 * i + j) * chans + start, count), count)
            first, second = (cells[k, span, lanes].astype(F32) for k in range(2))
            mixed.append((wide[t, rows] * first + wide[2 + t, rows] * second) * (1.0 / 9.0))
        for x in range(13):
            if x % 2 == 1 or x == 0:
                value = mixed[x // 2]
            elif x == 12:
                value = mixed[5]
            else:
                value = mixed[x // 2 - 1] + mixed[x // 2]
            out_ref[t, 26 * i + x, rows, lanes] = (value + above[t, x, :, lanes]).astype(BF16)
            out_ref[t, 26 * i + 13 + x, rows, lanes] = value.astype(BF16)
            above[t, x, :, lanes] = value


def shares(live_ref, groups, base):
    counts = [live_ref[k] for k in range(groups)]
    excess, free = [], []
    taken = given = 0
    for count in counts:
        excess.append(taken)
        free.append(given)
        taken = taken + jnp.maximum(count - base, 0)
        given = given + jnp.maximum(base - count, 0)
    return counts, excess, free


def picks(count, free, other, excess, base, spare, slots_in_lanes):
    shape = (spare, base) if slots_in_lanes else (base, spare)
    slot = lax.broadcasted_iota(jnp.int32, shape, 1 if slots_in_lanes else 0)
    row = lax.broadcasted_iota(jnp.int32, shape, 0 if slots_in_lanes else 1)
    hit = (slot - count + free == row + excess) & (slot >= count) & (row < other - base)
    return jnp.where(hit, 1.0, 0.0).astype(BF16)


def gather_phase(nz, cut, base, features_on, live_ref, pool_ref, pool, s_ref, acts_in, sums_ref, w_ref, maps_in, wide,
                 g_ref, acts_to, out_ref, total_ref, mixed_ref, sums_in, mix_in, sems,
                 keep_sem, out_sem, w_sem, col_sem, acts_sem,
                 acts_out, wbuf, col, grads, cells, order, mix_total):
    (line_send, line_recv, cross_send, cross_recv, half_send, half_recv, core_send, core_recv,
     small_send, small_recv, sums_mid, mix_mid) = sems
    b, m, z, c, columns = neighbours()
    rows = s_ref.shape[1]
    spans = (pl.ds(0, cut), pl.ds(cut, base - cut), pl.ds(base, rows - base))
    spare = rows - base
    sibling = m + 1 - 2 * c

    def small(kind, axis, src, dst):
        return remote(src, dst, small_send.at[kind, axis], small_recv.at[kind, axis], (columns[1 + axis], m))

    def place(p, r, zz):
        return g_ref.at[columns[r], 2 * zz + c, :, spans[p], :]

    def half(p, r, zz, t):
        return g_ref.at[columns[r], 2 * zz + c, t, spans[p], :]

    def line(k, zz, up, own=False):
        p, r = {0: (0, 0), 5: (2, 0)}.get(k, (1, k - 1))
        src = s_ref.at[:, spans[p], :] if own else place(p, r, zz)
        side = 1 if up else 0
        to = m + 2 if up else m - 2
        return remote(src, place(p, r, zz), line_send.at[side, k, zz], line_recv.at[k, zz], (b, to))

    def cross(p, axis, zz, own=False):
        src = s_ref.at[:, spans[p], :] if own else place(p, 0, zz)
        slot = zz if p == 0 else nz
        return remote(
            src, place(p, 0, zz), cross_send.at[axis, slot], cross_recv.at[axis, slot], (columns[1 + axis], m)
        )

    def cross_wait(p, axis, zz):
        slot = zz if p == 0 else nz
        here = place(p, 1 + axis, zz)
        remote(here, here, cross_send.at[axis, slot], cross_recv.at[axis, slot], (columns[1 + axis], m)).wait_recv()

    def diagonal(p, axis, zz):
        slot = zz if p == 0 else nz
        block = half(p, 2 - axis, zz, 1 - axis)
        return remote(block, block, half_send.at[axis, slot], half_recv.at[axis, slot], (columns[1 + axis], m))

    def diagonal_wait(p, axis, zz):
        slot = zz if p == 0 else nz
        block = half(p, 3, zz, 1 - axis)
        remote(block, block, half_send.at[axis, slot], half_recv.at[axis, slot], (columns[1 + axis], m)).wait_recv()

    def core(p, r, zz, own=False):
        src = s_ref.at[:, spans[p], :] if own else place(p, r, zz)
        return remote(src, place(p, r, zz), core_send.at[p, r, zz], core_recv.at[p, r, zz], (b, sibling))

    def core_wait(p, r, zz):
        block = g_ref.at[columns[r], 2 * zz + 1 - c, :, spans[p], :]
        remote(block, block, core_send.at[p, r, zz], core_recv.at[p, r, zz], (b, sibling)).wait_recv()

    def sides(d, body):
        if d == 0:
            body(z, None)
            return
        pl.when(z + d < nz)(lambda: body(z + d, False))
        pl.when(z - d >= 0)(lambda: body(z - d, True))

    def onward(k, zz, up):
        if up:
            pl.when(z < nz - 1)(lambda: line(k, zz, True).start())
        else:
            pl.when(z > 0)(lambda: line(k, zz, False).start())

    mine = pltpu.make_async_copy(s_ref, g_ref.at[b, m], keep_sem)

    def launch(k):
        pl.when(z < nz - 1)(lambda: line(k, z, True, True).start())
        pl.when(z > 0)(lambda: line(k, z, False, True).start())

    first_sums = small(0, 0, sums_ref, sums_in.at[0])
    first_sums.start()
    launch(5)
    core(2, 0, z, True).start()
    counts, excess, free = shares(live_ref, 4, base)
    live = live_ref[b]
    offset = 0
    for k in range(1, 4):
        offset = offset + jnp.where(b >= k, jnp.maximum(base - counts[k - 1], 0), 0)
    chosen = jnp.concatenate(
        [picks(live, offset, counts[k], excess[k], base, spare, False) for k in range(4)], axis=1
    )
    for axis in range(2):
        pool.end(axis)
    for t in range(2):
        moved = jnp.dot(chosen, pool_ref[t], preferred_element_type=F32)
        s_ref[t, :base, :] = (s_ref[t, :base, :].astype(F32) + moved).astype(BF16)
    cross(1, 0, z, True).start()
    cross(1, 1, z, True).start()
    launch(0)
    cross(0, 0, z, True).start()
    cross(0, 1, z, True).start()
    launch(1)
    core(0, 0, z, True).start()
    core(1, 0, z, True).start()
    mine.start()

    def pass_cross(p, zz):
        for axis in range(2):
            cross_wait(p, axis, zz)
            diagonal(p, 1 - axis, zz).start()
            core(p, 1 + axis, zz).start()

    def end_diagonal(p, zz):
        for axis in range(2):
            diagonal_wait(p, axis, zz)
        core(p, 3, zz).start()

    def arrive(zz, up):
        line(0, zz, up).wait_recv()
        onward(0, zz, up)
        cross(0, 0, zz).start()
        cross(0, 1, zz).start()
        core(0, 0, zz).start()
        for k, p in ((1, 1), (5, 2)):
            line(k, zz, up).wait_recv()
            onward(k, zz, up)
            core(p, 0, zz).start()

    def late(zz, up):
        for k in range(2, 5):
            line(k, zz, up).wait_recv()
            onward(k, zz, up)
            core(1, k - 1, zz).start()

    def spread():
        for k in range(2, 5):
            pl.when(z < nz - 1)(lambda k=k: line(k, z, True).start())
            pl.when(z > 0)(lambda k=k: line(k, z, False).start())

    def join_towers(k, carry):
        here = pl.ds(pl.multiple_of(k * 16, 16), 16)
        both = jnp.stack([acts_in[t, here, :].astype(F32) for t in range(2)], axis=1)
        acts_out[here, :, :] = both.astype(BF16)
        return carry

    pass_cross(1, z)
    lax.fori_loop(0, rows // 16, join_towers, 0)
    store_acts = pltpu.make_async_copy(acts_out, acts_to, acts_sem)
    store_acts.start()
    sides(1, arrive)
    pass_cross(0, z)
    end_diagonal(1, z)
    sides(2, arrive)
    width, chans = w_ref.shape[1], maps_in.shape[2]
    outs = s_ref.shape[2]
    piece = wbuf.shape[1]
    pieces = width // piece

    def weights(k):
        t, at = k // pieces, k % pieces * piece
        return pltpu.make_async_copy(w_ref.at[t, pl.ds(at, piece), :], wbuf.at[k % 2], w_sem.at[k % 2])

    def column(t, j):
        return pltpu.make_async_copy(
            g_ref.at[b, j, t], col.at[:, pl.ds(j * outs, outs)], col_sem.at[j]
        )

    def features_grad(t):
        for k in range(t * pieces, (t + 1) * pieces):
            if k + 1 < 2 * pieces:
                weights(k + 1).start()
            weights(k).wait()
            if k == t * pieces:
                for j in range(2 * nz):
                    column(t, j).wait()
            value = lax.dot_general(
                wbuf[k % 2], col[...], (((1,), (1,)), ((), ())), preferred_element_type=F32
            )
            lane = lax.broadcasted_iota(jnp.int32, value.shape, 1)
            grads[pl.ds(k % pieces * piece, piece), :] = jnp.where(lane < live, value, 0.0).astype(BF16)
        cells[t] = jnp.dot(order[...], grads[...], preferred_element_type=F32).astype(BF16)

    blocks = rows // 128

    def maps_back(step, carry):
        i = step // blocks
        lanes = pl.ds(pl.multiple_of(step % blocks * 128, 128), 128)
        mix_row(chans, i, lanes, maps_in, cells, mix_total)
        return carry

    weights(0).start()
    fill_order(order, chans, True)
    mix_total[...] = jnp.zeros_like(mix_total)
    first_sums.wait()
    sums_mid[...] = sums_ref[...] + sums_in[0]
    second_sums = small(0, 1, sums_mid, sums_in.at[1])
    second_sums.start()
    outer = (z == 0) | (z == nz - 1)
    inner = (z > 0) & (z < nz - 1)

    @pl.when(outer)
    def _():
        sides(1, lambda zz, up: pass_cross(0, zz))
        sides(3, arrive)
        spread()

    features_on(0)
    mine.wait()
    for zz in range(nz):
        for p in range(3):
            core_wait(p, 0, zz)
    for j in range(2 * nz):
        column(0, j).start()
    features_grad(0)
    for j in range(2 * nz):
        column(1, j).start()
    pl.when(inner)(spread)

    @pl.when(outer)
    def _():
        sides(1, late)
        sides(2, lambda zz, up: pass_cross(0, zz))

    features_grad(1)

    @pl.when(inner)
    def _():
        sides(1, lambda zz, up: pass_cross(0, zz))
        sides(1, late)

    end_diagonal(0, z)
    pl.when(inner)(lambda: sides(2, late))
    lax.fori_loop(0, 3 * blocks, maps_back, 0)
    pl.when(outer)(lambda: sides(2, late))
    sides(3, lambda zz, up: pass_cross(0, zz))
    lax.fori_loop(3 * blocks, 6 * blocks, maps_back, 0)
    store_cells = pltpu.make_async_copy(cells, out_ref, out_sem)
    store_cells.start()
    for k in range(4):
        mix_in[0, k] = jnp.broadcast_to(jnp.sum(mix_total[k], axis=1, keepdims=True), (chans, 128))
    first_mix = small(1, 0, mix_in.at[0], mix_in.at[1])
    first_mix.start()
    pl.when(inner)(lambda: sides(2, lambda zz, up: pass_cross(0, zz)))
    sides(1, lambda zz, up: end_diagonal(0, zz))
    first_mix.wait()
    mix_mid[...] = mix_in[0] + mix_in[1]
    second_mix = small(1, 1, mix_mid, mix_in.at[2])
    second_mix.start()
    sides(2, lambda zz, up: end_diagonal(0, zz))
    sides(3, late)
    sides(3, lambda zz, up: end_diagonal(0, zz))
    second_sums.wait()
    total_ref[...] = sums_mid[...] + sums_in[1]
    second_mix.wait()
    mixed_ref[...] = mix_mid[...] + mix_in[2]
    store_cells.wait()
    store_acts.wait()

    for zz in range(nz):
        for r in range(4):
            for p in range(2):
                if r > 0:
                    core_wait(p, r, zz)
                core(p, r, zz).wait_send()
        core(2, 0, zz).wait_send()
        for axis in range(2):
            cross(0, axis, zz).wait_send()
            diagonal(0, axis, zz).wait_send()
        for k in range(6):
            pl.when((z < nz - 1) & (z >= zz))(lambda k=k, zz=zz: line(k, zz, True).wait_send())
            pl.when((z > 0) & (z <= zz))(lambda k=k, zz=zz: line(k, zz, False).wait_send())
    for axis in range(2):
        cross(1, axis, z).wait_send()
        diagonal(1, axis, z).wait_send()


def head_rows(hidden, cot, keep, mix, act_ref, grad_ref, here, lanes):
    active, slope, pulled = [], [], []
    for t in range(2):
        value, rate = gelu_parts(hidden[t])
        active.append(value)
        slope.append(rate)
        pulled.append(cot[t] * keep)
    for i in range(2):
        mixed = mix[2 * i] * active[0] + mix[2 * i + 1] * active[1]
        act_ref[i, here, lanes] = (mixed * keep).astype(BF16)
    terms = [pulled[i] * active[j] for i in range(2) for j in range(2)]
    for j in range(2):
        grad = (mix[j] * pulled[0] + mix[2 + j] * pulled[1]) * slope[j]
        grad_ref[j, here, lanes] = grad.astype(BF16)
        terms.append(grad)
    return terms


def step_kernel(nz, cut, base, live_ref, maps_ref, w_ref, cot_raw, bias_ref, mix_ref, mix_in_ref,
                g_ref, fta_ref, acts_to, out_ref, total_ref, mixed_ref,
                maps_in, rb, inb, ft_ref, s_ref, acts_in, sums_ref, wide, sums_in, mix_in,
                maps_sem, swap_send, swap_recv, hop_send, hop_recv,
                feat_send, feat_recv, turn_send, turn_recv, feat_keep,
                pool_ref, pool_send, pool_recv, pool_turn_send, pool_turn_recv, *rest):
    b, m, z, c, columns = neighbours()
    sibling = m + 1 - 2 * c
    chans, rows = maps_in.shape[2:]
    width, outs = w_ref.shape[1], s_ref.shape[2]
    span = rows // 2

    def load_maps(h):
        lanes = pl.ds(h * span, span)
        return pltpu.make_async_copy(maps_ref.at[:, :, :, lanes], maps_in.at[:, :, :, lanes], maps_sem.at[h])

    for h in (1, 0):
        load_maps(h).start()

    def features(r, t, h):
        start = pl.multiple_of(columns[r] * rows + h * span, span)
        return fta_ref.at[t, :, pl.ds(start, span)]

    def mine(t, h):
        return pltpu.make_async_copy(ft_ref.at[t, :, pl.ds(h * span, span)], features(0, t, h), feat_keep.at[t, h])

    def feature(axis, t, h):
        return remote(ft_ref.at[t, :, pl.ds(h * span, span)], features(0, t, h), feat_send.at[axis, t, h],
                      feat_recv.at[axis, t, h], (columns[1 + axis], m))

    def feature_wait(axis, t, h):
        here = features(1 + axis, t, h)
        remote(here, here, feat_send.at[axis, t, h], feat_recv.at[axis, t, h], (columns[1 + axis], m)).wait_recv()

    def turn(axis, h):
        here = features(2 - axis, 1 - axis, h)
        return remote(here, here, turn_send.at[axis, h], turn_recv.at[axis, h], (columns[1 + axis], m))

    def turn_wait(axis, h):
        here = features(3, 1 - axis, h)
        remote(here, here, turn_send.at[axis, h], turn_recv.at[axis, h], (columns[1 + axis], m)).wait_recv()

    def features_on(h):
        for axis in range(2):
            feature_wait(1 - axis, 1 - axis, h)
            turn(axis, h).start()

    spare = rows - base

    class pool:
        def slot(r, t=None):
            start = pl.ds(pl.multiple_of(columns[r] * spare, spare), spare)
            return pool_ref.at[:, start, :] if t is None else pool_ref.at[t, start, :]

        def go(axis):
            return remote(s_ref.at[:, pl.ds(base, spare), :], pool.slot(0), pool_send.at[axis], pool_recv.at[axis],
                          (columns[1 + axis], m))

        def come(axis):
            here = pool.slot(1 + axis)
            remote(here, here, pool_send.at[axis], pool_recv.at[axis], (columns[1 + axis], m)).wait_recv()

        def turn(axis):
            here = pool.slot(2 - axis, 1 - axis)
            return remote(here, here, pool_turn_send.at[axis], pool_turn_recv.at[axis], (columns[1 + axis], m))

        def end(axis):
            here = pool.slot(3, 1 - axis)
            remote(here, here, pool_turn_send.at[axis], pool_turn_recv.at[axis], (columns[1 + axis], m)).wait_recv()

    def forward(cells, order, f_ref, cot_in, cot_ref, wbuf, pb, sb, cot_sem, w_sem):
        live = live_ref[b]
        near = jnp.where(z < nz // 2, 1, 0)

        def weights(i, t, own):
            zd = near * (nz - 1 - i) + (1 - near) * i
            j = 2 * zd + (c if own else 1 - c)
            lanes = pl.ds(pl.multiple_of(j * outs, outs), outs)
            k = 2 * t + own
            return pltpu.make_async_copy(w_ref.at[t, :, lanes], wbuf.at[k], w_sem.at[k])

        for t in range(2):
            for own in range(2):
                weights(0, t, own).start()
        load_cot = pltpu.make_async_copy(cot_raw, cot_in, cot_sem)
        load_cot.start()
        fill_order(order, chans, False)
        spread_mix(mix_in_ref, wide)
        greet(columns, m, z, c, nz)

        def swap(d, t, h):
            here = pl.ds(h * span, span)
            return remote(sb.at[d, t, here], rb.at[d, t, here], swap_send.at[d, t, h], swap_recv.at[d, t, h], (b, sibling))

        def hop(up, d, t, h):
            here = pl.ds(h * span, span)
            return remote(rb.at[d, t, here], inb.at[d + up, t, here], hop_send.at[d, t, h], hop_recv.at[up, d, t, h],
                          (b, m + 4 * up - 2))

        step = 64

        def relay(up, dm, t, h, first):
            zm = up * z + (1 - up) * (nz - 1 - z)
            d = up * dm + (1 - up) * (nz - 1 - dm)

            def go():
                swap(d, t, h).wait_recv()
                if not first:
                    hop(up, d, t, h).wait_recv()

                def add(k, carry):
                    here = pl.ds(pl.multiple_of(h * span + k * step, step), step)
                    value = pb[d, t, here, :] + rb[d, t, here, :].astype(F32)
                    if not first:
                        value += inb[d + up, t, here, :].astype(F32)
                    rb[d, t, here, :] = value.astype(BF16)
                    return carry

                lax.fori_loop(0, span // step, add, 0)
                hop(up, d, t, h).start()

            pl.when((zm == 0 if first else zm > 0) & (zm < dm))(go)

        narrow = span // 128

        def pool_maps(h):
            def pool_row(step, carry):
                i = step // narrow
                at = pl.multiple_of(step % narrow * 128, 128)
                lanes = pl.ds(pl.multiple_of(h * span + at, 128), 128)
                first = pooled_row(maps_in, 0, i, lanes)
                second = pooled_row(maps_in, 1, i, lanes)
                for t in range(2):
                    for j in range(6):
                        value = wide[2 * t] * first[j] + wide[2 * t + 1] * second[j]
                        start = pl.multiple_of((6 * i + j) * chans, chans)
                        cells[t, pl.ds(start, chans), pl.ds(at, 128)] = value.astype(BF16)
                return carry

            load_maps(h).wait()
            lax.fori_loop(0, 6 * narrow, pool_row, 0)
            for t in range(2):
                moved = jnp.dot(order[...], cells[t], preferred_element_type=F32).astype(BF16)
                ft_ref[t, :, pl.ds(h * span, span)] = moved
                f_ref[t, pl.ds(h * span, span), :] = moved.T
            for k in range(2):
                feature(0, k, h).start()
                feature(1, 1 - k, h).start()

        def produce(i, h):
            zd = near * (nz - 1 - i) + (1 - near) * i
            here = pl.ds(h * span, span)
            for t in range(2):
                for own in range(2):
                    if h == 1:
                        weights(i, t, own).wait()
                    part = jnp.dot(f_ref[t, here, :], wbuf[2 * t + own], preferred_element_type=F32)
                    if own:
                        pb[zd, t, here, :] = part
                    else:
                        sb[zd, t, here, :] = part.astype(BF16)
                        swap(zd, t, h).start()
                    if h == 0:
                        pl.when(i < nz - 1)(lambda t=t, own=own: weights(i + 1, t, own).start())
                relay(near, nz - 1 - i, t, h, True)

        for h in (1, 0):
            pool_maps(h)
            produce(0, h)

        def both(i, carry):
            for h in (1, 0):
                produce(i, h)
            return carry

        lax.fori_loop(1, nz, both, 0)

        features_on(1)
        for t in range(2):
            for h in range(2):
                mine(t, h).start()
        load_cot.wait()

        def part_towers(k, carry):
            here = pl.ds(pl.multiple_of(k * 16, 16), 16)
            both = cot_in[here, :, :].astype(F32)
            for t in range(2):
                cot_ref[t, here, :] = both[:, t, :].astype(BF16)
            return carry

        lax.fori_loop(0, rows // 16, part_towers, 0)
        for dm in range(nz - 1, 0, -1):
            for h in (1, 0):
                for t in range(2):
                    relay(near, dm, t, h, False)
                    relay(1 - near, dm, t, h, False)

        tile, high = 256, 16
        for h in (1, 0):
            for t in range(2):
                swap(z, t, h).wait_recv()
                pl.when(z > 0)(lambda t=t, h=h: hop(1, z, t, h).wait_recv())
                pl.when(z < nz - 1)(lambda t=t, h=h: hop(0, z, t, h).wait_recv())

                def gather(k, carry, t=t, h=h):
                    here = pl.ds(pl.multiple_of(h * span + k * step, step), step)
                    pb[z, t, here, :] += rb[z, t, here, :].astype(F32)
                    for up in range(2):
                        inside = z > 0 if up else z < nz - 1

                        @pl.when(inside)
                        def _(up=up):
                            pb[z, t, here, :] += inb[z + up, t, here, :].astype(F32)

                    return carry

                lax.fori_loop(0, span // step, gather, 0)
            if h == 0:
                for axis in range(2):
                    pool.come(axis)
                    pool.turn(1 - axis).start()
            for lane in range(outs // tile):
                lanes = pl.ds(lane * tile, tile)
                bias = [bias_ref[pl.ds(t, 1), lanes] for t in range(2)]
                mix = [mix_ref[k // 2, pl.ds(k % 2, 1), lanes] for k in range(4)]

                def block(k, totals, lanes=lanes, bias=bias, mix=mix):
                    here = pl.ds(pl.multiple_of(k * high, high), high)
                    hidden = [pb[z, t, here, lanes] + bias[t] for t in range(2)]
                    cot = [cot_ref[t, here, lanes].astype(F32) for t in range(2)]
                    place = k * high + lax.broadcasted_iota(jnp.int32, (high, tile), 0)
                    keep = jnp.where(place < live, 1.0, 0.0)
                    terms = head_rows(hidden, cot, keep, mix, acts_in, s_ref, here, lanes)
                    return tuple(a + v[:8] + v[8:] for a, v in zip(totals, terms))

                zero = jnp.zeros((8, tile), F32)
                count = span // high
                totals = lax.fori_loop(h * count, (h + 1) * count, block, (zero,) * 6)
                for k in range(6):
                    value = jnp.sum(totals[k], axis=0, keepdims=True)
                    sums_ref[k, :, lanes] = value if h == 1 else sums_ref[k, :, lanes] + value
            if h == 1:
                here = pl.ds(pl.multiple_of(b * spare, spare), spare)
                pool_ref[:, here, :] = s_ref[:, base:, :]
                for axis in range(2):
                    pool.go(axis).start()
        for d in range(nz):
            for t in range(2):
                for h in range(2):
                    swap(d, t, h).wait_send()
                    pl.when(z < d)(lambda d=d, t=t, h=h: hop(1, d, t, h).wait_send())
                    pl.when(z > d)(lambda d=d, t=t, h=h: hop(0, d, t, h).wait_send())

    vmem, dma = pltpu.VMEM, pltpu.SemaphoreType.DMA
    pl.run_scoped(
        forward,
        vmem((2, width, span), BF16),
        vmem((width, width), BF16),
        vmem((2, rows, width), BF16),
        vmem(cot_raw.shape, BF16),
        vmem((2, rows, outs), BF16),
        vmem((4, width, outs), BF16),
        vmem((nz, 2, rows, outs), F32),
        vmem((nz, 2, rows, outs), BF16),
        dma,
        dma((4,)),
    )
    pl.run_scoped(
        functools.partial(gather_phase, nz, cut, base, features_on, live_ref, pool_ref, pool, s_ref, acts_in, sums_ref, w_ref, maps_in, wide,
                          g_ref, acts_to, out_ref, total_ref, mixed_ref, sums_in, mix_in, rest),
        dma,
        dma,
        dma((2,)),
        dma((2 * nz,)),
        dma,
        vmem((rows, 2, outs), BF16),
        vmem((2, width // 3, 2 * nz * outs), BF16),
        vmem((rows, 2 * nz * outs), BF16),
        vmem((width, rows), BF16),
        vmem((2, width, rows), BF16),
        vmem((width, width), BF16),
        vmem((4, chans, 128), F32),
    )
    for h in range(2):
        for axis in range(2):
            feature_wait(axis, 1 - axis, h)
            turn_wait(axis, h)
            turn(axis, h).wait_send()
            for t in range(2):
                feature(axis, t, h).wait_send()
        for t in range(2):
            mine(t, h).wait()
    for axis in range(2):
        pool.go(axis).wait_send()
        pool.turn(axis).wait_send()


def step_all(mesh, live, maps, weight, cot, bias, mix, mix_in):
    groups, parts = mesh.shape["batch"], mesh.shape["mp"]
    nz = parts // 2
    chans, rows = maps.shape[2:]
    width = weight.shape[1]
    outs = weight.shape[2] // parts
    base = rows * 3 // 4
    cut = rows * 19 // 32
    vmem, dma = pltpu.VMEM, pltpu.SemaphoreType.DMA
    here = pl.BlockSpec(memory_space=pltpu.VMEM)
    far = pl.BlockSpec(memory_space=pl.ANY)
    sums = (6, 1, outs)
    return pl.pallas_call(
        functools.partial(step_kernel, nz, cut, base),
        in_specs=[pl.BlockSpec(memory_space=pltpu.SMEM), far, far, far, here, here, here],
        out_specs=[far, far, far, far, here, here],
        out_shape=[
            jax.ShapeDtypeStruct((groups, parts, 2, rows, outs), BF16),
            jax.ShapeDtypeStruct((2, width, groups * rows), BF16),
            jax.ShapeDtypeStruct((rows, 2, outs), BF16),
            jax.ShapeDtypeStruct((2, width, rows), BF16),
            jax.ShapeDtypeStruct(sums, F32),
            jax.ShapeDtypeStruct((4, chans, 128), F32),
        ],
        scratch_shapes=[
            vmem(maps.shape, BF16),
            vmem((nz, 2, rows, outs), BF16),
            vmem((nz + 1, 2, rows, outs), BF16),
            vmem((2, width, rows), BF16),
            vmem((2, rows, outs), BF16),
            vmem((2, rows, outs), BF16),
            vmem(sums, F32),
            vmem((4, chans, 128), F32),
            vmem((2,) + sums, F32),
            vmem((3, 4, chans, 128), F32),
            dma((2,)),
            dma((nz, 2, 2)),
            dma((nz, 2, 2)),
            dma((nz, 2, 2)),
            dma((2, nz, 2, 2)),
            dma((2, 2, 2)),
            dma((2, 2, 2)),
            dma((2, 2)),
            dma((2, 2)),
            dma((2, 2)),
            vmem((2, groups * (rows - base), outs), BF16),
            dma((2,)),
            dma((2,)),
            dma((2,)),
            dma((2,)),
            dma((2, 6, nz)),
            dma((6, nz)),
            dma((2, nz + 1)),
            dma((2, nz + 1)),
            dma((2, nz + 1)),
            dma((2, nz + 1)),
            dma((3, 4, nz)),
            dma((3, 4, nz)),
            dma((2, 2)),
            dma((2, 2)),
            vmem(sums, F32),
            vmem((4, chans, 128), F32),
        ],
        compiler_params=pltpu.CompilerParams(
            collective_id=0, has_side_effects=True, vmem_limit_bytes=VMEM_LIMIT
        ),
        name="step_all",
    )(live, maps, weight, cot, bias, mix, mix_in)


def turn_mix(wide):
    chans = wide.shape[0]
    rows = lax.broadcasted_iota(jnp.int32, (chans, chans), 0)
    cols = lax.broadcasted_iota(jnp.int32, (chans, chans), 1)
    return jnp.sum(jnp.where(rows == cols, wide[:, :chans], 0.0), axis=0, keepdims=True)


def update_kernel(base, live_ref, ft_ref, s_ref, m_ref, w_ref, cells_ref, acts_ref, sums_ref, mixed_ref,
                  bias_ref, bias_m_ref, in_ref, in_m_ref, out_ref, out_m_ref,
                  grad_to, next_to, moment_to, maps_to, acts_to, bias_g, bias_n, bias_mn,
                  in_g, in_n, in_mn, out_g, out_n, out_mn,
                  raw, chosen, ft, s_in, m_in, w_in, g_out, n_out, m_out, maps_out, cells, above, wide, acts_mid,
                  ft_sem, in_sem, out_sem, cells_sem, maps_sem, acts_sem):
    groups, parts, _, rows, tile = s_ref.shape
    spare = rows - base
    steps, ahead, behind = 2 * parts, s_in.shape[0], g_out.shape[0]
    chans, lanes_all = maps_out.shape[2:]
    share = chans // 2

    def loads(i):
        t, j, slot = i // parts, i % parts, i % ahead
        lanes = pl.ds(pl.multiple_of(j * tile, tile), tile)
        return [
            pltpu.make_async_copy(s_ref.at[:, j, t, pl.ds(0, base), :], s_in.at[slot], in_sem.at[slot, 0]),
            pltpu.make_async_copy(m_ref.at[t, :, lanes], m_in.at[slot], in_sem.at[slot, 1]),
            pltpu.make_async_copy(w_ref.at[t, :, lanes], w_in.at[slot], in_sem.at[slot, 2]),
        ]

    def stores(i):
        t, j, slot = i // parts, i % parts, i % behind
        lanes = pl.ds(pl.multiple_of(j * tile, tile), tile)
        return [
            pltpu.make_async_copy(g_out.at[slot], grad_to.at[t, :, lanes], out_sem.at[slot, 0]),
            pltpu.make_async_copy(m_out.at[slot], moment_to.at[t, :, lanes], out_sem.at[slot, 1]),
            pltpu.make_async_copy(n_out.at[slot], next_to.at[t, :, lanes], out_sem.at[slot, 2]),
        ]

    def each(copies, act):
        for copy in copies:
            act(copy)

    start, wait = lambda copy: copy.start(), lambda copy: copy.wait()

    load_cells = pltpu.make_async_copy(cells_ref, cells, cells_sem)

    def maps_store(unit, t):
        rows_two = pl.ds(pl.multiple_of(unit % 6 * 26, 26), 26)
        block = (t, rows_two, pl.ds(pl.multiple_of(unit // 6 * share, share), share))
        return pltpu.make_async_copy(maps_out.at[block], maps_to.at[block], maps_sem.at[unit, t])

    def last_store(half, t):
        block = (t, pl.ds(156, 13), pl.ds(half * share, share))
        return pltpu.make_async_copy(maps_out.at[block], maps_to.at[block], maps_sem.at[12 + half, t])

    def unpool(unit):
        i = unit % 6
        start = pl.multiple_of(unit // 6 * share, share)

        @pl.when(i == 0)
        def _():
            above[...] = jnp.zeros_like(above)

        def lane_block(k, carry):
            lanes = pl.ds(pl.multiple_of(k * 128, 128), 128)
            unpool_row(chans, i, (start, share), lanes, cells, above, wide, maps_out)
            return carry

        lax.fori_loop(0, lanes_all // 128, lane_block, 0)
        for t in range(2):
            maps_store(unit, t).start()
        for half in range(2):

            @pl.when(unit == 6 * half + 5)
            def _(half=half):
                for t in range(2):
                    for x in range(13):
                        maps_out[t, 156 + x, pl.ds(half * share, share)] = above[t, x].astype(BF16)
                    last_store(half, t).start()

    load_acts = pltpu.make_async_copy(acts_ref, acts_mid, acts_sem.at[0])
    store_acts = pltpu.make_async_copy(acts_mid, acts_to, acts_sem.at[1])
    towers = [pltpu.make_async_copy(ft_ref.at[t], raw, ft_sem.at[t]) for t in range(2)]
    towers[0].start()
    each(loads(0), start)
    counts, excess, free = shares(live_ref, groups, base)
    for k in range(groups):
        for n in range(groups):
            chosen[pl.ds(n * spare, spare), pl.ds(k * base, base)] = picks(
                counts[k], free[k], counts[n], excess[n], base, spare, True
            )

    def pack(t):
        last = jnp.concatenate([raw[:, k * rows + base : (k + 1) * rows] for k in range(groups)], axis=1)
        for k in range(groups):
            lanes = pl.ds(k * base, base)
            moved = jnp.dot(last, chosen[:, lanes], preferred_element_type=F32)
            lane = lax.broadcasted_iota(jnp.int32, moved.shape, 1)
            kept = raw[:, k * rows : k * rows + base].astype(F32)
            ft[:, lanes] = jnp.where(lane < counts[k], kept, moved).astype(BF16)

    def step(grad, value, moment, rate, at, grad_ref, next_ref, moment_ref):
        after = MOMENTUM * moment[at] + grad
        grad_ref[at] = grad
        moment_ref[at] = after
        next_ref[at] = value[at] - rate * after

    for i in range(2):
        at = (pl.ds(i, 1), slice(None))
        step(sums_ref[4 + i], bias_ref, bias_m_ref, DENSE_RATE, at, bias_g, bias_n, bias_mn)
        for j in range(2):
            at = (i, pl.ds(j, 1), slice(None))
            step(sums_ref[2 * i + j], out_ref, out_m_ref, STITCH_RATE, at, out_g, out_n, out_mn)
            step(turn_mix(mixed_ref[2 * i + j]), in_ref, in_m_ref, STITCH_RATE, at, in_g, in_n, in_mn)

    spread_mix(in_ref, wide)
    towers[0].wait()
    for i in range(1, ahead):
        each(loads(i), start)
    pack(0)
    towers[1].start()

    def body(i, carry):
        slot, to = i % ahead, i % behind

        pl.when(i == 0)(load_acts.start)
        pl.when(i == 0)(load_cells.start)
        pl.when(i == 2)(load_cells.wait)
        pl.when((i >= 2) & (i < 14))(lambda: unpool(i - 2))

        @pl.when(i == ahead)
        def _():
            load_acts.wait()
            store_acts.start()


        @pl.when(i == parts)
        def _():
            towers[1].wait()
            pack(1)

        each(loads(i), wait)
        pl.when(i >= behind)(lambda: each(stores(i - behind), wait))
        grad = jnp.dot(
            ft[...], s_in[slot].reshape(groups * base, tile), preferred_element_type=F32
        )
        g_out[to] = grad
        moment = MOMENTUM * m_in[slot] + grad
        m_out[to] = moment
        n_out[to] = (w_in[slot].astype(F32) - DENSE_RATE * moment).astype(BF16)
        each(stores(i), start)
        pl.when(i + ahead < steps)(lambda: each(loads(i + ahead), start))
        return carry

    lax.fori_loop(0, steps, body, 0)
    for k in range(behind):
        each(stores(steps - behind + k), wait)
    for t in range(2):
        for unit in range(12):
            maps_store(unit, t).wait()
        for half in range(2):
            last_store(half, t).wait()
    store_acts.wait()


def weight_update(live, ft_all, gathered, moment, weight, maps_shape, cells, acts, sums, mixed, smalls):
    groups, parts, _, rows, outs = gathered.shape
    width = weight.shape[1]
    chans = maps_shape[2]
    base = rows * 3 // 4
    here = pl.BlockSpec(memory_space=pltpu.VMEM)
    far = pl.BlockSpec(memory_space=pl.ANY)
    ahead, behind = 3, 2
    vmem, dma = pltpu.VMEM, pltpu.SemaphoreType.DMA
    return pl.pallas_call(
        functools.partial(update_kernel, base),
        in_specs=[pl.BlockSpec(memory_space=pltpu.SMEM)] + [far] * 6 + [here] * (2 + len(smalls)),
        out_specs=[far] * 5 + [here] * 9,
        out_shape=[
            jax.ShapeDtypeStruct(moment.shape, F32),
            jax.ShapeDtypeStruct(moment.shape, BF16),
            jax.ShapeDtypeStruct(moment.shape, F32),
            jax.ShapeDtypeStruct(maps_shape, BF16),
            jax.ShapeDtypeStruct(acts.shape, BF16),
        ]
        + [jax.ShapeDtypeStruct(a.shape, F32) for a in smalls[::2] for _ in range(3)],
        scratch_shapes=[
            vmem((width, groups * rows), BF16),
            vmem((groups * (rows - base), groups * base), BF16),
            vmem((width, groups * base), BF16),
            vmem((ahead, groups, base, outs), BF16),
            vmem((ahead, width, outs), F32),
            vmem((ahead, width, outs), BF16),
            vmem((behind, width, outs), F32),
            vmem((behind, width, outs), BF16),
            vmem((behind, width, outs), F32),
            vmem(maps_shape, BF16),
            vmem(cells.shape, BF16),
            vmem((2, 13, chans // 2, rows), F32),
            vmem((4, chans, 128), F32),
            vmem(acts.shape, BF16),
            dma((2,)),
            dma((ahead, 3)),
            dma((behind, 3)),
            dma,
            dma((14, 2)),
            dma((2,)),
        ],
        compiler_params=params(),
        name="weight_update",
    )(live, ft_all, gathered, moment, weight, cells, acts, sums, mixed, *smalls)


def fast_shards(
    mesh,
    input_maps,
    dense_weight,
    dense_bias,
    stitch_in,
    stitch_out,
    weight_moment,
    bias_moment,
    stitch_in_moment,
    stitch_out_moment,
    cotangent,
    live_rows,
):
    maps = jnp.transpose(input_maps, (1, 3, 2, 0))
    gathered, ft_all, acts, cells, sums, mixed = step_all(
        mesh, live_rows, maps, dense_weight, cotangent, dense_bias, stitch_out, stitch_in
    )
    (
        weight_grad,
        weight_next,
        weight_moment_next,
        maps_grad,
        activations,
        bias_grad,
        bias_next,
        bias_moment_next,
        stitch_in_grad,
        stitch_in_next,
        stitch_in_moment_next,
        stitch_out_grad,
        stitch_out_next,
        stitch_out_moment_next,
    ) = weight_update(
        live_rows,
        ft_all,
        gathered,
        weight_moment,
        dense_weight,
        maps.shape,
        cells,
        acts,
        sums,
        mixed,
        [dense_bias, bias_moment, stitch_in, stitch_in_moment, stitch_out, stitch_out_moment],
    )
    maps_grad = jnp.transpose(maps_grad, (3, 0, 2, 1))
    return (
        activations,
        maps_grad,
        weight_grad,
        bias_grad,
        stitch_in_grad,
        stitch_out_grad,
        weight_next,
        bias_next,
        stitch_in_next,
        stitch_out_next,
        weight_moment_next,
        bias_moment_next,
        stitch_in_moment_next,
        stitch_out_moment_next,
    )


def choose(mesh, *args):
    rows, _, chans, _ = args[0].shape
    outs = args[2].shape[1]
    shape = mesh.shape["batch"] == 4 and mesh.shape["mp"] == 8
    if shape and rows == 512 and outs == 512 and chans == 32:
        return fast_shards(mesh, *args)
    return shards(*args)


def solution(mesh):
    in_specs = (
        P("batch", None, "mp", None),
        P(None, "mp", None),
        P(None, "mp"),
        P(None, None, "mp"),
        P(None, None, "mp"),
        P(None, "mp", None),
        P(None, "mp"),
        P(None, None, "mp"),
        P(None, None, "mp"),
        P("batch", None, "mp"),
        P(),
    )
    out_specs = (
        P("batch", None, "mp"),
        P("batch", None, "mp", None),
        P(None, "mp", None),
        P(None, "mp"),
        P(None, None, "mp"),
        P(None, None, "mp"),
        P(None, "mp", None),
        P(None, "mp"),
        P(None, None, "mp"),
        P(None, None, "mp"),
        P(None, "mp", None),
        P(None, "mp"),
        P(None, None, "mp"),
        P(None, None, "mp"),
    )
    body = functools.partial(choose, mesh)
    return jax.shard_map(body, mesh=mesh, in_specs=in_specs, out_specs=out_specs, check_vma=False)
```

```python
import functools

import jax
import jax.numpy as jnp
from jax import lax
from jax.experimental import pallas as pl
from jax.experimental.pallas import tpu as pltpu
from jax.sharding import PartitionSpec as P

MESH = pl.DeviceIdType.MESH
BF16 = jnp.bfloat16
F32 = jnp.float32
VMEM_LIMIT = 60 * 1024 * 1024

MOMENTUM = 0.9
DENSE_RATE = 0.01
STITCH_RATE = 0.1


def pool_table():
    pixels = jnp.arange(169, dtype=jnp.int32)
    cells = jnp.arange(36, dtype=jnp.int32)
    pixel_row = (pixels // 13)[:, None]
    pixel_col = (pixels % 13)[:, None]
    cell_row = (cells // 6)[None, :]
    cell_col = (cells % 6)[None, :]
    inside = (
        (pixel_row >= 2 * cell_row)
        & (pixel_row <= 2 * cell_row + 2)
        & (pixel_col >= 2 * cell_col)
        & (pixel_col <= 2 * cell_col + 2)
    )
    return inside.astype(jnp.float32)


def gelu_tanh(value):
    return jax.nn.gelu(value, approximate=True)


def head(summed, cotangent, keep, dense_bias, stitch_out):
    hidden = summed + dense_bias[None]
    active, gelu_pull = jax.vjp(gelu_tanh, hidden)
    mixed = stitch_out[None, :, 0] * active[:, 0:1] + stitch_out[None, :, 1] * active[:, 1:2]
    activations = (mixed * keep[:, None, None]).astype(jnp.bfloat16)
    pulled = cotangent.astype(jnp.float32) * keep[:, None, None]
    stitch_out_grad = jnp.einsum("nio,njo->ijo", pulled, active, precision=lax.Precision.HIGHEST)
    active_grad = stitch_out[0][None] * pulled[:, 0:1] + stitch_out[1][None] * pulled[:, 1:2]
    hidden_grad = gelu_pull(active_grad)[0]
    bias_grad = jnp.sum(hidden_grad, axis=0)
    return (activations, hidden_grad.astype(jnp.bfloat16), bias_grad, stitch_out_grad)


def rows_layer(features, cotangent, keep, dense_weight, dense_bias, stitch_out):
    terms = jnp.einsum("ntk,tko->nto", features, dense_weight, preferred_element_type=jnp.float32)
    summed = lax.psum_scatter(terms, "mp", scatter_dimension=2, tiled=True)
    activations, summed_grad, bias_grad, stitch_out_grad = head(
        summed, cotangent, keep, dense_bias, stitch_out
    )
    piece = lax.all_gather(summed_grad, "mp", axis=2, tiled=True)
    inputs_grad = jnp.einsum(
        "nto,tko->ntk", piece, dense_weight, preferred_element_type=jnp.float32
    )
    update = jnp.einsum("ntk,nto->tko", features, piece, preferred_element_type=jnp.float32)
    weight_grad = update
    inputs_grad, weight_grad = (inputs_grad, weight_grad)
    return (activations, inputs_grad.astype(jnp.bfloat16), weight_grad, bias_grad, stitch_out_grad)


def dense_layer(features, cotangent, keep, dense_weight, dense_bias, stitch_out):
    return rows_layer(features, cotangent, keep, dense_weight, dense_bias, stitch_out)


def shards(
    input_maps,
    dense_weight,
    dense_bias,
    stitch_in,
    stitch_out,
    weight_moment,
    bias_moment,
    stitch_in_moment,
    stitch_out_moment,
    cotangent,
    live_rows,
):
    rows = input_maps.shape[0]
    chans = input_maps.shape[2]
    width = chans * 36
    group = lax.axis_index("batch")
    positions = jnp.arange(rows, dtype=jnp.int32)
    keep = (positions < live_rows[group]).astype(jnp.float32)
    table = pool_table()
    pooled = (
        jnp.einsum(
            "ntck,kq->ntcq",
            input_maps,
            table.astype(jnp.bfloat16),
            preferred_element_type=jnp.float32,
        )
        / 9.0
    )
    stitched = (
        stitch_in[None, :, 0, :, None] * pooled[:, 0:1]
        + stitch_in[None, :, 1, :, None] * pooled[:, 1:2]
    )
    features = stitched.reshape(rows, 2, width).astype(jnp.bfloat16)
    activations, inputs_grad, weight_grad, bias_grad, stitch_out_grad = dense_layer(
        features, cotangent, keep, dense_weight, dense_bias, stitch_out
    )
    stitched_grad = inputs_grad.astype(jnp.float32).reshape(rows, 2, chans, 36)
    stitch_in_grad = jnp.einsum(
        "nicq,njcq->ijc", stitched_grad, pooled, precision=lax.Precision.HIGHEST
    )
    pooled_grad = (
        stitch_in[0][None, :, :, None] * stitched_grad[:, 0:1]
        + stitch_in[1][None, :, :, None] * stitched_grad[:, 1:2]
    )
    maps_grad = jnp.einsum(
        "ntcq,kq->ntck", pooled_grad / 9.0, table, precision=lax.Precision.HIGHEST
    ).astype(jnp.bfloat16)
    weight_grad, bias_grad, stitch_in_grad, stitch_out_grad = lax.psum(
        (weight_grad, bias_grad, stitch_in_grad, stitch_out_grad), "batch"
    )
    weight_moment_next = MOMENTUM * weight_moment + weight_grad
    weight_next = (dense_weight.astype(jnp.float32) - DENSE_RATE * weight_moment_next).astype(
        jnp.bfloat16
    )
    bias_moment_next = MOMENTUM * bias_moment + bias_grad
    bias_next = dense_bias - DENSE_RATE * bias_moment_next
    stitch_in_moment_next = MOMENTUM * stitch_in_moment + stitch_in_grad
    stitch_in_next = stitch_in - STITCH_RATE * stitch_in_moment_next
    stitch_out_moment_next = MOMENTUM * stitch_out_moment + stitch_out_grad
    stitch_out_next = stitch_out - STITCH_RATE * stitch_out_moment_next
    return (
        activations,
        maps_grad,
        weight_grad,
        bias_grad,
        stitch_in_grad,
        stitch_out_grad,
        weight_next,
        bias_next,
        stitch_in_next,
        stitch_out_next,
        weight_moment_next,
        bias_moment_next,
        stitch_in_moment_next,
        stitch_out_moment_next,
    )


def params():
    return pltpu.CompilerParams(vmem_limit_bytes=VMEM_LIMIT)


def full(shape):
    return pl.BlockSpec(shape, lambda *_: (0,) * len(shape))


def fill_order(order, chans, inverse):
    size = order.shape[0]
    rows = lax.broadcasted_iota(jnp.int32, (size, size), 0)
    cols = lax.broadcasted_iota(jnp.int32, (size, size), 1)
    natural, cells = (cols, rows) if inverse else (rows, cols)
    shift = chans.bit_length() - 1
    hit = natural == 36 * (cells & (chans - 1)) + (cells >> shift)
    order[...] = jnp.where(hit, 1.0, 0.0).astype(BF16)


def spread_mix(mix_ref, wide):
    chans = wide.shape[1]
    rows = lax.broadcasted_iota(jnp.int32, (chans, chans), 0)
    cols = lax.broadcasted_iota(jnp.int32, (chans, chans), 1)
    for k in range(4):
        line = jnp.broadcast_to(mix_ref[k // 2, pl.ds(k % 2, 1), :], (chans, chans))
        column = jnp.sum(jnp.where(rows == cols, line, 0.0), axis=1, keepdims=True)
        wide[k] = jnp.broadcast_to(column, wide.shape[1:])


def pooled_row(maps_ref, tower, i, lanes):
    sums = None
    for dy in range(3):
        line = [maps_ref[tower, 26 * i + 13 * dy + x, :, lanes].astype(F32) for x in range(13)]
        cells = [line[2 * j] + line[2 * j + 1] + line[2 * j + 2] for j in range(6)]
        sums = cells if sums is None else [a + b for a, b in zip(sums, cells)]
    return [s * (1.0 / 9.0) for s in sums]


def gelu_parts(v):
    root = 0.7978845608028654
    square = v * v
    tanh = jnp.tanh(root * v * (1.0 + 0.044715 * square))
    half = 0.5 * (1.0 + tanh)
    slope = half + 0.5 * v * (1.0 - tanh * tanh) * root * (1.0 + 3.0 * 0.044715 * square)
    return v * half, slope


def neighbours():
    b, m = lax.axis_index("batch"), lax.axis_index("mp")
    columns = (b, b + 1 - 2 * (b % 2), b + 2 - 4 * (b // 2), 3 - b)
    return b, m, m // 2, m % 2, columns


def greet(columns, m, z, c, nz):
    b, bx, by, _ = columns
    sibling = m + 1 - 2 * c
    barrier = pltpu.get_barrier_semaphore()

    def signal(bb, mm):
        pl.semaphore_signal(barrier, inc=1, device_id=(bb, mm), device_id_type=MESH)

    signal(bx, m)
    signal(by, m)
    signal(b, sibling)
    pl.when(z > 0)(lambda: signal(b, m - 2))
    pl.when(z < nz - 1)(lambda: signal(b, m + 2))
    pl.semaphore_wait(barrier, 3 + jnp.where(z > 0, 1, 0) + jnp.where(z < nz - 1, 1, 0))


def remote(src, dst, send, recv, device):
    return pltpu.make_async_remote_copy(
        src_ref=src, dst_ref=dst, send_sem=send, recv_sem=recv, device_id=device, device_id_type=MESH
    )


def mix_row(chans, i, lanes, maps_ref, cells, total):
    pooled = [pooled_row(maps_ref, t, i, lanes) for t in range(2)]
    sums = [total[k] for k in range(4)]
    for j in range(6):
        span = pl.ds(pl.multiple_of((6 * i + j) * chans, chans), chans)
        for t in range(2):
            grad = cells[t, span, lanes].astype(F32)
            for s in range(2):
                sums[2 * t + s] += grad * pooled[s][j]
    for k in range(4):
        total[k] = sums[k]


def unpool_row(chans, i, channels, lanes, cells, above, wide, out_ref):
    start, count = channels
    rows = pl.ds(start, count)
    for t in range(2):
        mixed = []
        for j in range(6):
            span = pl.ds(pl.multiple_of((6 * i + j) * chans + start, count), count)
            first, second = (cells[k, span, lanes].astype(F32) for k in range(2))
            mixed.append((wide[t, rows] * first + wide[2 + t, rows] * second) * (1.0 / 9.0))
        for x in range(13):
            if x % 2 == 1 or x == 0:
                value = mixed[x // 2]
            elif x == 12:
                value = mixed[5]
            else:
                value = mixed[x // 2 - 1] + mixed[x // 2]
            out_ref[t, 26 * i + x, rows, lanes] = (value + above[t, x, :, lanes]).astype(BF16)
            out_ref[t, 26 * i + 13 + x, rows, lanes] = value.astype(BF16)
            above[t, x, :, lanes] = value


def shares(live_ref, groups, base):
    counts = [live_ref[k] for k in range(groups)]
    excess, free = [], []
    taken = given = 0
    for count in counts:
        excess.append(taken)
        free.append(given)
        taken = taken + jnp.maximum(count - base, 0)
        given = given + jnp.maximum(base - count, 0)
    return counts, excess, free


def picks(count, free, other, excess, base, spare, slots_in_lanes):
    shape = (spare, base) if slots_in_lanes else (base, spare)
    slot = lax.broadcasted_iota(jnp.int32, shape, 1 if slots_in_lanes else 0)
    row = lax.broadcasted_iota(jnp.int32, shape, 0 if slots_in_lanes else 1)
    hit = (slot - count + free == row + excess) & (slot >= count) & (row < other - base)
    return jnp.where(hit, 1.0, 0.0).astype(BF16)


def gather_phase(nz, cut, base, features_on, live_ref, pool_ref, pool, s_ref, acts_in, sums_ref, w_ref, maps_in, wide,
                 g_ref, acts_to, out_ref, total_ref, mixed_ref, sums_in, mix_in, sems,
                 keep_sem, out_sem, w_sem, col_sem, acts_sem,
                 acts_out, wbuf, col, grads, cells, order, mix_total):
    (line_send, line_recv, cross_send, cross_recv, half_send, half_recv, core_send, core_recv,
     small_send, small_recv, sums_mid, mix_mid) = sems
    b, m, z, c, columns = neighbours()
    rows = s_ref.shape[1]
    spans = (pl.ds(0, cut), pl.ds(cut, base - cut), pl.ds(base, rows - base))
    spare = rows - base
    sibling = m + 1 - 2 * c

    def small(kind, axis, src, dst):
        return remote(src, dst, small_send.at[kind, axis], small_recv.at[kind, axis], (columns[1 + axis], m))

    def place(p, r, zz):
        return g_ref.at[columns[r], 2 * zz + c, :, spans[p], :]

    def half(p, r, zz, t):
        return g_ref.at[columns[r], 2 * zz + c, t, spans[p], :]

    def line(k, zz, up, own=False):
        p, r = {0: (0, 0), 5: (2, 0)}.get(k, (1, k - 1))
        src = s_ref.at[:, spans[p], :] if own else place(p, r, zz)
        side = 1 if up else 0
        to = m + 2 if up else m - 2
        return remote(src, place(p, r, zz), line_send.at[side, k, zz], line_recv.at[k, zz], (b, to))

    def cross(p, axis, zz, own=False):
        src = s_ref.at[:, spans[p], :] if own else place(p, 0, zz)
        slot = zz if p == 0 else nz
        return remote(
            src, place(p, 0, zz), cross_send.at[axis, slot], cross_recv.at[axis, slot], (columns[1 + axis], m)
        )

    def cross_wait(p, axis, zz):
        slot = zz if p == 0 else nz
        here = place(p, 1 + axis, zz)
        remote(here, here, cross_send.at[axis, slot], cross_recv.at[axis, slot], (columns[1 + axis], m)).wait_recv()

    def diagonal(p, axis, zz):
        slot = zz if p == 0 else nz
        block = half(p, 2 - axis, zz, 1 - axis)
        return remote(block, block, half_send.at[axis, slot], half_recv.at[axis, slot], (columns[1 + axis], m))

    def diagonal_wait(p, axis, zz):
        slot = zz if p == 0 else nz
        block = half(p, 3, zz, 1 - axis)
        remote(block, block, half_send.at[axis, slot], half_recv.at[axis, slot], (columns[1 + axis], m)).wait_recv()

    def core(p, r, zz, own=False):
        src = s_ref.at[:, spans[p], :] if own else place(p, r, zz)
        return remote(src, place(p, r, zz), core_send.at[p, r, zz], core_recv.at[p, r, zz], (b, sibling))

    def core_wait(p, r, zz):
        block = g_ref.at[columns[r], 2 * zz + 1 - c, :, spans[p], :]
        remote(block, block, core_send.at[p, r, zz], core_recv.at[p, r, zz], (b, sibling)).wait_recv()

    def sides(d, body):
        if d == 0:
            body(z, None)
            return
        pl.when(z + d < nz)(lambda: body(z + d, False))
        pl.when(z - d >= 0)(lambda: body(z - d, True))

    def onward(k, zz, up):
        if up:
            pl.when(z < nz - 1)(lambda: line(k, zz, True).start())
        else:
            pl.when(z > 0)(lambda: line(k, zz, False).start())

    mine = pltpu.make_async_copy(s_ref, g_ref.at[b, m], keep_sem)

    def launch(k):
        pl.when(z < nz - 1)(lambda: line(k, z, True, True).start())
        pl.when(z > 0)(lambda: line(k, z, False, True).start())

    first_sums = small(0, 0, sums_ref, sums_in.at[0])
    first_sums.start()
    launch(5)
    core(2, 0, z, True).start()
    counts, excess, free = shares(live_ref, 4, base)
    live = live_ref[b]
    offset = 0
    for k in range(1, 4):
        offset = offset + jnp.where(b >= k, jnp.maximum(base - counts[k - 1], 0), 0)
    chosen = jnp.concatenate(
        [picks(live, offset, counts[k], excess[k], base, spare, False) for k in range(4)], axis=1
    )
    for axis in range(2):
        pool.end(axis)
    for t in range(2):
        moved = jnp.dot(chosen, pool_ref[t], preferred_element_type=F32)
        s_ref[t, :base, :] = (s_ref[t, :base, :].astype(F32) + moved).astype(BF16)
    cross(1, 0, z, True).start()
    cross(1, 1, z, True).start()
    launch(0)
    cross(0, 0, z, True).start()
    cross(0, 1, z, True).start()
    launch(1)
    core(0, 0, z, True).start()
    core(1, 0, z, True).start()
    mine.start()

    def pass_cross(p, zz):
        for axis in range(2):
            cross_wait(p, axis, zz)
            diagonal(p, 1 - axis, zz).start()
            core(p, 1 + axis, zz).start()

    def end_diagonal(p, zz):
        for axis in range(2):
            diagonal_wait(p, axis, zz)
        core(p, 3, zz).start()

    def arrive(zz, up):
        line(0, zz, up).wait_recv()
        onward(0, zz, up)
        cross(0, 0, zz).start()
        cross(0, 1, zz).start()
        core(0, 0, zz).start()
        for k, p in ((1, 1), (5, 2)):
            line(k, zz, up).wait_recv()
            onward(k, zz, up)
            core(p, 0, zz).start()

    def late(zz, up):
        for k in range(2, 5):
            line(k, zz, up).wait_recv()
            onward(k, zz, up)
            core(1, k - 1, zz).start()

    def spread():
        for k in range(2, 5):
            pl.when(z < nz - 1)(lambda k=k: line(k, z, True).start())
            pl.when(z > 0)(lambda k=k: line(k, z, False).start())

    def join_towers(k, carry):
        here = pl.ds(pl.multiple_of(k * 16, 16), 16)
        both = jnp.stack([acts_in[t, here, :].astype(F32) for t in range(2)], axis=1)
        acts_out[here, :, :] = both.astype(BF16)
        return carry

    pass_cross(1, z)
    lax.fori_loop(0, rows // 16, join_towers, 0)
    store_acts = pltpu.make_async_copy(acts_out, acts_to, acts_sem)
    store_acts.start()
    sides(1, arrive)
    pass_cross(0, z)
    end_diagonal(1, z)
    sides(2, arrive)
    width, chans = w_ref.shape[1], maps_in.shape[2]
    outs = s_ref.shape[2]
    piece = wbuf.shape[1]
    pieces = width // piece

    def weights(k):
        t, at = k // pieces, k % pieces * piece
        return pltpu.make_async_copy(w_ref.at[t, pl.ds(at, piece), :], wbuf.at[k % 2], w_sem.at[k % 2])

    def column(t, j):
        return pltpu.make_async_copy(
            g_ref.at[b, j, t], col.at[:, pl.ds(j * outs, outs)], col_sem.at[j]
        )

    def features_grad(t):
        for k in range(t * pieces, (t + 1) * pieces):
            if k + 1 < 2 * pieces:
                weights(k + 1).start()
            weights(k).wait()
            if k == t * pieces:
                for j in range(2 * nz):
                    column(t, j).wait()
            value = lax.dot_general(
                wbuf[k % 2], col[...], (((1,), (1,)), ((), ())), preferred_element_type=F32
            )
            lane = lax.broadcasted_iota(jnp.int32, value.shape, 1)
            grads[pl.ds(k % pieces * piece, piece), :] = jnp.where(lane < live, value, 0.0).astype(BF16)
        cells[t] = jnp.dot(order[...], grads[...], preferred_element_type=F32).astype(BF16)

    blocks = rows // 128

    def maps_back(step, carry):
        i = step // blocks
        lanes = pl.ds(pl.multiple_of(step % blocks * 128, 128), 128)
        mix_row(chans, i, lanes, maps_in, cells, mix_total)
        return carry

    weights(0).start()
    fill_order(order, chans, True)
    mix_total[...] = jnp.zeros_like(mix_total)
    first_sums.wait()
    sums_mid[...] = sums_ref[...] + sums_in[0]
    second_sums = small(0, 1, sums_mid, sums_in.at[1])
    second_sums.start()
    outer = (z == 0) | (z == nz - 1)
    inner = (z > 0) & (z < nz - 1)

    @pl.when(outer)
    def _():
        sides(1, lambda zz, up: pass_cross(0, zz))
        sides(3, arrive)
        spread()

    features_on(0)
    mine.wait()
    for zz in range(nz):
        for p in range(3):
            core_wait(p, 0, zz)
    for j in range(2 * nz):
        column(0, j).start()
    pl.when(inner)(spread)
    features_grad(0)
    for j in range(2 * nz):
        column(1, j).start()

    @pl.when(outer)
    def _():
        sides(1, late)
        sides(2, lambda zz, up: pass_cross(0, zz))

    features_grad(1)

    @pl.when(inner)
    def _():
        sides(1, lambda zz, up: pass_cross(0, zz))
        sides(1, late)

    end_diagonal(0, z)
    pl.when(inner)(lambda: sides(2, late))
    lax.fori_loop(0, 3 * blocks, maps_back, 0)
    pl.when(outer)(lambda: sides(2, late))
    sides(3, lambda zz, up: pass_cross(0, zz))
    lax.fori_loop(3 * blocks, 6 * blocks, maps_back, 0)
    store_cells = pltpu.make_async_copy(cells, out_ref, out_sem)
    store_cells.start()
    for k in range(4):
        mix_in[0, k] = jnp.broadcast_to(jnp.sum(mix_total[k], axis=1, keepdims=True), (chans, 128))
    first_mix = small(1, 0, mix_in.at[0], mix_in.at[1])
    first_mix.start()
    pl.when(inner)(lambda: sides(2, lambda zz, up: pass_cross(0, zz)))
    sides(1, lambda zz, up: end_diagonal(0, zz))
    first_mix.wait()
    mix_mid[...] = mix_in[0] + mix_in[1]
    second_mix = small(1, 1, mix_mid, mix_in.at[2])
    second_mix.start()
    sides(2, lambda zz, up: end_diagonal(0, zz))
    sides(3, late)
    sides(3, lambda zz, up: end_diagonal(0, zz))
    second_sums.wait()
    total_ref[...] = sums_mid[...] + sums_in[1]
    second_mix.wait()
    mixed_ref[...] = mix_mid[...] + mix_in[2]
    store_cells.wait()
    store_acts.wait()

    for zz in range(nz):
        for r in range(4):
            for p in range(2):
                if r > 0:
                    core_wait(p, r, zz)
                core(p, r, zz).wait_send()
        core(2, 0, zz).wait_send()
        for axis in range(2):
            cross(0, axis, zz).wait_send()
            diagonal(0, axis, zz).wait_send()
        for k in range(6):
            pl.when((z < nz - 1) & (z >= zz))(lambda k=k, zz=zz: line(k, zz, True).wait_send())
            pl.when((z > 0) & (z <= zz))(lambda k=k, zz=zz: line(k, zz, False).wait_send())
    for axis in range(2):
        cross(1, axis, z).wait_send()
        diagonal(1, axis, z).wait_send()


def head_rows(hidden, cot, keep, mix, act_ref, grad_ref, here, lanes):
    active, slope, pulled = [], [], []
    for t in range(2):
        value, rate = gelu_parts(hidden[t])
        active.append(value)
        slope.append(rate)
        pulled.append(cot[t] * keep)
    for i in range(2):
        mixed = mix[2 * i] * active[0] + mix[2 * i + 1] * active[1]
        act_ref[i, here, lanes] = (mixed * keep).astype(BF16)
    terms = [pulled[i] * active[j] for i in range(2) for j in range(2)]
    for j in range(2):
        grad = (mix[j] * pulled[0] + mix[2 + j] * pulled[1]) * slope[j]
        grad_ref[j, here, lanes] = grad.astype(BF16)
        terms.append(grad)
    return terms


def step_kernel(nz, cut, base, live_ref, maps_ref, w_ref, cot_raw, bias_ref, mix_ref, mix_in_ref,
                g_ref, fta_ref, acts_to, out_ref, total_ref, mixed_ref,
                maps_in, rb, inb, ft_ref, s_ref, acts_in, sums_ref, wide, sums_in, mix_in,
                maps_sem, swap_send, swap_recv, hop_send, hop_recv,
                feat_send, feat_recv, turn_send, turn_recv, feat_keep,
                pool_ref, pool_send, pool_recv, pool_turn_send, pool_turn_recv, *rest):
    b, m, z, c, columns = neighbours()
    sibling = m + 1 - 2 * c
    chans, rows = maps_in.shape[2:]
    width, outs = w_ref.shape[1], s_ref.shape[2]
    span = rows // 2

    def load_maps(h):
        lanes = pl.ds(h * span, span)
        return pltpu.make_async_copy(maps_ref.at[:, :, :, lanes], maps_in.at[:, :, :, lanes], maps_sem.at[h])

    for h in (1, 0):
        load_maps(h).start()

    def features(r, t, h):
        start = pl.multiple_of(columns[r] * rows + h * span, span)
        return fta_ref.at[t, :, pl.ds(start, span)]

    def mine(t, h):
        return pltpu.make_async_copy(ft_ref.at[t, :, pl.ds(h * span, span)], features(0, t, h), feat_keep.at[t, h])

    def feature(axis, t, h):
        return remote(ft_ref.at[t, :, pl.ds(h * span, span)], features(0, t, h), feat_send.at[axis, t, h],
                      feat_recv.at[axis, t, h], (columns[1 + axis], m))

    def feature_wait(axis, t, h):
        here = features(1 + axis, t, h)
        remote(here, here, feat_send.at[axis, t, h], feat_recv.at[axis, t, h], (columns[1 + axis], m)).wait_recv()

    def turn(axis, h):
        here = features(2 - axis, 1 - axis, h)
        return remote(here, here, turn_send.at[axis, h], turn_recv.at[axis, h], (columns[1 + axis], m))

    def turn_wait(axis, h):
        here = features(3, 1 - axis, h)
        remote(here, here, turn_send.at[axis, h], turn_recv.at[axis, h], (columns[1 + axis], m)).wait_recv()

    def features_on(h):
        for axis in range(2):
            feature_wait(1 - axis, 1 - axis, h)
            turn(axis, h).start()

    spare = rows - base

    class pool:
        def slot(r, t=None):
            start = pl.ds(pl.multiple_of(columns[r] * spare, spare), spare)
            return pool_ref.at[:, start, :] if t is None else pool_ref.at[t, start, :]

        def go(axis):
            return remote(s_ref.at[:, pl.ds(base, spare), :], pool.slot(0), pool_send.at[axis], pool_recv.at[axis],
                          (columns[1 + axis], m))

        def come(axis):
            here = pool.slot(1 + axis)
            remote(here, here, pool_send.at[axis], pool_recv.at[axis], (columns[1 + axis], m)).wait_recv()

        def turn(axis):
            here = pool.slot(2 - axis, 1 - axis)
            return remote(here, here, pool_turn_send.at[axis], pool_turn_recv.at[axis], (columns[1 + axis], m))

        def end(axis):
            here = pool.slot(3, 1 - axis)
            remote(here, here, pool_turn_send.at[axis], pool_turn_recv.at[axis], (columns[1 + axis], m)).wait_recv()

    def forward(cells, order, f_ref, cot_in, cot_ref, wbuf, pb, sb, cot_sem, w_sem):
        live = live_ref[b]
        near = jnp.where(z < nz // 2, 1, 0)

        def weights(i, t, own):
            zd = near * (nz - 1 - i) + (1 - near) * i
            j = 2 * zd + (c if own else 1 - c)
            lanes = pl.ds(pl.multiple_of(j * outs, outs), outs)
            k = 2 * t + own
            return pltpu.make_async_copy(w_ref.at[t, :, lanes], wbuf.at[k], w_sem.at[k])

        for t in range(2):
            for own in range(2):
                weights(0, t, own).start()
        load_cot = pltpu.make_async_copy(cot_raw, cot_in, cot_sem)
        load_cot.start()
        fill_order(order, chans, False)
        spread_mix(mix_in_ref, wide)
        greet(columns, m, z, c, nz)

        def swap(d, t, h):
            here = pl.ds(h * span, span)
            return remote(sb.at[d, t, here], rb.at[d, t, here], swap_send.at[d, t, h], swap_recv.at[d, t, h], (b, sibling))

        def hop(up, d, t, h):
            here = pl.ds(h * span, span)
            return remote(rb.at[d, t, here], inb.at[d + up, t, here], hop_send.at[d, t, h], hop_recv.at[up, d, t, h],
                          (b, m + 4 * up - 2))

        step = 64

        def relay(up, dm, t, h, first):
            zm = up * z + (1 - up) * (nz - 1 - z)
            d = up * dm + (1 - up) * (nz - 1 - dm)

            def go():
                swap(d, t, h).wait_recv()
                if not first:
                    hop(up, d, t, h).wait_recv()

                def add(k, carry):
                    here = pl.ds(pl.multiple_of(h * span + k * step, step), step)
                    value = pb[d, t, here, :] + rb[d, t, here, :].astype(F32)
                    if not first:
                        value += inb[d + up, t, here, :].astype(F32)
                    rb[d, t, here, :] = value.astype(BF16)
                    return carry

                lax.fori_loop(0, span // step, add, 0)
                hop(up, d, t, h).start()

            pl.when((zm == 0 if first else zm > 0) & (zm < dm))(go)

        narrow = span // 128

        def pool_maps(h):
            def pool_row(step, carry):
                i = step // narrow
                at = pl.multiple_of(step % narrow * 128, 128)
                lanes = pl.ds(pl.multiple_of(h * span + at, 128), 128)
                first = pooled_row(maps_in, 0, i, lanes)
                second = pooled_row(maps_in, 1, i, lanes)
                for t in range(2):
                    for j in range(6):
                        value = wide[2 * t] * first[j] + wide[2 * t + 1] * second[j]
                        start = pl.multiple_of((6 * i + j) * chans, chans)
                        cells[t, pl.ds(start, chans), pl.ds(at, 128)] = value.astype(BF16)
                return carry

            load_maps(h).wait()
            lax.fori_loop(0, 6 * narrow, pool_row, 0)
            for t in range(2):
                moved = jnp.dot(order[...], cells[t], preferred_element_type=F32).astype(BF16)
                ft_ref[t, :, pl.ds(h * span, span)] = moved
                f_ref[t, pl.ds(h * span, span), :] = moved.T
            for k in range(2):
                feature(0, k, h).start()
                feature(1, 1 - k, h).start()

        def produce(i, h):
            zd = near * (nz - 1 - i) + (1 - near) * i
            here = pl.ds(h * span, span)
            for t in range(2):
                for own in range(2):
                    if h == 1:
                        weights(i, t, own).wait()
                    part = jnp.dot(f_ref[t, here, :], wbuf[2 * t + own], preferred_element_type=F32)
                    if own:
                        pb[zd, t, here, :] = part
                    else:
                        sb[zd, t, here, :] = part.astype(BF16)
                        swap(zd, t, h).start()
                    if h == 0:
                        pl.when(i < nz - 1)(lambda t=t, own=own: weights(i + 1, t, own).start())
                relay(near, nz - 1 - i, t, h, True)

        for h in (1, 0):
            pool_maps(h)
            produce(0, h)

        def both(i, carry):
            for h in (1, 0):
                produce(i, h)
            return carry

        lax.fori_loop(1, nz, both, 0)

        features_on(1)
        for t in range(2):
            for h in range(2):
                mine(t, h).start()
        load_cot.wait()

        def part_towers(k, carry):
            here = pl.ds(pl.multiple_of(k * 16, 16), 16)
            both = cot_in[here, :, :].astype(F32)
            for t in range(2):
                cot_ref[t, here, :] = both[:, t, :].astype(BF16)
            return carry

        lax.fori_loop(0, rows // 16, part_towers, 0)
        for dm in range(nz - 1, 0, -1):
            for h in (1, 0):
                for t in range(2):
                    relay(near, dm, t, h, False)
                    relay(1 - near, dm, t, h, False)

        tile, high = 256, 16
        for h in (1, 0):
            for t in range(2):
                swap(z, t, h).wait_recv()
                pl.when(z > 0)(lambda t=t, h=h: hop(1, z, t, h).wait_recv())
                pl.when(z < nz - 1)(lambda t=t, h=h: hop(0, z, t, h).wait_recv())

                def gather(k, carry, t=t, h=h):
                    here = pl.ds(pl.multiple_of(h * span + k * step, step), step)
                    pb[z, t, here, :] += rb[z, t, here, :].astype(F32)
                    for up in range(2):
                        inside = z > 0 if up else z < nz - 1

                        @pl.when(inside)
                        def _(up=up):
                            pb[z, t, here, :] += inb[z + up, t, here, :].astype(F32)

                    return carry

                lax.fori_loop(0, span // step, gather, 0)
            if h == 0:
                for axis in range(2):
                    pool.come(axis)
                    pool.turn(1 - axis).start()
            for lane in range(outs // tile):
                lanes = pl.ds(lane * tile, tile)
                bias = [bias_ref[pl.ds(t, 1), lanes] for t in range(2)]
                mix = [mix_ref[k // 2, pl.ds(k % 2, 1), lanes] for k in range(4)]

                def block(k, totals, lanes=lanes, bias=bias, mix=mix):
                    here = pl.ds(pl.multiple_of(k * high, high), high)
                    hidden = [pb[z, t, here, lanes] + bias[t] for t in range(2)]
                    cot = [cot_ref[t, here, lanes].astype(F32) for t in range(2)]
                    place = k * high + lax.broadcasted_iota(jnp.int32, (high, tile), 0)
                    keep = jnp.where(place < live, 1.0, 0.0)
                    terms = head_rows(hidden, cot, keep, mix, acts_in, s_ref, here, lanes)
                    return tuple(a + v[:8] + v[8:] for a, v in zip(totals, terms))

                zero = jnp.zeros((8, tile), F32)
                count = span // high
                totals = lax.fori_loop(h * count, (h + 1) * count, block, (zero,) * 6)
                for k in range(6):
                    value = jnp.sum(totals[k], axis=0, keepdims=True)
                    sums_ref[k, :, lanes] = value if h == 1 else sums_ref[k, :, lanes] + value
            if h == 1:
                here = pl.ds(pl.multiple_of(b * spare, spare), spare)
                pool_ref[:, here, :] = s_ref[:, base:, :]
                for axis in range(2):
                    pool.go(axis).start()
        for d in range(nz):
            for t in range(2):
                for h in range(2):
                    swap(d, t, h).wait_send()
                    pl.when(z < d)(lambda d=d, t=t, h=h: hop(1, d, t, h).wait_send())
                    pl.when(z > d)(lambda d=d, t=t, h=h: hop(0, d, t, h).wait_send())

    vmem, dma = pltpu.VMEM, pltpu.SemaphoreType.DMA
    pl.run_scoped(
        forward,
        vmem((2, width, span), BF16),
        vmem((width, width), BF16),
        vmem((2, rows, width), BF16),
        vmem(cot_raw.shape, BF16),
        vmem((2, rows, outs), BF16),
        vmem((4, width, outs), BF16),
        vmem((nz, 2, rows, outs), F32),
        vmem((nz, 2, rows, outs), BF16),
        dma,
        dma((4,)),
    )
    pl.run_scoped(
        functools.partial(gather_phase, nz, cut, base, features_on, live_ref, pool_ref, pool, s_ref, acts_in, sums_ref, w_ref, maps_in, wide,
                          g_ref, acts_to, out_ref, total_ref, mixed_ref, sums_in, mix_in, rest),
        dma,
        dma,
        dma((2,)),
        dma((2 * nz,)),
        dma,
        vmem((rows, 2, outs), BF16),
        vmem((2, width // 3, 2 * nz * outs), BF16),
        vmem((rows, 2 * nz * outs), BF16),
        vmem((width, rows), BF16),
        vmem((2, width, rows), BF16),
        vmem((width, width), BF16),
        vmem((4, chans, 128), F32),
    )
    for h in range(2):
        for axis in range(2):
            feature_wait(axis, 1 - axis, h)
            turn_wait(axis, h)
            turn(axis, h).wait_send()
            for t in range(2):
                feature(axis, t, h).wait_send()
        for t in range(2):
            mine(t, h).wait()
    for axis in range(2):
        pool.go(axis).wait_send()
        pool.turn(axis).wait_send()


def step_all(mesh, live, maps, weight, cot, bias, mix, mix_in):
    groups, parts = mesh.shape["batch"], mesh.shape["mp"]
    nz = parts // 2
    chans, rows = maps.shape[2:]
    width = weight.shape[1]
    outs = weight.shape[2] // parts
    base = rows * 3 // 4
    cut = rows * 19 // 32
    vmem, dma = pltpu.VMEM, pltpu.SemaphoreType.DMA
    here = pl.BlockSpec(memory_space=pltpu.VMEM)
    far = pl.BlockSpec(memory_space=pl.ANY)
    sums = (6, 1, outs)
    return pl.pallas_call(
        functools.partial(step_kernel, nz, cut, base),
        in_specs=[pl.BlockSpec(memory_space=pltpu.SMEM), far, far, far, here, here, here],
        out_specs=[far, far, far, far, here, here],
        out_shape=[
            jax.ShapeDtypeStruct((groups, parts, 2, rows, outs), BF16),
            jax.ShapeDtypeStruct((2, width, groups * rows), BF16),
            jax.ShapeDtypeStruct((rows, 2, outs), BF16),
            jax.ShapeDtypeStruct((2, width, rows), BF16),
            jax.ShapeDtypeStruct(sums, F32),
            jax.ShapeDtypeStruct((4, chans, 128), F32),
        ],
        scratch_shapes=[
            vmem(maps.shape, BF16),
            vmem((nz, 2, rows, outs), BF16),
            vmem((nz + 1, 2, rows, outs), BF16),
            vmem((2, width, rows), BF16),
            vmem((2, rows, outs), BF16),
            vmem((2, rows, outs), BF16),
            vmem(sums, F32),
            vmem((4, chans, 128), F32),
            vmem((2,) + sums, F32),
            vmem((3, 4, chans, 128), F32),
            dma((2,)),
            dma((nz, 2, 2)),
            dma((nz, 2, 2)),
            dma((nz, 2, 2)),
            dma((2, nz, 2, 2)),
            dma((2, 2, 2)),
            dma((2, 2, 2)),
            dma((2, 2)),
            dma((2, 2)),
            dma((2, 2)),
            vmem((2, groups * (rows - base), outs), BF16),
            dma((2,)),
            dma((2,)),
            dma((2,)),
            dma((2,)),
            dma((2, 6, nz)),
            dma((6, nz)),
            dma((2, nz + 1)),
            dma((2, nz + 1)),
            dma((2, nz + 1)),
            dma((2, nz + 1)),
            dma((3, 4, nz)),
            dma((3, 4, nz)),
            dma((2, 2)),
            dma((2, 2)),
            vmem(sums, F32),
            vmem((4, chans, 128), F32),
        ],
        compiler_params=pltpu.CompilerParams(
            collective_id=0, has_side_effects=True, vmem_limit_bytes=VMEM_LIMIT
        ),
        name="step_all",
    )(live, maps, weight, cot, bias, mix, mix_in)


def turn_mix(wide):
    chans = wide.shape[0]
    rows = lax.broadcasted_iota(jnp.int32, (chans, chans), 0)
    cols = lax.broadcasted_iota(jnp.int32, (chans, chans), 1)
    return jnp.sum(jnp.where(rows == cols, wide[:, :chans], 0.0), axis=0, keepdims=True)


def update_kernel(base, live_ref, ft_ref, s_ref, m_ref, w_ref, cells_ref, acts_ref, sums_ref, mixed_ref,
                  bias_ref, bias_m_ref, in_ref, in_m_ref, out_ref, out_m_ref,
                  grad_to, next_to, moment_to, maps_to, acts_to, bias_g, bias_n, bias_mn,
                  in_g, in_n, in_mn, out_g, out_n, out_mn,
                  raw, chosen, ft, s_in, m_in, w_in, g_out, n_out, m_out, maps_out, cells, above, wide, acts_mid,
                  ft_sem, in_sem, out_sem, cells_sem, maps_sem, acts_sem):
    groups, parts, _, rows, tile = s_ref.shape
    spare = rows - base
    steps, ahead, behind = 2 * parts, s_in.shape[0], g_out.shape[0]
    chans, lanes_all = maps_out.shape[2:]
    share = chans // 2

    def loads(i):
        t, j, slot = i // parts, i % parts, i % ahead
        lanes = pl.ds(pl.multiple_of(j * tile, tile), tile)
        return [
            pltpu.make_async_copy(s_ref.at[:, j, t, pl.ds(0, base), :], s_in.at[slot], in_sem.at[slot, 0]),
            pltpu.make_async_copy(m_ref.at[t, :, lanes], m_in.at[slot], in_sem.at[slot, 1]),
            pltpu.make_async_copy(w_ref.at[t, :, lanes], w_in.at[slot], in_sem.at[slot, 2]),
        ]

    def stores(i):
        t, j, slot = i // parts, i % parts, i % behind
        lanes = pl.ds(pl.multiple_of(j * tile, tile), tile)
        return [
            pltpu.make_async_copy(g_out.at[slot], grad_to.at[t, :, lanes], out_sem.at[slot, 0]),
            pltpu.make_async_copy(m_out.at[slot], moment_to.at[t, :, lanes], out_sem.at[slot, 1]),
            pltpu.make_async_copy(n_out.at[slot], next_to.at[t, :, lanes], out_sem.at[slot, 2]),
        ]

    def each(copies, act):
        for copy in copies:
            act(copy)

    start, wait = lambda copy: copy.start(), lambda copy: copy.wait()

    load_cells = pltpu.make_async_copy(cells_ref, cells, cells_sem)

    def maps_store(unit, t):
        rows_two = pl.ds(pl.multiple_of(unit % 6 * 26, 26), 26)
        block = (t, rows_two, pl.ds(pl.multiple_of(unit // 6 * share, share), share))
        return pltpu.make_async_copy(maps_out.at[block], maps_to.at[block], maps_sem.at[unit, t])

    def last_store(half, t):
        block = (t, pl.ds(156, 13), pl.ds(half * share, share))
        return pltpu.make_async_copy(maps_out.at[block], maps_to.at[block], maps_sem.at[12 + half, t])

    def unpool(unit):
        i = unit % 6
        start = pl.multiple_of(unit // 6 * share, share)

        @pl.when(i == 0)
        def _():
            above[...] = jnp.zeros_like(above)

        def lane_block(k, carry):
            lanes = pl.ds(pl.multiple_of(k * 128, 128), 128)
            unpool_row(chans, i, (start, share), lanes, cells, above, wide, maps_out)
            return carry

        lax.fori_loop(0, lanes_all // 128, lane_block, 0)
        for t in range(2):
            maps_store(unit, t).start()
        for half in range(2):

            @pl.when(unit == 6 * half + 5)
            def _(half=half):
                for t in range(2):
                    for x in range(13):
                        maps_out[t, 156 + x, pl.ds(half * share, share)] = above[t, x].astype(BF16)
                    last_store(half, t).start()

    load_acts = pltpu.make_async_copy(acts_ref, acts_mid, acts_sem.at[0])
    store_acts = pltpu.make_async_copy(acts_mid, acts_to, acts_sem.at[1])
    towers = [pltpu.make_async_copy(ft_ref.at[t], raw, ft_sem.at[t]) for t in range(2)]
    towers[0].start()
    each(loads(0), start)
    counts, excess, free = shares(live_ref, groups, base)
    for k in range(groups):
        for n in range(groups):
            chosen[pl.ds(n * spare, spare), pl.ds(k * base, base)] = picks(
                counts[k], free[k], counts[n], excess[n], base, spare, True
            )

    def pack(t):
        last = jnp.concatenate([raw[:, k * rows + base : (k + 1) * rows] for k in range(groups)], axis=1)
        for k in range(groups):
            lanes = pl.ds(k * base, base)
            moved = jnp.dot(last, chosen[:, lanes], preferred_element_type=F32)
            lane = lax.broadcasted_iota(jnp.int32, moved.shape, 1)
            kept = raw[:, k * rows : k * rows + base].astype(F32)
            ft[:, lanes] = jnp.where(lane < counts[k], kept, moved).astype(BF16)

    def step(grad, value, moment, rate, at, grad_ref, next_ref, moment_ref):
        after = MOMENTUM * moment[at] + grad
        grad_ref[at] = grad
        moment_ref[at] = after
        next_ref[at] = value[at] - rate * after

    for i in range(2):
        at = (pl.ds(i, 1), slice(None))
        step(sums_ref[4 + i], bias_ref, bias_m_ref, DENSE_RATE, at, bias_g, bias_n, bias_mn)
        for j in range(2):
            at = (i, pl.ds(j, 1), slice(None))
            step(sums_ref[2 * i + j], out_ref, out_m_ref, STITCH_RATE, at, out_g, out_n, out_mn)
            step(turn_mix(mixed_ref[2 * i + j]), in_ref, in_m_ref, STITCH_RATE, at, in_g, in_n, in_mn)

    spread_mix(in_ref, wide)
    towers[0].wait()
    for i in range(1, ahead):
        each(loads(i), start)
    pack(0)
    towers[1].start()

    def body(i, carry):
        slot, to = i % ahead, i % behind

        pl.when(i == 0)(load_acts.start)
        pl.when(i == 0)(load_cells.start)
        pl.when(i == 2)(load_cells.wait)
        pl.when((i >= 2) & (i < 14))(lambda: unpool(i - 2))

        @pl.when(i == ahead)
        def _():
            load_acts.wait()
            store_acts.start()


        @pl.when(i == parts)
        def _():
            towers[1].wait()
            pack(1)

        each(loads(i), wait)
        pl.when(i >= behind)(lambda: each(stores(i - behind), wait))
        grad = jnp.dot(
            ft[...], s_in[slot].reshape(groups * base, tile), preferred_element_type=F32
        )
        g_out[to] = grad
        moment = MOMENTUM * m_in[slot] + grad
        m_out[to] = moment
        n_out[to] = (w_in[slot].astype(F32) - DENSE_RATE * moment).astype(BF16)
        each(stores(i), start)
        pl.when(i + ahead < steps)(lambda: each(loads(i + ahead), start))
        return carry

    lax.fori_loop(0, steps, body, 0)
    for k in range(behind):
        each(stores(steps - behind + k), wait)
    for t in range(2):
        for unit in range(12):
            maps_store(unit, t).wait()
        for half in range(2):
            last_store(half, t).wait()
    store_acts.wait()


def weight_update(live, ft_all, gathered, moment, weight, maps_shape, cells, acts, sums, mixed, smalls):
    groups, parts, _, rows, outs = gathered.shape
    width = weight.shape[1]
    chans = maps_shape[2]
    base = rows * 3 // 4
    here = pl.BlockSpec(memory_space=pltpu.VMEM)
    far = pl.BlockSpec(memory_space=pl.ANY)
    ahead, behind = 3, 2
    vmem, dma = pltpu.VMEM, pltpu.SemaphoreType.DMA
    return pl.pallas_call(
        functools.partial(update_kernel, base),
        in_specs=[pl.BlockSpec(memory_space=pltpu.SMEM)] + [far] * 6 + [here] * (2 + len(smalls)),
        out_specs=[far] * 5 + [here] * 9,
        out_shape=[
            jax.ShapeDtypeStruct(moment.shape, F32),
            jax.ShapeDtypeStruct(moment.shape, BF16),
            jax.ShapeDtypeStruct(moment.shape, F32),
            jax.ShapeDtypeStruct(maps_shape, BF16),
            jax.ShapeDtypeStruct(acts.shape, BF16),
        ]
        + [jax.ShapeDtypeStruct(a.shape, F32) for a in smalls[::2] for _ in range(3)],
        scratch_shapes=[
            vmem((width, groups * rows), BF16),
            vmem((groups * (rows - base), groups * base), BF16),
            vmem((width, groups * base), BF16),
            vmem((ahead, groups, base, outs), BF16),
            vmem((ahead, width, outs), F32),
            vmem((ahead, width, outs), BF16),
            vmem((behind, width, outs), F32),
            vmem((behind, width, outs), BF16),
            vmem((behind, width, outs), F32),
            vmem(maps_shape, BF16),
            vmem(cells.shape, BF16),
            vmem((2, 13, chans // 2, rows), F32),
            vmem((4, chans, 128), F32),
            vmem(acts.shape, BF16),
            dma((2,)),
            dma((ahead, 3)),
            dma((behind, 3)),
            dma,
            dma((14, 2)),
            dma((2,)),
        ],
        compiler_params=params(),
        name="weight_update",
    )(live, ft_all, gathered, moment, weight, cells, acts, sums, mixed, *smalls)


def fast_shards(
    mesh,
    input_maps,
    dense_weight,
    dense_bias,
    stitch_in,
    stitch_out,
    weight_moment,
    bias_moment,
    stitch_in_moment,
    stitch_out_moment,
    cotangent,
    live_rows,
):
    maps = jnp.transpose(input_maps, (1, 3, 2, 0))
    gathered, ft_all, acts, cells, sums, mixed = step_all(
        mesh, live_rows, maps, dense_weight, cotangent, dense_bias, stitch_out, stitch_in
    )
    (
        weight_grad,
        weight_next,
        weight_moment_next,
        maps_grad,
        activations,
        bias_grad,
        bias_next,
        bias_moment_next,
        stitch_in_grad,
        stitch_in_next,
        stitch_in_moment_next,
        stitch_out_grad,
        stitch_out_next,
        stitch_out_moment_next,
    ) = weight_update(
        live_rows,
        ft_all,
        gathered,
        weight_moment,
        dense_weight,
        maps.shape,
        cells,
        acts,
        sums,
        mixed,
        [dense_bias, bias_moment, stitch_in, stitch_in_moment, stitch_out, stitch_out_moment],
    )
    maps_grad = jnp.transpose(maps_grad, (3, 0, 2, 1))
    return (
        activations,
        maps_grad,
        weight_grad,
        bias_grad,
        stitch_in_grad,
        stitch_out_grad,
        weight_next,
        bias_next,
        stitch_in_next,
        stitch_out_next,
        weight_moment_next,
        bias_moment_next,
        stitch_in_moment_next,
        stitch_out_moment_next,
    )


def choose(mesh, *args):
    rows, _, chans, _ = args[0].shape
    outs = args[2].shape[1]
    shape = mesh.shape["batch"] == 4 and mesh.shape["mp"] == 8
    if shape and rows == 512 and outs == 512 and chans == 32:
        return fast_shards(mesh, *args)
    return shards(*args)


def solution(mesh):
    in_specs = (
        P("batch", None, "mp", None),
        P(None, "mp", None),
        P(None, "mp"),
        P(None, None, "mp"),
        P(None, None, "mp"),
        P(None, "mp", None),
        P(None, "mp"),
        P(None, None, "mp"),
        P(None, None, "mp"),
        P("batch", None, "mp"),
        P(),
    )
    out_specs = (
        P("batch", None, "mp"),
        P("batch", None, "mp", None),
        P(None, "mp", None),
        P(None, "mp"),
        P(None, None, "mp"),
        P(None, None, "mp"),
        P(None, "mp", None),
        P(None, "mp"),
        P(None, None, "mp"),
        P(None, None, "mp"),
        P(None, "mp", None),
        P(None, "mp"),
        P(None, None, "mp"),
        P(None, None, "mp"),
    )
    body = functools.partial(choose, mesh)
    return jax.shard_map(body, mesh=mesh, in_specs=in_specs, out_specs=out_specs, check_vma=False)
```
